128 devices in a mesh: corpus: 8 (over z, core), rerank: 16 (over x, y).
Axes of the slice: x: 4, y: 4, z: 4, core: 2. Of those that a mesh axis runs over, the one named last changes fastest.
Arguments:
- store_rows: bfloat16 [256, 512, 3584], P('corpus', 'rerank'), may hold values from -400 to 400
- block_lengths: int32 [256], replicated, may hold values from 128 to 512
- queries: bfloat16 [32, 64, 3584], P(None, 'rerank'), may hold values from -400 to 400
- cand_owner: int32 [256, 1], replicated, may hold values from 0 to 7; in each aligned block of 32 rows (0 to 31, 32 to 63, ...) at most 5 rows name the same one
- cand_block: int32 [256], replicated, may hold values from 0 to 31
- cand_query: int32 [256], replicated, may hold values from 0 to 31
- norm_gain: bfloat16 [3584], replicated, may hold values from 0.099609375 to 1.8984375
- w_query: bfloat16 [3584, 1792], P('rerank'), may hold values from -8 to 8
- w_key: bfloat16 [3584, 256], P('rerank'), may hold values from -1 to 1
- w_value: bfloat16 [3584, 256], P('rerank'), may hold values from -0.09375 to 0.09375
- w_score: bfloat16 [1792], replicated, may hold values from -0.125 to 0.125
Outputs:
- passage_context: bfloat16 [320, 512, 1792], P('corpus', 'rerank')
- pair_scores: float32 [256], P(('corpus', 'rerank'))
The draws below stay inside these ranges and needn't reach their ends.
Inputs may be any that keep to these rules, and one draw needn't show every extreme that they name: `cand_owner`: at most 5 of the 32 pairs of one corpus group (an aligned block of rows) name the same owner, in every draw, some group names one owner in exactly 5 of its 32 pairs.
All inputs are finite; a program needn't handle non-finite values.
Results may differ from the reference program's by a relative error of at most 0.013.
Values may be sent and summed in bfloat16 or wider, within the bound.
No kernel may reach another device: no remote copies, remote signals or barrier semaphores. Data moves between devices by JAX's collectives and lax.ppermute only.
A program may use at most 128 MiB of HBM per device.

```python
import math
import jax
import jax.numpy as jnp
import numpy as np
from jax import lax

D = 3584
HDIM = 128
QHEADS = 14
KVHEADS = 2
QW = 1792
KW = 256
BLK = 512
QLEN = 64
CAP = 5
PAIR_C = 32
PAIRS = 256
OWN_BLKS = 32
NQ = 32
BLOCKS = 256
N_CORPUS = 8


def hidden_rows(key, shape):
    noise_key = jax.random.fold_in(key, 3)
    column_key = jax.random.fold_in(key, 5)
    row_key = jax.random.fold_in(key, 7)
    base = jax.random.truncated_normal(noise_key, -4.0, 4.0, shape, jnp.float32)
    columns = jnp.exp(jax.random.uniform(column_key, (shape[-1],), jnp.float32, 0.0, math.log(10.0)))
    row_scale = jnp.exp(jax.random.uniform(row_key, shape[:-1] + (1,), jnp.float32, 0.0, math.log(10.0)))
    return jnp.clip(base * columns * row_scale, -400.0, 400.0)


def draw_store_rows(key, part):
    return hidden_rows(jax.random.fold_in(key, 101), (BLOCKS, BLK, D)).astype(jnp.bfloat16)


def draw_queries(key, part):
    return hidden_rows(jax.random.fold_in(key, 202), (NQ, QLEN, D)).astype(jnp.bfloat16)


def key_matrix(key):
    return jax.random.truncated_normal(jax.random.fold_in(key, 11), -4.0, 4.0, (D, KVHEADS * HDIM), jnp.float32) * D ** (-0.5)


def draw_w_key(key, part):
    return key_matrix(key).astype(jnp.bfloat16)


def draw_w_query(key, part):
    noise = jax.random.truncated_normal(jax.random.fold_in(key, 23), -4.0, 4.0, (D, QHEADS * HDIM), jnp.float32) * D ** (-0.5)
    return noise.astype(jnp.bfloat16)


def plant(array, rng, least, high):
    spot = [jax.random.randint(jax.random.fold_in(rng, axis), (), 0, length) for axis, length in enumerate(array.shape)]
    widest = array.shape.index(max(array.shape))
    beside = spot[:widest] + [(spot[widest] + 1) % array.shape[widest]] + spot[widest + 1:]
    return array.at[tuple(spot)].set(least).at[tuple(beside)].set(high)


def block_levels(own_key, dims, cuts, smallest, largest):
    def one(position, blocks):
        heights = jax.random.uniform(jax.random.fold_in(jax.random.fold_in(own_key, 6), position), (blocks,), jnp.float32, smallest / len(cuts), largest / len(cuts))
        return jnp.repeat(jnp.exp(heights), dims[position] // blocks).reshape((-1,) + (1,) * (len(dims) - position - 1))

    factor_of = one(*cuts[0])
    for cut in cuts[1:]:
        factor_of = factor_of * one(*cut)
    return factor_of


def deal_out(own_key, own, number, rows, count, top, bound, slope):
    ranking = jax.random.permutation(own_key, count)
    heavy_load, usual = load_shares(count, rows * top, bound, slope, True), load_shares(count, rows * top, bound, slope, False)
    places = jnp.arange(count)

    def named(lengths, turn):
        used = int((lengths > 0).sum())
        fixed = max(1, used // 4)
        passed = fixed + (places - fixed + turn * (used - fixed)) % max(1, count - fixed)
        return jnp.zeros((count,), jnp.int32).at[ranking[jnp.where(places < fixed, places, passed)]].set(jnp.asarray(lengths, jnp.int32))

    lengths = jnp.where(number % 4 == 0, named(heavy_load, number // 4), named(usual, number - number // 4 - 1))
    mixed = jax.random.permutation(jax.random.fold_in(own, 3), count)
    donor, taker = mixed[0:count // 2 * 2:2], mixed[1:count // 2 * 2:2]
    margin = jnp.minimum(lengths[donor] - 1, bound - lengths[taker]) // 2
    margin = jnp.where((donor == ranking[0]) | (taker == ranking[0]) | (lengths[taker] == 0), 0, jnp.maximum(margin, 0))
    passed = jax.random.randint(jax.random.fold_in(own, 4), (count // 2,), 0, 1 << 20) % (margin + 1)
    lengths = lengths.at[donor].add(-passed).at[taker].add(passed)
    labels = jnp.searchsorted(jnp.cumsum(lengths), jnp.arange(rows * top), side="right").astype(jnp.int32)
    listing = labels.reshape(top, rows).T
    listing = listing[jax.random.permutation(jax.random.fold_in(own, 1), rows)]
    turn = jax.random.randint(jax.random.fold_in(own, 2), (rows, 1), 0, top)
    return jnp.take_along_axis(listing, (jnp.arange(top)[None, :] + turn) % top, axis=1)


def load_shares(number_of, total, reach, lean, full):
    loads = [(1 << 20) // math.isqrt(standing ** lean) + 1 for standing in range(1, number_of + 1)]
    largest = reach if full else min(reach, max(-(-total // number_of), total * loads[0] // sum(loads)))
    least = 1 if total - largest >= number_of - 1 else 0
    counts, rest = [largest] + [least] * (number_of - 1), total - largest - least * (number_of - 1)
    while rest > 0:
        free = [i for i in range(1, number_of) if counts[i] < largest] or [i for i in range(1, number_of) if counts[i] < reach]
        mass, budget = sum([loads[i] for i in free]), rest
        for i in free:
            addition = min(reach - counts[i], max(1, budget * loads[i] // mass), rest)
            counts[i] = counts[i] + addition
            rest = rest - addition
    return np.array(counts)


def gaussian(key, dims, deviation, reach, split=(), kind=jnp.bfloat16):
    result = jax.random.normal(key, dims, jnp.float32) * deviation
    if len(split) > 0:
        result = block_levels(key, dims, split, -0.22, 0.18) * result
    return jnp.clip(result, min=-reach, max=reach).astype(kind)


def setup_inputs(seed: int = 0) -> dict:
    seeds = jax.random.split(jax.random.key(seed), 12)
    store_rows = draw_store_rows(jax.random.fold_in(seeds[11], 71), 0)
    block_lengths = plant(jax.random.randint(seeds[1], (BLOCKS,), BLK // 4, BLK + 1), jax.random.fold_in(seeds[1], 1), BLK // 4, BLK).astype(jnp.int32)
    queries = draw_queries(jax.random.fold_in(seeds[11], 71), 0)
    cand_owner_keys = jax.random.split(jax.random.fold_in(seeds[3], 1), PAIRS // PAIR_C)
    cand_owner_turns = jax.random.permutation(jax.random.fold_in(seeds[3], 3), PAIRS // PAIR_C)
    cand_owner = jax.vmap(lambda own, number: deal_out(jax.random.fold_in(seeds[3], 2), own, number, PAIR_C, N_CORPUS, 1, CAP, 2))(cand_owner_keys, cand_owner_turns).reshape((PAIRS, 1))
    cand_block = plant(jax.random.randint(seeds[4], (PAIRS,), 0, OWN_BLKS), jax.random.fold_in(seeds[4], 1), 0, OWN_BLKS - 1).astype(jnp.int32)
    cand_query = plant(jax.random.randint(seeds[5], (PAIRS,), 0, NQ), jax.random.fold_in(seeds[5], 1), 0, NQ - 1).astype(jnp.int32)
    norm_gain = jnp.clip(1.0 + 0.18 * jax.random.normal(seeds[6], (D,), jnp.float32), 0.099609375, 1.8984375).astype(jnp.bfloat16)
    w_query = draw_w_query(jax.random.fold_in(seeds[11], 71), 0)
    w_key = draw_w_key(jax.random.fold_in(seeds[11], 71), 0)
    w_value = gaussian(seeds[9], (D, KW), D ** -0.5, 0.09375, ((0, 16),))
    w_score = gaussian(seeds[10], (QW,), QW ** -0.5, 0.125)
    return {"store_rows": store_rows, "block_lengths": block_lengths, "queries": queries, "cand_owner": cand_owner, "cand_block": cand_block, "cand_query": cand_query, "norm_gain": norm_gain, "w_query": w_query, "w_key": w_key, "w_value": w_value, "w_score": w_score}


ROPE_BASE = 1000000.0
EPSILON = 1e-06

def rotate(values, positions):
    head_dim = values.shape[-1]
    half_dim = head_dim // 2
    inverse = jnp.power(ROPE_BASE, -2.0 * jnp.arange(half_dim, dtype=jnp.float32) / head_dim)
    angles = positions.astype(jnp.float32)[..., None] * inverse
    cosine = jnp.cos(angles)[..., None, :]
    sine_part = jnp.sin(angles)[..., None, :]
    lower = values[..., :half_dim]
    upper = values[..., half_dim:]
    return jnp.concatenate([lower * cosine - upper * sine_part, upper * cosine + lower * sine_part], axis=-1)

def attend(joined, length, norm_gain, w_query, w_key, w_value, w_score):
    seq_len = joined.shape[0]
    widened = joined.astype(jnp.float32)
    inverse_rms = lax.rsqrt(lax.optimization_barrier(jnp.mean(widened * widened, axis=-1, keepdims=True)) + EPSILON)
    normed = (widened * inverse_rms * norm_gain.astype(jnp.float32)).astype(jnp.bfloat16)
    query_raw = jnp.dot(normed, w_query, preferred_element_type=jnp.float32)
    key_raw = jnp.dot(normed, w_key, preferred_element_type=jnp.float32)
    value_raw = jnp.dot(normed, w_value, preferred_element_type=jnp.float32)
    token_ids = jnp.arange(seq_len, dtype=jnp.int32)
    positions = jnp.where(token_ids < BLK, token_ids, length + token_ids - BLK)
    query_rot = rotate(query_raw.reshape(seq_len, QHEADS, HDIM), positions).astype(jnp.bfloat16)
    key_rot = rotate(key_raw.reshape(seq_len, KVHEADS, HDIM), positions).astype(jnp.bfloat16)
    values = value_raw.reshape(seq_len, KVHEADS, HDIM).astype(jnp.bfloat16)
    grouped = query_rot.reshape(seq_len, KVHEADS, QHEADS // KVHEADS, HDIM)
    logits = jnp.einsum('skgd,tkd->kgst', grouped.astype(jnp.float32), key_rot.astype(jnp.float32)) * HDIM ** (-0.5)
    live = (token_ids < length) | (token_ids >= BLK)
    allowed = live[None, :] & (token_ids[None, :] <= token_ids[:, None])
    masked = jnp.where(allowed, logits, -1e+30)
    peak = lax.optimization_barrier(jnp.max(masked, axis=-1, keepdims=True))
    weights = jnp.where(allowed, jnp.exp(masked - peak), 0.0)
    probs = (weights / lax.optimization_barrier(jnp.sum(weights, axis=-1, keepdims=True))).astype(jnp.bfloat16)
    context = jnp.einsum('kgst,tkd->skgd', probs.astype(jnp.float32), values.astype(jnp.float32))
    context = context.reshape(seq_len, QHEADS * HDIM).astype(jnp.bfloat16)
    score = jnp.dot(context[seq_len - 1], w_score, preferred_element_type=jnp.float32)
    keep = token_ids[:BLK] < length
    passage = jnp.where(keep[:, None], context[:BLK], jnp.zeros((), jnp.bfloat16))
    return (passage, score)

def reference(store_rows, block_lengths, queries, cand_owner, cand_block, cand_query, norm_gain, w_query, w_key, w_value, w_score):
    pair_total = cand_block.shape[0]
    pair_group = pair_total // N_CORPUS
    owners = cand_owner[:, 0]
    pair_order = jnp.arange(pair_total, dtype=jnp.int32)
    group_of = pair_order // pair_group
    earlier = (owners[:, None] == owners[None, :]) & (group_of[:, None] == group_of[None, :]) & (pair_order[None, :] < pair_order[:, None])
    owner_rank = lax.optimization_barrier(jnp.sum(earlier.astype(jnp.int32), axis=1))
    block_of = owners * OWN_BLKS + cand_block

    def run_pair(index):
        block = block_of[index]
        joined = jnp.concatenate([store_rows[block], queries[cand_query[index]]], axis=0)
        return attend(joined, block_lengths[block], norm_gain, w_query, w_key, w_value, w_score)
    passages, pair_scores = lax.map(run_pair, pair_order)
    slot_ids = ((owners * N_CORPUS + group_of) * CAP + owner_rank).astype(jnp.int32)
    passage_context = jnp.zeros((N_CORPUS * N_CORPUS * CAP, BLK, QHEADS * HDIM), jnp.bfloat16).at[slot_ids].set(passages)
    return (passage_context, pair_scores)
```

```python
import jax
import jax.numpy as jnp
from jax import lax
from jax.experimental import pallas as pl
from jax.experimental.pallas import tpu as pltpu
from jax.sharding import PartitionSpec as P

HDIM = 128
QHEADS = 14
KVHEADS = 2
PER = QHEADS // KVHEADS
QW = QHEADS * HDIM
KW = KVHEADS * HDIM
BLK = 512
QLEN = 64
CAP = 5
SIDE = 4
ROPE_BASE = 1000000.0
EPSILON = 1e-06
SCALE2 = HDIM ** (-0.5) * 1.4426950408889634
VMEM = 56 * 1024 * 1024


def rope_tables(positions):
    half = HDIM // 2
    inverse = jnp.power(ROPE_BASE, -2.0 * jnp.arange(half, dtype=jnp.float32) / HDIM)
    angles = positions.astype(jnp.float32)[:, None] * inverse
    cosine, sine = jnp.cos(angles), jnp.sin(angles)
    return (
        jnp.concatenate([cosine, cosine], axis=1),
        jnp.concatenate([-sine, sine], axis=1),
    )


def spin(part, cosine, sine):
    return part * cosine + pltpu.roll(part, HDIM // 2, part.ndim - 1) * sine


def shift(value, dim, step):
    def moved(index):
        x, y = index // SIDE, index % SIDE
        if dim == "x":
            x = (x + step) % SIDE
        else:
            y = (y + step) % SIDE
        return x * SIDE + y

    return lax.ppermute(value, "rerank", [(i, moved(i)) for i in range(SIDE * SIDE)])


def ring(value, dim):
    half = value.shape[0] // 2
    low = shift(value, dim, 1)
    high = shift(value, dim, -1)
    far_low = shift(low[:half], dim, 1)
    far_high = shift(high[half:], dim, -1)
    return value, low, high, jnp.concatenate([far_low, far_high], axis=0)


def plane_gather(value, first, second):
    return ring(jnp.stack(ring(value, first), axis=1), second)


def norm_kv_kernel(store_ref, query_ref, gain_ref, w_ref, cos_ref, sin_ref, normed_ref, kv_ref):
    step = pl.program_id(0)
    last = pl.num_programs(0) - 1

    def work(rows):
        wide = rows.astype(jnp.float32)
        inverse = lax.rsqrt(jnp.mean(wide * wide, axis=-1, keepdims=True) + EPSILON)
        normed = (wide * inverse * gain_ref[...]).astype(jnp.bfloat16)
        normed_ref[...] = normed
        raw = jnp.dot(normed, w_ref[...], preferred_element_type=jnp.float32)
        for head in range(KVHEADS):
            cols = slice(head * HDIM, (head + 1) * HDIM)
            kv_ref[:, cols] = spin(raw[:, cols], cos_ref[0], sin_ref[0]).astype(jnp.bfloat16)
        kv_ref[:, KW:] = raw[:, KW:].astype(jnp.bfloat16)

    @pl.when(step < last)
    def _():
        work(store_ref[...])

    @pl.when(step == last)
    def _():
        work(query_ref[...])


def norm_kv(store, query, gain, w_kv, cosine, sine):
    tile = query.shape[0]
    tiles = store.shape[0] // tile
    width = store.shape[1]
    table = pl.BlockSpec((1, tile, HDIM), lambda i: (i // tiles, 0, 0))
    return pl.pallas_call(
        norm_kv_kernel,
        grid=(tiles + 1,),
        in_specs=[
            pl.BlockSpec((tile, width), lambda i: (jnp.minimum(i, tiles - 1), 0)),
            pl.BlockSpec((tile, width), lambda i: (0, 0)),
            pl.BlockSpec((1, width), lambda i: (0, 0)),
            pl.BlockSpec((width, 2 * KW), lambda i: (0, 0)),
            table,
            table,
        ],
        out_specs=[
            pl.BlockSpec((tile, width), lambda i: (i, 0)),
            pl.BlockSpec((tile, 2 * KW), lambda i: (i, 0)),
        ],
        out_shape=[
            jax.ShapeDtypeStruct(((tiles + 1) * tile, width), jnp.bfloat16),
            jax.ShapeDtypeStruct(((tiles + 1) * tile, 2 * KW), jnp.bfloat16),
        ],
        compiler_params=pltpu.CompilerParams(vmem_limit_bytes=VMEM),
        name="norm_kv",
    )(store, query, gain, w_kv, cosine, sine)


def query_kernel(normed_ref, w_ref, cos_ref, sin_ref, out_ref, last_ref):
    rows = out_ref.shape[0]
    tokens = cos_ref.shape[0]
    raw = jnp.dot(normed_ref[...], w_ref[...], preferred_element_type=jnp.float32)
    for head in range(out_ref.shape[1] // HDIM):
        cols = slice(head * HDIM, (head + 1) * HDIM)
        part = raw[:rows, cols].reshape(rows // tokens, tokens, HDIM)
        turned = spin(part, cos_ref[...][None], sin_ref[...][None])
        out_ref[:, cols] = turned.reshape(rows, HDIM).astype(jnp.bfloat16)
    last_ref[...] = raw[rows:]


def project_query(normed, w_query, cosine, sine, rows):
    width = normed.shape[1]
    chunk = 2 * HDIM
    extra = 16
    table = pl.BlockSpec(cosine.shape, lambda i: (0, 0))
    return pl.pallas_call(
        query_kernel,
        grid=(QW // chunk,),
        in_specs=[
            pl.BlockSpec((rows + extra, width), lambda i: (0, 0)),
            pl.BlockSpec((width, chunk), lambda i: (0, i)),
            table,
            table,
        ],
        out_specs=[
            pl.BlockSpec((rows, chunk), lambda i: (0, i)),
            pl.BlockSpec((extra, chunk), lambda i: (0, i)),
        ],
        out_shape=[
            jax.ShapeDtypeStruct((rows, QW), jnp.bfloat16),
            jax.ShapeDtypeStruct((extra, QW), jnp.float32),
        ],
        compiler_params=pltpu.CompilerParams(vmem_limit_bytes=VMEM),
        name="project_query",
    )(normed, w_query, cosine, sine)


def attend_kernel(slot_ref, block_ref, length_ref, base_ref, q_ref, *rest):
    kv_refs, (kpos_ref, out_ref, held) = rest[: 2 * SIDE], rest[2 * SIDE :]
    step = pl.program_id(0)
    tokens = q_ref.shape[1]
    half_blocks = base_ref[1]
    base = base_ref[0]
    block = block_ref[step]
    length = length_ref[step]
    before = block_ref[jnp.maximum(step - 1, 0)]
    fresh = (block >= 0) & ((step == 0) | (block != before))
    alive = base < length

    def work(refs, kpos):
        rows = PER * tokens
        qpos = base + lax.rem(lax.broadcasted_iota(jnp.int32, (rows, 1), 0), tokens)
        allowed = (kpos <= qpos) & (kpos < length)
        kept = (base + lax.broadcasted_iota(jnp.int32, (tokens, 1), 0)) < length
        for g in range(KVHEADS):
            queries = jnp.concatenate(
                [q_ref[0, :, (g * PER + h) * HDIM : (g * PER + h + 1) * HDIM] for h in range(PER)],
                axis=0,
            )
            flat = SIDE * tokens
            keys = jnp.concatenate(
                [r[0, :, :, g * HDIM : (g + 1) * HDIM].reshape(flat, HDIM) for r in refs], axis=0
            )
            values = jnp.concatenate(
                [r[0, :, :, KW + g * HDIM : KW + (g + 1) * HDIM].reshape(flat, HDIM) for r in refs],
                axis=0,
            )
            logits = lax.dot_general(
                queries, keys, (((1,), (1,)), ((), ())), preferred_element_type=jnp.float32
            )
            logits = jnp.where(allowed, logits * SCALE2, -1e30)
            weights = jnp.exp2(logits - jnp.max(logits, axis=-1, keepdims=True))
            total = jnp.sum(weights, axis=-1, keepdims=True)
            mixed = jnp.dot(
                weights.astype(jnp.bfloat16), values, preferred_element_type=jnp.float32
            ) / total
            for h in range(PER):
                part = mixed[h * tokens : (h + 1) * tokens]
                held[:, (g * PER + h) * HDIM : (g * PER + h + 1) * HDIM] = jnp.where(
                    kept, part, 0.0
                ).astype(jnp.bfloat16)

    @pl.when(fresh & alive & (block < half_blocks))
    def _():
        work(kv_refs[:SIDE], kpos_ref[0:1, :])

    @pl.when(fresh & alive & (block >= half_blocks))
    def _():
        work(kv_refs[SIDE:], kpos_ref[1:2, :])

    @pl.when((block >= 0) & alive)
    def _():
        out_ref[0] = held[...]

    @pl.when((block < 0) | jnp.logical_not(alive))
    def _():
        out_ref[0] = jnp.zeros_like(held)


def attend(order, blocks, lengths, base, queries, first, second, kpos):
    slots = order.shape[0]
    tokens = queries.shape[1]
    half = first[0].shape[0]

    def in_first(i, order, blocks, lengths, base):
        return (jnp.clip(blocks[i], 0, half - 1), 0, 0, 0)

    def in_second(i, order, blocks, lengths, base):
        return (jnp.clip(blocks[i] - half, 0, half - 1), 0, 0, 0)

    piece = (1, SIDE, tokens, 2 * KW)
    return pl.pallas_call(
        attend_kernel,
        grid_spec=pltpu.PrefetchScalarGridSpec(
            num_scalar_prefetch=4,
            grid=(slots,),
            in_specs=[
                pl.BlockSpec(
                    (1, tokens, QW), lambda i, o, b, l, s: (jnp.maximum(b[i], 0), 0, 0)
                ),
                *[pl.BlockSpec(piece, in_first) for _ in first],
                *[pl.BlockSpec(piece, in_second) for _ in second],
                pl.BlockSpec((2, BLK), lambda i, o, b, l, s: (0, 0)),
            ],
            out_specs=pl.BlockSpec((1, tokens, QW), lambda i, o, b, l, s: (o[i], 0, 0)),
            scratch_shapes=[pltpu.VMEM((tokens, QW), jnp.bfloat16)],
        ),
        out_shape=jax.ShapeDtypeStruct((slots, tokens, QW), jnp.bfloat16),
        compiler_params=pltpu.CompilerParams(vmem_limit_bytes=VMEM),
        name="attend",
    )(order, blocks, lengths, base, queries, *first, *second, kpos)


def score_kernel(count_ref, block_ref, length_ref, which_ref, half_ref, last_ref, *rest):
    kv_refs, rest = rest[: 2 * SIDE], rest[2 * SIDE :]
    qkv_ref, kpos_ref, cos_ref, sin_ref, w_ref, out_ref = rest
    step = pl.program_id(0)
    block = block_ref[step]
    length = length_ref[step]
    which = which_ref[step]

    def work(refs, kpos):
        tokens = refs[0].shape[2]
        flat = SIDE * tokens
        live = kpos < length
        span = qkv_ref.shape[0]
        lane = lax.broadcasted_iota(jnp.int32, (1, span), 1)
        own = lax.rem(lax.div(lane, half_ref[1]), half_ref[2]) == which
        far_cos, far_sin = cos_ref[pl.ds(length + QLEN - 1, 1), :], sin_ref[pl.ds(length + QLEN - 1, 1), :]
        near_cos, near_sin = cos_ref[QLEN - 1 : QLEN, :], sin_ref[QLEN - 1 : QLEN, :]
        total_score = jnp.zeros((1, HDIM), jnp.float32)
        for g in range(KVHEADS):
            raw = last_ref[which, g]
            far = spin(raw, far_cos, far_sin).astype(jnp.bfloat16)
            near = spin(raw, near_cos, near_sin).astype(jnp.bfloat16)
            keys = jnp.concatenate(
                [r[0, :, :, g * HDIM : (g + 1) * HDIM].reshape(flat, HDIM) for r in refs], axis=0
            )
            values = jnp.concatenate(
                [r[0, :, :, KW + g * HDIM : KW + (g + 1) * HDIM].reshape(flat, HDIM) for r in refs],
                axis=0,
            )
            over = (((1,), (1,)), ((), ()))
            passage = lax.dot_general(far, keys, over, preferred_element_type=jnp.float32)
            question = lax.dot_general(
                near,
                qkv_ref[:, g * HDIM : (g + 1) * HDIM],
                over,
                preferred_element_type=jnp.float32,
            )
            passage = jnp.where(live, passage * SCALE2, -1e30)
            question = jnp.where(own, question * SCALE2, -1e30)
            peak = jnp.maximum(
                jnp.max(passage, axis=-1, keepdims=True), jnp.max(question, axis=-1, keepdims=True)
            )
            passage = jnp.exp2(passage - peak)
            question = jnp.exp2(question - peak)
            total = jnp.sum(passage, axis=-1, keepdims=True) + jnp.sum(
                question, axis=-1, keepdims=True
            )
            mixed = jnp.dot(
                passage.astype(jnp.bfloat16), values, preferred_element_type=jnp.float32
            ) + jnp.dot(
                question.astype(jnp.bfloat16),
                qkv_ref[:, KW + g * HDIM : KW + (g + 1) * HDIM],
                preferred_element_type=jnp.float32,
            )
            context = (mixed / total).astype(jnp.bfloat16).astype(jnp.float32)
            total_score += jnp.sum(context * w_ref[g], axis=0, keepdims=True)
        score = jnp.sum(total_score, axis=-1, keepdims=True)
        out_ref[pl.ds(step, 1), :] = jnp.broadcast_to(score, (1, HDIM))

    busy = step < count_ref[0]

    @pl.when(busy & (block < half_ref[0]))
    def _():
        work(kv_refs[:SIDE], kpos_ref[0:1, :])

    @pl.when(busy & (block >= half_ref[0]))
    def _():
        work(kv_refs[SIDE:], kpos_ref[1:2, :])


def score(count, blocks, lengths, which, sizes, last, first, second, question_kv, kpos, cosine, sine, w):
    slots = blocks.shape[0]
    half = first[0].shape[0]
    tokens = first[0].shape[2]

    def in_first(i, count, blocks, *_):
        return (jnp.clip(blocks[i], 0, half - 1), 0, 0, 0)

    def in_second(i, count, blocks, *_):
        return (jnp.clip(blocks[i] - half, 0, half - 1), 0, 0, 0)

    piece = (1, SIDE, tokens, 2 * KW)

    def whole(array):
        return pl.BlockSpec(array.shape, lambda i, *_: (0,) * array.ndim)

    padded = (slots + 7) // 8 * 8
    return pl.pallas_call(
        score_kernel,
        grid_spec=pltpu.PrefetchScalarGridSpec(
            num_scalar_prefetch=5,
            grid=(slots,),
            in_specs=[
                whole(last),
                *[pl.BlockSpec(piece, in_first) for _ in first],
                *[pl.BlockSpec(piece, in_second) for _ in second],
                whole(question_kv),
                whole(kpos),
                whole(cosine),
                whole(sine),
                whole(w),
            ],
            out_specs=pl.BlockSpec((padded, HDIM), lambda i, *_: (0, 0)),
        ),
        out_shape=jax.ShapeDtypeStruct((padded, HDIM), jnp.float32),
        compiler_params=pltpu.CompilerParams(vmem_limit_bytes=VMEM),
        name="score",
    )(
        count,
        blocks,
        lengths,
        which,
        jnp.array([half, *sizes], jnp.int32),
        last,
        *first,
        *second,
        question_kv,
        kpos,
        cosine,
        sine,
        w,
    )


def sorted_by(key):
    count = key.shape[0]
    place = jnp.arange(count, dtype=jnp.int32)
    ahead = (key[None, :] < key[:, None]) | (
        (key[None, :] == key[:, None]) & (place[None, :] < place[:, None])
    )
    rank = jnp.sum(ahead.astype(jnp.int32), axis=1)
    chosen = rank[None, :] == place[:, None]

    def arrange(values):
        return jnp.sum(jnp.where(chosen, values[None, :], 0), axis=1).astype(jnp.int32)

    return arrange


def on_device(
    store_rows,
    block_lengths,
    queries,
    cand_owner,
    cand_block,
    cand_query,
    norm_gain,
    w_query,
    w_key,
    w_value,
    w_score,
):
    n_corpus = lax.axis_size("corpus")
    n_rerank = lax.axis_size("rerank")
    corpus_index = lax.axis_index("corpus")
    member = lax.axis_index("rerank")
    pair_total = cand_block.shape[0]
    pair_group = pair_total // n_corpus
    own_blocks, tokens, width = store_rows.shape
    n_query, q_tokens, _ = queries.shape
    q_dev = n_query // n_rerank
    half_blocks = own_blocks // 2

    owners = cand_owner[:, 0]
    pair_order = jnp.arange(pair_total, dtype=jnp.int32)
    group_of = pair_order // pair_group
    earlier = (
        (owners[:, None] == owners[None, :])
        & (group_of[:, None] == group_of[None, :])
        & (pair_order[None, :] < pair_order[:, None])
    )
    owner_rank = jnp.sum(earlier.astype(jnp.int32), axis=1)
    slot_ids = jnp.arange(n_corpus * CAP, dtype=jnp.int32)
    wanted = (
        (group_of[None, :] == (slot_ids // CAP)[:, None])
        & (owners[None, :] == corpus_index)
        & (owner_rank[None, :] == (slot_ids % CAP)[:, None])
    )
    present = jnp.any(wanted, axis=1)

    def of_slot(values):
        return jnp.sum(jnp.where(wanted, values[None, :], 0), axis=1)

    slot_block, slot_query, slot_pair = of_slot(cand_block), of_slot(cand_query), of_slot(pair_order)
    own_lengths = lax.dynamic_slice_in_dim(block_lengths, corpus_index * own_blocks, own_blocks, 0)
    block_ids = jnp.arange(own_blocks, dtype=jnp.int32)
    slot_length = jnp.sum(
        jnp.where(slot_block[:, None] == block_ids[None, :], own_lengths[None, :], 0), axis=1
    )
    by_block = sorted_by(jnp.where(present, slot_block, own_blocks))
    order = by_block(slot_ids)
    order_block = by_block(jnp.where(present, slot_block, -1))
    order_length = by_block(slot_length)
    mine = present & (slot_query // q_dev == member)
    by_mine = sorted_by(jnp.where(mine, slot_block, own_blocks))
    mine_count = jnp.sum(mine.astype(jnp.int32)).reshape(1)
    mine_block, mine_length = by_mine(slot_block), by_mine(slot_length)
    mine_which, mine_pair = by_mine(slot_query % q_dev), by_mine(slot_pair)

    asked = lax.all_to_all(
        queries.reshape(n_rerank, q_dev * q_tokens * width), "rerank", 0, 0, tiled=True
    )
    asked = asked[::-1].reshape(n_rerank * q_dev * q_tokens, width)
    asked_row = jnp.arange(asked.shape[0], dtype=jnp.int32)
    per_member = q_dev * q_tokens
    asked_token = q_tokens * (n_rerank - 1 - asked_row // per_member) + asked_row % q_tokens

    all_cos, all_sin = rope_tables(jnp.arange(BLK + QLEN, dtype=jnp.int32))
    base = member * tokens
    own_cos, own_sin = rope_tables(base + jnp.arange(tokens, dtype=jnp.int32))
    asked_cos, asked_sin = rope_tables(asked_token)
    repeats = asked.shape[0] // tokens

    def tables(own, other):
        return jnp.stack([jnp.tile(own, (repeats, 1)), other])

    w_kv = lax.all_gather(
        jnp.concatenate([w_key, w_value], axis=1), "rerank", axis=0, tiled=True
    )
    w_q = lax.all_gather(w_query, "rerank", axis=0, tiled=True)
    gain = norm_gain.astype(jnp.float32).reshape(1, width)
    row_count = own_blocks * tokens
    normed, kv = norm_kv(
        store_rows.reshape(row_count, width),
        asked,
        gain,
        w_kv,
        tables(own_cos, asked_cos),
        tables(own_sin, asked_sin),
    )
    passage_kv = kv[:row_count].reshape(own_blocks, tokens, 2 * KW)
    question_kv = kv[row_count:]
    first = plane_gather(passage_kv[:half_blocks], "y", "x")
    second = plane_gather(passage_kv[half_blocks:], "x", "y")
    query_rot, query_last = project_query(normed, w_q, own_cos, own_sin, row_count)

    hops = jnp.array([0, -1, 1, 2], jnp.int32)
    xs, ys = (member // SIDE + hops) % SIDE, (member % SIDE + hops) % SIDE
    inside = jnp.arange(tokens, dtype=jnp.int32)
    kpos = jnp.stack(
        [
            ((xs[:, None] * SIDE + ys[None, :])[:, :, None] * tokens + inside).reshape(BLK),
            ((xs[None, :] * SIDE + ys[:, None])[:, :, None] * tokens + inside).reshape(BLK),
        ]
    )

    last = query_last[q_tokens - 1 : per_member : q_tokens].reshape(q_dev, KVHEADS, PER, HDIM)
    last = jnp.pad(last, ((0, 0), (0, 0), (0, 8 - PER), (0, 0)))
    head_w = jnp.pad(
        w_score.astype(jnp.float32).reshape(KVHEADS, PER, HDIM), ((0, 0), (0, 8 - PER), (0, 0))
    )
    scored = score(
        mine_count,
        mine_block,
        mine_length,
        mine_which,
        (q_tokens, q_dev),
        last,
        first,
        second,
        question_kv,
        kpos,
        all_cos,
        all_sin,
        head_w,
    )[: n_corpus * CAP, 0]
    valid = slot_ids < mine_count[0]
    placed = jnp.sum(
        jnp.where(
            valid[:, None] & (mine_pair[:, None] == pair_order[None, :]), scored[:, None], 0.0
        ),
        axis=0,
    )
    shared = jnp.sum(
        lax.all_to_all(placed.reshape(n_corpus, pair_group), "corpus", 0, 0, tiled=True), axis=0
    )
    pair_scores = jnp.sum(
        lax.all_to_all(
            shared.reshape(n_rerank, pair_group // n_rerank), "rerank", 0, 0, tiled=True
        ),
        axis=0,
    )
    limits = jnp.stack([base, jnp.int32(half_blocks)])
    passage_context = attend(
        order,
        order_block,
        order_length,
        limits,
        query_rot.reshape(own_blocks, tokens, QW),
        first,
        second,
        kpos,
    )
    return (passage_context, pair_scores)


def solution(mesh):
    placed = (
        P("corpus", "rerank", None),
        P(),
        P(None, "rerank", None),
        P(),
        P(),
        P(),
        P(),
        P("rerank", None),
        P("rerank", None),
        P("rerank", None),
        P(),
    )
    return jax.shard_map(
        on_device,
        mesh=mesh,
        in_specs=placed,
        out_specs=(P("corpus", "rerank", None), P(("corpus", "rerank"))),
        check_vma=False,
    )
```

```python
import jax
import jax.numpy as jnp
from jax import lax
from jax.experimental import pallas as pl
from jax.experimental.pallas import tpu as pltpu
from jax.sharding import PartitionSpec as P

HDIM = 128
QHEADS = 14
KVHEADS = 2
PER = QHEADS // KVHEADS
QW = QHEADS * HDIM
KW = KVHEADS * HDIM
BLK = 512
QLEN = 64
CAP = 5
SIDE = 4
ROPE_BASE = 1000000.0
EPSILON = 1e-06
SCALE2 = HDIM ** (-0.5) * 1.4426950408889634
VMEM = 56 * 1024 * 1024


def rope_tables(positions):
    half = HDIM // 2
    inverse = jnp.power(ROPE_BASE, -2.0 * jnp.arange(half, dtype=jnp.float32) / HDIM)
    angles = positions.astype(jnp.float32)[:, None] * inverse
    cosine, sine = jnp.cos(angles), jnp.sin(angles)
    return (
        jnp.concatenate([cosine, cosine], axis=1),
        jnp.concatenate([-sine, sine], axis=1),
    )


def spin(part, cosine, sine):
    return part * cosine + pltpu.roll(part, HDIM // 2, part.ndim - 1) * sine


def shift(value, dim, step):
    def moved(index):
        x, y = index // SIDE, index % SIDE
        if dim == "x":
            x = (x + step) % SIDE
        else:
            y = (y + step) % SIDE
        return x * SIDE + y

    return lax.ppermute(value, "rerank", [(i, moved(i)) for i in range(SIDE * SIDE)])


def tie(*values):
    return lax.optimization_barrier(values)


def plane_gather(value_a, value_b, cut):
    a_low, a_high = shift(value_a, "y", 1), shift(value_a, "y", -1)
    b_low, b_high = shift(value_b, "x", 1), shift(value_b, "x", -1)
    a_low, a_high, b_low, b_high = tie(a_low, a_high, b_low, b_high)
    a_far = shift(a_low[:cut], "y", 1), shift(a_high[cut:], "y", -1)
    b_far = shift(b_low[:cut], "x", 1), shift(b_high[cut:], "x", -1)
    a_far, b_far = tie(a_far, b_far)
    a_own = jnp.stack([value_a, a_low, a_high, jnp.concatenate(a_far, axis=0)])
    b_own = jnp.stack([value_b, b_low, b_high, jnp.concatenate(b_far, axis=0)])
    a_own, b_own = tie(a_own, b_own)
    a_low, a_high = shift(a_own, "x", 1), shift(a_own, "x", -1)
    b_low, b_high = shift(b_own, "y", 1), shift(b_own, "y", -1)
    a_low, a_high, b_low, b_high = tie(a_low, a_high, b_low, b_high)
    a_far = shift(a_low[:2], "x", 1), shift(a_high[2:], "x", -1)
    b_far = shift(b_low[:2], "y", 1), shift(b_high[2:], "y", -1)
    a_far, b_far = tie(a_far, b_far)
    return (a_own, a_low, a_high, *a_far), (b_own, b_low, b_high, *b_far)


HOPS = (0, -1, 1, 2)
BACK = (0, 1, 3, 2)


def part_of(parts, swapped, dx, dy):
    outer, inner = (dy, dx) if swapped else (dx, dy)
    if outer < 3:
        return parts[outer], inner
    return (parts[3], inner) if inner < 2 else (parts[4], inner - 2)


def norm_kernel(x_ref, gain_ref, out_ref):
    wide = x_ref[...].astype(jnp.float32)
    inverse = lax.rsqrt(jnp.mean(wide * wide, axis=-1, keepdims=True) + EPSILON)
    out_ref[...] = (wide * inverse * gain_ref[...]).astype(jnp.bfloat16)


def norm(rows, gain):
    tile = 128
    width = rows.shape[1]
    block = pl.BlockSpec((tile, width), lambda i: (i, 0))
    return pl.pallas_call(
        norm_kernel,
        grid=(rows.shape[0] // tile,),
        in_specs=[block, pl.BlockSpec((1, width), lambda i: (0, 0))],
        out_specs=block,
        out_shape=jax.ShapeDtypeStruct(rows.shape, jnp.bfloat16),
        compiler_params=pltpu.CompilerParams(vmem_limit_bytes=VMEM),
        name="norm",
    )(rows, gain)


def key_value_kernel(place_ref, normed_ref, *rest):
    parts_a, parts_b, rest = rest[:5], rest[5:10], rest[10:]
    cos_ref, sin_ref, kv_ref, w_ref, sems = rest
    ranks, depth, _ = w_ref.shape
    half = depth // 2

    @pl.when(pl.program_id(0) == 0)
    def _():
        copies = []
        for dx in range(SIDE):
            for dy in range(SIDE):
                rank = place_ref[dx * SIDE + dy]
                for which, parts in enumerate((parts_a, parts_b)):
                    ref, index = part_of(parts, which == 1, dx, dy)
                    copies.append(
                        pltpu.make_async_copy(
                            ref.at[index],
                            w_ref.at[rank, pl.ds(which * half, half)],
                            sems.at[len(copies)],
                        )
                    )
        for copy in copies:
            copy.start()
        for copy in copies:
            copy.wait()

    rows = normed_ref.shape[0]
    tokens = cos_ref.shape[0]
    weights = w_ref[...].reshape(ranks * depth, 2 * KW)
    raw = jnp.dot(normed_ref[...], weights, preferred_element_type=jnp.float32)
    for head in range(KVHEADS):
        cols = slice(head * HDIM, (head + 1) * HDIM)
        part = raw[:, cols].reshape(rows // tokens, tokens, HDIM)
        turned = spin(part, cos_ref[...][None], sin_ref[...][None])
        kv_ref[:, cols] = turned.reshape(rows, HDIM).astype(jnp.bfloat16)
    kv_ref[:, KW:] = raw[:, KW:].astype(jnp.bfloat16)


def key_value(place, normed, parts_a, parts_b, cosine, sine, ranks):
    tile = 256
    rows, width = normed.shape
    table = pl.BlockSpec(cosine.shape, lambda i, p: (0, 0))
    anywhere = pl.BlockSpec(memory_space=pl.ANY)
    depth = width // ranks
    return pl.pallas_call(
        key_value_kernel,
        grid_spec=pltpu.PrefetchScalarGridSpec(
            num_scalar_prefetch=1,
            grid=(rows // tile,),
            in_specs=[pl.BlockSpec((tile, width), lambda i, p: (i, 0)), *[anywhere] * 10, table, table],
            out_specs=[
                pl.BlockSpec((tile, 2 * KW), lambda i, p: (i, 0)),
                pl.BlockSpec((ranks, depth, 2 * KW), lambda i, p: (0, 0, 0)),
            ],
            scratch_shapes=[pltpu.SemaphoreType.DMA((2 * SIDE * SIDE,))],
        ),
        out_shape=[
            jax.ShapeDtypeStruct((rows, 2 * KW), jnp.bfloat16),
            jax.ShapeDtypeStruct((ranks, depth, 2 * KW), jnp.bfloat16),
        ],
        compiler_params=pltpu.CompilerParams(vmem_limit_bytes=VMEM),
        name="key_value",
    )(place, normed, *parts_a, *parts_b, cosine, sine)


def asked_kernel(x_ref, gain_ref, w_ref, cos_ref, sin_ref, normed_ref, kv_ref):
    norm_kernel(x_ref, gain_ref, normed_ref)
    raw = jnp.dot(normed_ref[...], w_ref[...], preferred_element_type=jnp.float32)
    for head in range(KVHEADS):
        cols = slice(head * HDIM, (head + 1) * HDIM)
        kv_ref[:, cols] = spin(raw[:, cols], cos_ref[...], sin_ref[...]).astype(jnp.bfloat16)
    kv_ref[:, KW:] = raw[:, KW:].astype(jnp.bfloat16)


def asked_key_value(rows, gain, w_kv, cosine, sine):
    return pl.pallas_call(
        asked_kernel,
        out_shape=[
            jax.ShapeDtypeStruct(rows.shape, jnp.bfloat16),
            jax.ShapeDtypeStruct((rows.shape[0], 2 * KW), jnp.bfloat16),
        ],
        compiler_params=pltpu.CompilerParams(vmem_limit_bytes=VMEM),
        name="asked_key_value",
    )(rows, gain, w_kv, cosine, sine)


def query_kernel(
    source_ref, normed_ref, asked_ref, mine_ref, other_ref, cos_ref, sin_ref, out_ref, last_ref, w_ref, sems
):
    ranks, depth, _ = w_ref.shape
    strip = mine_ref.shape[2]
    zs = mine_ref.shape[0]
    step = pl.program_id(0)

    @pl.when(step == 0)
    def _():
        def copy(ref, index, q):
            return pltpu.make_async_copy(
                ref.at[index], w_ref.at[:, pl.ds(q * strip, strip)], sems.at[q]
            )

        for q in range(depth // strip):
            source = source_ref[q]

            @pl.when(source < zs)
            def _():
                copy(mine_ref, jnp.minimum(source, zs - 1), q).start()

            @pl.when(source >= zs)
            def _():
                copy(other_ref, jnp.maximum(source - zs, 0), q).start()

        for q in range(depth // strip):
            copy(mine_ref, 0, q).wait()

    rows, chunk = out_ref.shape
    tokens = cos_ref.shape[0]
    joined = jnp.concatenate([normed_ref[...], asked_ref[...]], axis=0)
    weights = w_ref[:, :, pl.ds(pl.multiple_of(step * chunk, HDIM), chunk)]
    raw = jnp.dot(joined, weights.reshape(ranks * depth, chunk), preferred_element_type=jnp.float32)
    for head in range(chunk // HDIM):
        cols = slice(head * HDIM, (head + 1) * HDIM)
        part = raw[:rows, cols].reshape(rows // tokens, tokens, HDIM)
        turned = spin(part, cos_ref[...][None], sin_ref[...][None])
        out_ref[:, cols] = turned.reshape(rows, HDIM).astype(jnp.bfloat16)
    last_ref[...] = raw[rows:]


def project_query(source, normed, asked, mine, other, cosine, sine):
    rows, width = normed.shape
    zs, ranks, strip, _ = mine.shape
    depth = width // ranks
    chunk = 2 * HDIM
    extra = 16
    table = pl.BlockSpec(cosine.shape, lambda i, s: (0, 0))
    anywhere = pl.BlockSpec(memory_space=pl.ANY)
    return pl.pallas_call(
        query_kernel,
        grid_spec=pltpu.PrefetchScalarGridSpec(
            num_scalar_prefetch=1,
            grid=(QW // chunk,),
            in_specs=[
                pl.BlockSpec((rows, width), lambda i, s: (0, 0)),
                pl.BlockSpec((extra, width), lambda i, s: (0, 0)),
                anywhere,
                anywhere,
                table,
                table,
            ],
            out_specs=[
                pl.BlockSpec((rows, chunk), lambda i, s: (0, i)),
                pl.BlockSpec((extra, chunk), lambda i, s: (0, i)),
            ],
            scratch_shapes=[
                pltpu.VMEM((ranks, depth, QW), jnp.bfloat16),
                pltpu.SemaphoreType.DMA((depth // strip,)),
            ],
        ),
        out_shape=[
            jax.ShapeDtypeStruct((rows, QW), jnp.bfloat16),
            jax.ShapeDtypeStruct((extra, QW), jnp.float32),
        ],
        compiler_params=pltpu.CompilerParams(vmem_limit_bytes=VMEM),
        name="project_query",
    )(source, normed, asked, mine, other, cosine, sine)


def attend_kernel(
    want_ref, slot_ref, length_ref, where_ref, q_ref, *rest, swapped, start, absent
):
    parts, kpos_ref = rest[:5], rest[5]
    out_ref, held, zeros, sems = rest[-4:]
    blocks, tokens, _ = q_ref.shape
    slots = slot_ref.shape[0]
    base = where_ref[0]
    row = where_ref[1]
    rows = PER * tokens
    zeros[...] = jnp.zeros_like(zeros)

    def attend_block(block, groups):
        length = length_ref[start + block]
        kpos = kpos_ref[0:1, : groups * SIDE * tokens]
        qpos = base + lax.rem(lax.broadcasted_iota(jnp.int32, (rows, 1), 0), tokens)
        allowed = (kpos <= qpos) & (kpos < length)
        kept = (base + lax.broadcasted_iota(jnp.int32, (tokens, 1), 0)) < length

        def side_by_side(first):
            picked = []
            for dx in BACK[:groups]:
                for dy in range(SIDE):
                    ref, index = part_of(parts, swapped, dx, dy)
                    picked.append(ref[index, block, :, first : first + HDIM])
            return jnp.concatenate(picked, axis=0)

        for g in range(KVHEADS):
            heads = range(g * PER, (g + 1) * PER)
            queries = jnp.concatenate(
                [q_ref[block, :, h * HDIM : (h + 1) * HDIM] for h in heads], axis=0
            )
            logits = lax.dot_general(
                queries,
                side_by_side(g * HDIM),
                (((1,), (1,)), ((), ())),
                preferred_element_type=jnp.float32,
            )
            logits = jnp.where(allowed, logits * SCALE2, -1e30)
            weights = jnp.exp2(logits - jnp.max(logits, axis=-1, keepdims=True))
            total = jnp.sum(weights, axis=-1, keepdims=True)
            mixed = jnp.dot(
                weights.astype(jnp.bfloat16),
                side_by_side(KW + g * HDIM),
                preferred_element_type=jnp.float32,
            ) / total
            for h in heads:
                at = (h - g * PER) * tokens
                held[block, :, h * HDIM : (h + 1) * HDIM] = jnp.where(
                    kept, mixed[at : at + tokens], 0.0
                ).astype(jnp.bfloat16)

    def each_block(groups):
        def body(block, carry):
            @pl.when((want_ref[start + block] > 0) & (base < length_ref[start + block]))
            def _():
                attend_block(block, groups)

            return carry

        lax.fori_loop(0, blocks, body, 0)

    for x in range(SIDE):

        @pl.when(row == x)
        def _(x=x):
            each_block(x + 1)

    def copies(slot, act):
        block = slot_ref[slot]
        here = (block >= start) & (block < start + blocks)
        local = jnp.clip(block - start, 0, blocks - 1)
        filled = here & (base < length_ref[start + local])
        empty = here & jnp.logical_not(base < length_ref[start + local])
        if absent:
            empty = empty | (block < 0)

        @pl.when(filled)
        def _():
            act(pltpu.make_async_copy(held.at[local], out_ref.at[slot], sems.at[slot]))

        @pl.when(empty)
        def _():
            act(pltpu.make_async_copy(zeros, out_ref.at[slot], sems.at[slot]))

    def send(slot, carry):
        copies(slot, lambda copy: copy.start())
        return carry

    def finish(slot, carry):
        copies(slot, lambda copy: copy.wait())
        return carry

    lax.fori_loop(0, slots, send, 0)
    lax.fori_loop(0, slots, finish, 0)


def attend(want, slot_block, lengths, where, queries, parts, kpos, swapped, start, earlier):
    blocks = parts[0].shape[1]
    _, tokens, width = queries.shape
    slots = slot_block.shape[0]
    anywhere = pl.BlockSpec(memory_space=pl.ANY)

    def whole(array):
        return pl.BlockSpec(array.shape, lambda i, *_: (0,) * array.ndim)

    given = () if earlier is None else (earlier,)
    return pl.pallas_call(
        lambda *refs: attend_kernel(
            *refs, swapped=swapped, start=start, absent=earlier is None
        ),
        grid_spec=pltpu.PrefetchScalarGridSpec(
            num_scalar_prefetch=4,
            grid=(1,),
            in_specs=[
                pl.BlockSpec((blocks, tokens, width), lambda i, *_: (start // blocks, 0, 0)),
                *[whole(part) for part in parts],
                whole(kpos),
                *[anywhere for _ in given],
            ],
            out_specs=anywhere,
            scratch_shapes=[
                pltpu.VMEM((blocks, tokens, width), jnp.bfloat16),
                pltpu.VMEM((tokens, width), jnp.bfloat16),
                pltpu.SemaphoreType.DMA((slots,)),
            ],
        ),
        out_shape=jax.ShapeDtypeStruct((slots, tokens, width), jnp.bfloat16),
        input_output_aliases={11: 0} if given else {},
        compiler_params=pltpu.CompilerParams(vmem_limit_bytes=VMEM),
        name="attend_second" if given else "attend_first",
    )(want, slot_block, lengths, where, queries, *parts, kpos, *given)


def score_kernel(count_ref, block_ref, length_ref, which_ref, size_ref, last_ref, *rest):
    parts_a, parts_b, rest = rest[:5], rest[5:10], rest[10:]
    qkv_ref, kpos_ref, cos_ref, sin_ref, w_ref, out_ref, kv_ref, sems = rest
    half, q_tokens, q_dev = size_ref[0], size_ref[1], size_ref[2]
    count = count_ref[0]

    def fetch(step, act):
        slot = lax.rem(step, 2)
        block = block_ref[step]
        for which, parts in enumerate((parts_a, parts_b)):

            @pl.when((block >= half) if which else (block < half))
            def _(which=which, parts=parts):
                local = jnp.clip(block - which * half, 0, parts[0].shape[1] - 1)
                at = 0
                for number, part in enumerate(parts):
                    size = part.shape[0]
                    act(
                        pltpu.make_async_copy(
                            part.at[:, local], kv_ref.at[slot, pl.ds(at, size)], sems.at[slot, number]
                        )
                    )
                    at += size

    @pl.when(count > 0)
    def _():
        fetch(0, lambda copy: copy.start())

    def body(step, carry):
        @pl.when(step + 1 < count)
        def _():
            fetch(step + 1, lambda copy: copy.start())

        fetch(step, lambda copy: copy.wait())
        slot = lax.rem(step, 2)
        length = length_ref[step]
        which = which_ref[step]
        second = (block_ref[step] >= half).astype(jnp.int32)
        kpos = kpos_ref[pl.ds(second, 1), :]
        live = kpos < length
        span = qkv_ref.shape[0]
        lane = lax.broadcasted_iota(jnp.int32, (1, span), 1)
        own = lax.rem(lax.div(lane, q_tokens), q_dev) == which
        at_far = pl.ds(length + QLEN - 1, 1)
        far_cos, far_sin = cos_ref[at_far, :], sin_ref[at_far, :]
        near_cos, near_sin = cos_ref[QLEN - 1 : QLEN, :], sin_ref[QLEN - 1 : QLEN, :]
        total_score = jnp.zeros((1, HDIM), jnp.float32)
        over = (((1,), (1,)), ((), ()))
        for g in range(KVHEADS):
            raw = last_ref[which, g]
            far = spin(raw, far_cos, far_sin).astype(jnp.bfloat16)
            near = spin(raw, near_cos, near_sin).astype(jnp.bfloat16)
            keys = kv_ref[slot, :, :, g * HDIM : (g + 1) * HDIM].reshape(BLK, HDIM)
            values = kv_ref[slot, :, :, KW + g * HDIM : KW + (g + 1) * HDIM].reshape(BLK, HDIM)
            passage = lax.dot_general(far, keys, over, preferred_element_type=jnp.float32)
            question = lax.dot_general(
                near,
                qkv_ref[:, g * HDIM : (g + 1) * HDIM],
                over,
                preferred_element_type=jnp.float32,
            )
            passage = jnp.where(live, passage * SCALE2, -1e30)
            question = jnp.where(own, question * SCALE2, -1e30)
            peak = jnp.maximum(
                jnp.max(passage, axis=-1, keepdims=True), jnp.max(question, axis=-1, keepdims=True)
            )
            passage = jnp.exp2(passage - peak)
            question = jnp.exp2(question - peak)
            total = jnp.sum(passage, axis=-1, keepdims=True) + jnp.sum(
                question, axis=-1, keepdims=True
            )
            mixed = jnp.dot(
                passage.astype(jnp.bfloat16), values, preferred_element_type=jnp.float32
            ) + jnp.dot(
                question.astype(jnp.bfloat16),
                qkv_ref[:, KW + g * HDIM : KW + (g + 1) * HDIM],
                preferred_element_type=jnp.float32,
            )
            context = (mixed / total).astype(jnp.bfloat16).astype(jnp.float32)
            total_score += jnp.sum(context * w_ref[g], axis=0, keepdims=True)
        result = jnp.sum(total_score, axis=-1, keepdims=True)
        out_ref[pl.ds(step, 1), :] = jnp.broadcast_to(result, (1, HDIM))
        return carry

    lax.fori_loop(0, count, body, 0)


def score(
    count, blocks, lengths, which, sizes, last, first, second, question_kv, kpos, cosine, sine, w
):
    slots = blocks.shape[0]
    anywhere = pl.BlockSpec(memory_space=pl.ANY)
    tokens = first[0].shape[2]

    def whole(array):
        return pl.BlockSpec(array.shape, lambda i, *_: (0,) * array.ndim)

    return pl.pallas_call(
        score_kernel,
        grid_spec=pltpu.PrefetchScalarGridSpec(
            num_scalar_prefetch=5,
            grid=(1,),
            in_specs=[
                whole(last),
                *[anywhere] * 10,
                whole(question_kv),
                whole(kpos),
                whole(cosine),
                whole(sine),
                whole(w),
            ],
            out_specs=pl.BlockSpec((slots, HDIM), lambda i, *_: (0, 0)),
            scratch_shapes=[
                pltpu.VMEM((2, SIDE * SIDE, tokens, 2 * KW), jnp.bfloat16),
                pltpu.SemaphoreType.DMA((2, 5)),
            ],
        ),
        out_shape=jax.ShapeDtypeStruct((slots, HDIM), jnp.float32),
        compiler_params=pltpu.CompilerParams(vmem_limit_bytes=VMEM),
        name="score",
    )(
        count,
        blocks,
        lengths,
        which,
        jnp.array([first[0].shape[1], *sizes], jnp.int32),
        last,
        *first,
        *second,
        question_kv,
        kpos,
        cosine,
        sine,
        w,
    )


def sorted_by(key):
    count = key.shape[0]
    place = jnp.arange(count, dtype=jnp.int32)
    ahead = (key[None, :] < key[:, None]) | (
        (key[None, :] == key[:, None]) & (place[None, :] < place[:, None])
    )
    rank = jnp.sum(ahead.astype(jnp.int32), axis=1)
    chosen = rank[None, :] == place[:, None]

    def arrange(values):
        return jnp.sum(jnp.where(chosen, values[None, :], 0), axis=1).astype(jnp.int32)

    return arrange


def on_device(
    store_rows,
    block_lengths,
    queries,
    cand_owner,
    cand_block,
    cand_query,
    norm_gain,
    w_query,
    w_key,
    w_value,
    w_score,
):
    n_corpus = lax.axis_size("corpus")
    n_rerank = lax.axis_size("rerank")
    corpus_index = lax.axis_index("corpus")
    member = lax.axis_index("rerank")
    pair_total = cand_block.shape[0]
    pair_group = pair_total // n_corpus
    own_blocks, tokens, width = store_rows.shape
    n_query, q_tokens, _ = queries.shape
    q_dev = n_query // n_rerank
    half_blocks = own_blocks // 2

    owners = cand_owner[:, 0]
    pair_order = jnp.arange(pair_total, dtype=jnp.int32)
    group_of = pair_order // pair_group
    earlier = (
        (owners[:, None] == owners[None, :])
        & (group_of[:, None] == group_of[None, :])
        & (pair_order[None, :] < pair_order[:, None])
    )
    owner_rank = jnp.sum(earlier.astype(jnp.int32), axis=1)
    slot_ids = jnp.arange(n_corpus * CAP, dtype=jnp.int32)
    wanted = (
        (group_of[None, :] == (slot_ids // CAP)[:, None])
        & (owners[None, :] == corpus_index)
        & (owner_rank[None, :] == (slot_ids % CAP)[:, None])
    )
    present = jnp.any(wanted, axis=1)

    def of_slot(values):
        return jnp.sum(jnp.where(wanted, values[None, :], 0), axis=1)

    slot_block, slot_query, slot_pair = of_slot(cand_block), of_slot(cand_query), of_slot(pair_order)
    own_lengths = lax.dynamic_slice_in_dim(block_lengths, corpus_index * own_blocks, own_blocks, 0)
    block_ids = jnp.arange(own_blocks, dtype=jnp.int32)
    slot_length = jnp.sum(
        jnp.where(slot_block[:, None] == block_ids[None, :], own_lengths[None, :], 0), axis=1
    )
    want = jnp.any(
        present[:, None] & (slot_block[:, None] == block_ids[None, :]), axis=0
    ).astype(jnp.int32)
    slot_or_none = jnp.where(present, slot_block, -1)
    mine = present & (slot_query // q_dev == member)
    by_mine = sorted_by(jnp.where(mine, slot_block, own_blocks))
    mine_count = jnp.sum(mine.astype(jnp.int32)).reshape(1)
    mine_block, mine_length = by_mine(slot_block), by_mine(slot_length)
    mine_which, mine_pair = by_mine(slot_query % q_dev), by_mine(slot_pair)

    depth = w_key.shape[0]
    core, z = corpus_index % 2, corpus_index // 2
    strip = w_query.shape[0] * 2 // (2 * n_corpus - 2)
    strips = depth // strip
    my_strip = lax.dynamic_slice_in_dim(
        w_query, jnp.minimum(corpus_index, strips - 1) * strip, strip, 0
    )
    strip_rows = lax.all_gather(my_strip, "rerank", axis=0, tiled=False)
    w_kv_own = jnp.concatenate([w_key, w_value], axis=1)
    half = depth // 2
    w_first, w_second = plane_gather(w_kv_own[:half], w_kv_own[half:], half // 32 * 16)
    gain = norm_gain.astype(jnp.float32).reshape(1, width)
    row_count = own_blocks * tokens
    normed = norm(store_rows.reshape(row_count, width), gain)

    all_cos, all_sin = rope_tables(jnp.arange(BLK + QLEN, dtype=jnp.int32))
    base = member * tokens
    own_cos, own_sin = rope_tables(base + jnp.arange(tokens, dtype=jnp.int32))
    x, y = member // SIDE, member % SIDE
    hops = jnp.array(HOPS, jnp.int32)
    xs, ys = (x + hops) % SIDE, (y + hops) % SIDE
    place = (xs[:, None] * SIDE + ys[None, :]).reshape(SIDE * SIDE)
    kv, w_kv = key_value(place, normed, w_first, w_second, own_cos, own_sin, n_rerank)
    passage_kv = kv.reshape(own_blocks, tokens, 2 * KW)
    first, second = plane_gather(
        passage_kv[:half_blocks], passage_kv[half_blocks:], half_blocks // 2
    )

    sent, _ = tie(queries, kv)
    asked = lax.all_to_all(
        sent.reshape(n_rerank, q_dev * q_tokens * width), "rerank", 0, 0, tiled=True
    )
    asked = asked[::-1].reshape(n_rerank * q_dev * q_tokens, width)
    asked_row = jnp.arange(asked.shape[0], dtype=jnp.int32)
    per_member = q_dev * q_tokens
    asked_token = q_tokens * (n_rerank - 1 - asked_row // per_member) + asked_row % q_tokens
    asked_cos, asked_sin = rope_tables(asked_token)
    asked_normed, question_kv = asked_key_value(
        asked, gain, w_kv.reshape(width, 2 * KW), asked_cos, asked_sin
    )

    def along_z(value, step):
        perm = [(i, ((i // 2 + step) % SIDE) * 2 + i % 2) for i in range(n_corpus)]
        return lax.ppermute(value, "corpus", perm)

    z_low, z_high = along_z(strip_rows, 1), along_z(strip_rows, -1)
    half_rank = n_rerank // 2
    z_far = jnp.concatenate(
        [along_z(z_low[:half_rank], 1), along_z(z_high[half_rank:], -1)], axis=0
    )
    mine_strips = jnp.stack([strip_rows, z_low, z_high, z_far])
    other_strips = lax.ppermute(
        mine_strips, "corpus", [(i, i + 1 - 2 * (i % 2)) for i in range(n_corpus)]
    )
    strip_ids = jnp.arange(strips, dtype=jnp.int32)
    back = jnp.array([0, 2, 3, 1], jnp.int32)
    away = jnp.take(back, (strip_ids // 2 - z) % SIDE)
    source = jnp.where(strip_ids % 2 == core, away, away + SIDE).astype(jnp.int32)
    query_rot, query_last = project_query(
        source, normed, asked_normed, mine_strips, other_strips, own_cos, own_sin
    )

    inside = jnp.arange(tokens, dtype=jnp.int32)

    def positions_of(ranks):
        return (ranks[..., None] * tokens + inside).reshape(1, BLK)

    xb = (x - jnp.arange(SIDE, dtype=jnp.int32)) % SIDE
    kpos = positions_of(xb[:, None] * SIDE + ys[None, :])
    part_pos = jnp.concatenate(
        [
            positions_of(xs[:, None] * SIDE + ys[None, :]),
            positions_of(xs[None, :] * SIDE + ys[:, None]),
        ]
    )

    last = query_last[q_tokens - 1 : per_member : q_tokens].reshape(q_dev, KVHEADS, PER, HDIM)
    last = jnp.pad(last, ((0, 0), (0, 0), (0, 8 - PER), (0, 0)))
    head_w = jnp.pad(
        w_score.astype(jnp.float32).reshape(KVHEADS, PER, HDIM), ((0, 0), (0, 8 - PER), (0, 0))
    )
    scored = score(
        mine_count,
        mine_block,
        mine_length,
        mine_which,
        (q_tokens, q_dev),
        last,
        first,
        second,
        question_kv,
        part_pos,
        all_cos,
        all_sin,
        head_w,
    )[: n_corpus * CAP, 0]
    valid = slot_ids < mine_count[0]
    placed = jnp.sum(
        jnp.where(
            valid[:, None] & (mine_pair[:, None] == pair_order[None, :]), scored[:, None], 0.0
        ),
        axis=0,
    )
    shared = jnp.sum(
        lax.all_to_all(placed.reshape(n_corpus, pair_group), "corpus", 0, 0, tiled=True), axis=0
    )
    pair_scores = jnp.sum(
        lax.all_to_all(
            shared.reshape(n_rerank, pair_group // n_rerank), "rerank", 0, 0, tiled=True
        ),
        axis=0,
    )
    where = jnp.stack([base, x]).astype(jnp.int32)
    query_rot = query_rot.reshape(own_blocks, tokens, QW)
    begun = attend(
        want, slot_or_none, own_lengths, where, query_rot, first, kpos, False, 0, None
    )
    passage_context = attend(
        want, slot_or_none, own_lengths, where, query_rot, second, kpos, True, half_blocks, begun
    )
    return (passage_context, pair_scores)


def solution(mesh):
    placed = (
        P("corpus", "rerank", None),
        P(),
        P(None, "rerank", None),
        P(),
        P(),
        P(),
        P(),
        P("rerank", None),
        P("rerank", None),
        P("rerank", None),
        P(),
    )
    return jax.shard_map(
        on_device,
        mesh=mesh,
        in_specs=placed,
        out_specs=(P("corpus", "rerank", None), P(("corpus", "rerank"))),
        check_vma=False,
    )
```

```python
import jax
import jax.numpy as jnp
from jax import lax
from jax.experimental import pallas as pl
from jax.experimental.pallas import tpu as pltpu
from jax.sharding import PartitionSpec as P

HDIM = 128
QHEADS = 14
KVHEADS = 2
PER = QHEADS // KVHEADS
QW = QHEADS * HDIM
KW = KVHEADS * HDIM
BLK = 512
QLEN = 64
CAP = 5
SIDE = 4
ROPE_BASE = 1000000.0
EPSILON = 1e-06
SCALE2 = HDIM ** (-0.5) * 1.4426950408889634
VMEM = 56 * 1024 * 1024


def rope_tables(positions):
    half = HDIM // 2
    inverse = jnp.power(ROPE_BASE, -2.0 * jnp.arange(half, dtype=jnp.float32) / HDIM)
    angles = positions.astype(jnp.float32)[:, None] * inverse
    cosine, sine = jnp.cos(angles), jnp.sin(angles)
    return (
        jnp.concatenate([cosine, cosine], axis=1),
        jnp.concatenate([-sine, sine], axis=1),
    )


def spin(part, cosine, sine):
    return part * cosine + pltpu.roll(part, HDIM // 2, part.ndim - 1) * sine


def shift(value, dim, step):
    def moved(index):
        x, y = index // SIDE, index % SIDE
        if dim == "x":
            x = (x + step) % SIDE
        else:
            y = (y + step) % SIDE
        return x * SIDE + y

    return lax.ppermute(value, "rerank", [(i, moved(i)) for i in range(SIDE * SIDE)])


def tie(*values):
    return lax.optimization_barrier(values)


def plane_gather(value_a, value_b):
    cut = value_a.shape[0] // 2
    a_low, a_high = shift(value_a, "y", 1), shift(value_a, "y", -1)
    b_low, b_high = shift(value_b, "x", 1), shift(value_b, "x", -1)
    a_low, a_high, b_low, b_high = tie(a_low, a_high, b_low, b_high)
    a_far = shift(a_low[:cut], "y", 1), shift(a_high[cut:], "y", -1)
    b_far = shift(b_low[:cut], "x", 1), shift(b_high[cut:], "x", -1)
    a0, b0 = jnp.stack([value_a, a_low]), jnp.stack([value_b, b_low])
    a0_low, a0_high = shift(a0, "x", 1), shift(a0, "x", -1)
    b0_low, b0_high = shift(b0, "y", 1), shift(b0, "y", -1)
    a_far, b_far = tie(a_far, b_far)
    a1 = jnp.stack([a_high, jnp.concatenate(a_far, axis=0)])
    b1 = jnp.stack([b_high, jnp.concatenate(b_far, axis=0)])
    a1_low, a1_high = shift(a1, "x", 1), shift(a1, "x", -1)
    b1_low, b1_high = shift(b1, "y", 1), shift(b1, "y", -1)
    a0_low, b0_low = tie(a0_low, b0_low)
    a0_far, b0_far = shift(a0_low, "x", 1), shift(b0_low, "y", 1)
    a1_high, b1_high = tie(a1_high, b1_high)
    a1_far, b1_far = shift(a1_high, "x", -1), shift(b1_high, "y", -1)
    return (
        (a0, a1, a0_low, a1_low, a0_high, a1_high, a0_far, a1_far),
        (b0, b1, b0_low, b1_low, b0_high, b1_high, b0_far, b1_far),
    )


PARTS = 8
HOPS = (0, -1, 1, 2)
BACK = (0, 1, 3, 2)


def part_of(parts, swapped, dx, dy):
    outer, inner = (dy, dx) if swapped else (dx, dy)
    return parts[2 * outer + inner // 2], inner % 2


def norm_kernel(x_ref, gain_ref, out_ref):
    wide = x_ref[...].astype(jnp.float32)
    inverse = lax.rsqrt(jnp.mean(wide * wide, axis=-1, keepdims=True) + EPSILON)
    out_ref[...] = (wide * inverse * gain_ref[...]).astype(jnp.bfloat16)


def norm(rows, gain):
    tile = 128
    width = rows.shape[1]
    block = pl.BlockSpec((tile, width), lambda i: (i, 0))
    return pl.pallas_call(
        norm_kernel,
        grid=(rows.shape[0] // tile,),
        in_specs=[block, pl.BlockSpec((1, width), lambda i: (0, 0))],
        out_specs=block,
        out_shape=jax.ShapeDtypeStruct(rows.shape, jnp.bfloat16),
        compiler_params=pltpu.CompilerParams(vmem_limit_bytes=VMEM),
        name="norm",
    )(rows, gain)


def key_value_kernel(normed_ref, w_ref, cos_ref, sin_ref, kv_ref):
    rows = normed_ref.shape[0]
    tokens = cos_ref.shape[0]
    raw = jnp.dot(normed_ref[...], w_ref[...], preferred_element_type=jnp.float32)
    for head in range(KVHEADS):
        cols = slice(head * HDIM, (head + 1) * HDIM)
        part = raw[:, cols].reshape(rows // tokens, tokens, HDIM)
        turned = spin(part, cos_ref[...][None], sin_ref[...][None])
        kv_ref[:, cols] = turned.reshape(rows, HDIM).astype(jnp.bfloat16)
    kv_ref[:, KW:] = raw[:, KW:].astype(jnp.bfloat16)


def key_value(normed, w_kv, cosine, sine):
    tile = 256
    rows, width = normed.shape
    table = pl.BlockSpec(cosine.shape, lambda i: (0, 0))
    return pl.pallas_call(
        key_value_kernel,
        grid=(rows // tile,),
        in_specs=[
            pl.BlockSpec((tile, width), lambda i: (i, 0)),
            pl.BlockSpec((width, 2 * KW), lambda i: (0, 0)),
            table,
            table,
        ],
        out_specs=pl.BlockSpec((tile, 2 * KW), lambda i: (i, 0)),
        out_shape=jax.ShapeDtypeStruct((rows, 2 * KW), jnp.bfloat16),
        compiler_params=pltpu.CompilerParams(vmem_limit_bytes=VMEM),
        name="key_value",
    )(normed, w_kv, cosine, sine)


def asked_kernel(x_ref, gain_ref, w_ref, cos_ref, sin_ref, normed_ref, kv_ref):
    norm_kernel(x_ref, gain_ref, normed_ref)
    raw = jnp.dot(normed_ref[...], w_ref[...], preferred_element_type=jnp.float32)
    for head in range(KVHEADS):
        cols = slice(head * HDIM, (head + 1) * HDIM)
        kv_ref[:, cols] = spin(raw[:, cols], cos_ref[...], sin_ref[...]).astype(jnp.bfloat16)
    kv_ref[:, KW:] = raw[:, KW:].astype(jnp.bfloat16)


def asked_key_value(rows, gain, w_kv, cosine, sine):
    return pl.pallas_call(
        asked_kernel,
        out_shape=[
            jax.ShapeDtypeStruct(rows.shape, jnp.bfloat16),
            jax.ShapeDtypeStruct((rows.shape[0], 2 * KW), jnp.bfloat16),
        ],
        compiler_params=pltpu.CompilerParams(vmem_limit_bytes=VMEM),
        name="asked_key_value",
    )(rows, gain, w_kv, cosine, sine)


def query_kernel(column_ref, *refs):
    strips, (normed_ref, asked_ref, cos_ref, sin_ref, out_ref, last_ref) = refs[:PARTS], refs[PARTS:-4]
    w_ref, x_ref, w_sems, x_sems = refs[-4:]
    step = pl.program_id(0)
    rows, chunk = out_ref.shape
    tokens = cos_ref.shape[0]
    extra = asked_ref.shape[0]

    def fetch(number):
        return pltpu.make_async_copy(strips[number], w_ref.at[number], w_sems.at[number])

    inputs = (
        pltpu.make_async_copy(normed_ref, x_ref.at[pl.ds(0, rows)], x_sems.at[0]),
        pltpu.make_async_copy(asked_ref, x_ref.at[pl.ds(rows, extra)], x_sems.at[1]),
    )

    @pl.when(step == 0)
    def _():
        for copy in inputs:
            copy.start()
        for number in range(PARTS):
            fetch(number).start()
        for copy in inputs:
            copy.wait()

    for number in range(PARTS):

        @pl.when(step == number)
        def _(number=number):
            fetch(number).wait()

    raw = jnp.dot(x_ref[...], w_ref[step], preferred_element_type=jnp.float32)
    for head in range(chunk // HDIM):
        cols = slice(head * HDIM, (head + 1) * HDIM)
        part = raw[:rows, cols].reshape(rows // tokens, tokens, HDIM)
        turned = spin(part, cos_ref[...][None], sin_ref[...][None])
        out_ref[:, cols] = turned.reshape(rows, HDIM).astype(jnp.bfloat16)
    last_ref[...] = raw[rows:]


def project_query(column, strips, normed, asked, cosine, sine):
    rows, width = normed.shape
    chunk = strips[0].shape[1]
    extra = asked.shape[0]
    table = pl.BlockSpec(cosine.shape, lambda i, c: (0, 0))
    anywhere = pl.BlockSpec(memory_space=pl.ANY)
    return pl.pallas_call(
        query_kernel,
        grid_spec=pltpu.PrefetchScalarGridSpec(
            num_scalar_prefetch=1,
            grid=(PARTS,),
            in_specs=[*[anywhere] * PARTS, anywhere, anywhere, table, table],
            out_specs=[
                pl.BlockSpec((rows, chunk), lambda i, c: (0, c[i])),
                pl.BlockSpec((extra, chunk), lambda i, c: (0, c[i])),
            ],
            scratch_shapes=[
                pltpu.VMEM((PARTS, width, chunk), jnp.bfloat16),
                pltpu.VMEM((rows + extra, width), jnp.bfloat16),
                pltpu.SemaphoreType.DMA((PARTS,)),
                pltpu.SemaphoreType.DMA((2,)),
            ],
        ),
        out_shape=[
            jax.ShapeDtypeStruct((rows, PARTS * chunk), jnp.bfloat16),
            jax.ShapeDtypeStruct((extra, PARTS * chunk), jnp.float32),
        ],
        compiler_params=pltpu.CompilerParams(vmem_limit_bytes=VMEM),
        name="project_query",
    )(column, *strips, normed, asked, cosine, sine)


def attend_kernel(
    want_ref, slot_ref, length_ref, where_ref, q_ref, *rest, swapped, start, absent
):
    parts, kpos_ref = rest[:PARTS], rest[PARTS]
    out_ref, held, zeros, sems = rest[-4:]
    blocks, tokens, _ = q_ref.shape
    slots = slot_ref.shape[0]
    base = where_ref[0]
    row = where_ref[1]
    rows = PER * tokens
    zeros[...] = jnp.zeros_like(zeros)

    def attend_block(block, groups):
        length = length_ref[start + block]
        kpos = kpos_ref[0:1, : groups * SIDE * tokens]
        qpos = base + lax.rem(lax.broadcasted_iota(jnp.int32, (rows, 1), 0), tokens)
        allowed = (kpos <= qpos) & (kpos < length)
        kept = (base + lax.broadcasted_iota(jnp.int32, (tokens, 1), 0)) < length

        def side_by_side(first):
            picked = []
            for dx in BACK[:groups]:
                for dy in range(SIDE):
                    ref, index = part_of(parts, swapped, dx, dy)
                    picked.append(ref[index, block, :, first : first + HDIM])
            return jnp.concatenate(picked, axis=0)

        for g in range(KVHEADS):
            heads = range(g * PER, (g + 1) * PER)
            queries = jnp.concatenate(
                [q_ref[block, :, h * HDIM : (h + 1) * HDIM] for h in heads], axis=0
            )
            logits = lax.dot_general(
                queries,
                side_by_side(g * HDIM),
                (((1,), (1,)), ((), ())),
                preferred_element_type=jnp.float32,
            )
            logits = jnp.where(allowed, logits * SCALE2, -1e30)
            weights = jnp.exp2(logits - jnp.max(logits, axis=-1, keepdims=True))
            total = jnp.sum(weights, axis=-1, keepdims=True)
            mixed = jnp.dot(
                weights.astype(jnp.bfloat16),
                side_by_side(KW + g * HDIM),
                preferred_element_type=jnp.float32,
            ) / total
            for h in heads:
                at = (h - g * PER) * tokens
                held[block, :, h * HDIM : (h + 1) * HDIM] = jnp.where(
                    kept, mixed[at : at + tokens], 0.0
                ).astype(jnp.bfloat16)

    def each_block(groups):
        def body(block, carry):
            @pl.when((want_ref[start + block] > 0) & (base < length_ref[start + block]))
            def _():
                attend_block(block, groups)

            return carry

        lax.fori_loop(0, blocks, body, 0)

    for x in range(SIDE):

        @pl.when(row == x)
        def _(x=x):
            each_block(x + 1)

    def copies(slot, act):
        block = slot_ref[slot]
        here = (block >= start) & (block < start + blocks)
        local = jnp.clip(block - start, 0, blocks - 1)
        filled = here & (base < length_ref[start + local])
        empty = here & jnp.logical_not(base < length_ref[start + local])
        if absent:
            empty = empty | (block < 0)

        @pl.when(filled)
        def _():
            act(pltpu.make_async_copy(held.at[local], out_ref.at[slot], sems.at[slot]))

        @pl.when(empty)
        def _():
            act(pltpu.make_async_copy(zeros, out_ref.at[slot], sems.at[slot]))

    def send(slot, carry):
        copies(slot, lambda copy: copy.start())
        return carry

    def finish(slot, carry):
        copies(slot, lambda copy: copy.wait())
        return carry

    lax.fori_loop(0, slots, send, 0)
    lax.fori_loop(0, slots, finish, 0)


def attend(want, slot_block, lengths, where, queries, parts, kpos, swapped, start, earlier):
    blocks, tokens = parts[0].shape[1:3]
    width = QW
    slots = slot_block.shape[0]
    anywhere = pl.BlockSpec(memory_space=pl.ANY)

    def whole(array):
        return pl.BlockSpec(array.shape, lambda i, *_: (0,) * array.ndim)

    given = () if earlier is None else (earlier,)
    return pl.pallas_call(
        lambda *refs: attend_kernel(
            *refs, swapped=swapped, start=start, absent=earlier is None
        ),
        grid_spec=pltpu.PrefetchScalarGridSpec(
            num_scalar_prefetch=4,
            grid=(1,),
            in_specs=[
                pl.BlockSpec((blocks, tokens, width), lambda i, *_: (start // blocks, 0, 0)),
                *[whole(part) for part in parts],
                whole(kpos),
                *[anywhere for _ in given],
            ],
            out_specs=anywhere,
            scratch_shapes=[
                pltpu.VMEM((blocks, tokens, width), jnp.bfloat16),
                pltpu.VMEM((tokens, width), jnp.bfloat16),
                pltpu.SemaphoreType.DMA((slots,)),
            ],
        ),
        out_shape=jax.ShapeDtypeStruct((slots, tokens, width), jnp.bfloat16),
        input_output_aliases={6 + PARTS: 0} if given else {},
        compiler_params=pltpu.CompilerParams(vmem_limit_bytes=VMEM),
        name="attend_second" if given else "attend_first",
    )(want, slot_block, lengths, where, queries, *parts, kpos, *given)


def score_kernel(count_ref, block_ref, length_ref, which_ref, size_ref, last_ref, *rest):
    parts_a, parts_b, rest = rest[:PARTS], rest[PARTS : 2 * PARTS], rest[2 * PARTS :]
    qkv_ref, kpos_ref, cos_ref, sin_ref, w_ref, out_ref, kv_ref, sems = rest
    half, q_span = size_ref[0], size_ref[1]
    count = count_ref[0]

    def fetch(step, act):
        slot = lax.rem(step, 2)
        block = block_ref[step]
        for which, parts in enumerate((parts_a, parts_b)):

            @pl.when((block >= half) if which else (block < half))
            def _(which=which, parts=parts):
                local = jnp.clip(block - which * half, 0, parts[0].shape[1] - 1)
                for number, part in enumerate(parts):
                    held = kv_ref.at[slot, pl.ds(2 * number, 2)]
                    act(pltpu.make_async_copy(part.at[:, local], held, sems.at[slot, number]))

    @pl.when(count > 0)
    def _():
        fetch(0, lambda copy: copy.start())

    def body(step, carry):
        @pl.when(step + 1 < count)
        def _():
            fetch(step + 1, lambda copy: copy.start())

        fetch(step, lambda copy: copy.wait())
        slot = lax.rem(step, 2)
        length = length_ref[step]
        which = which_ref[step]
        second = (block_ref[step] >= half).astype(jnp.int32)
        kpos = kpos_ref[pl.ds(second, 1), :]
        live = kpos < length
        span = qkv_ref.shape[0]
        lane = lax.broadcasted_iota(jnp.int32, (1, span), 1)
        own = lax.div(lane, q_span) == which
        at_far = pl.ds(length + QLEN - 1, 1)
        far_cos, far_sin = cos_ref[at_far, :], sin_ref[at_far, :]
        near_cos, near_sin = cos_ref[QLEN - 1 : QLEN, :], sin_ref[QLEN - 1 : QLEN, :]
        total_score = jnp.zeros((1, HDIM), jnp.float32)
        over = (((1,), (1,)), ((), ()))
        for g in range(KVHEADS):
            raw = last_ref[which, g]
            far = spin(raw, far_cos, far_sin).astype(jnp.bfloat16)
            near = spin(raw, near_cos, near_sin).astype(jnp.bfloat16)
            keys = kv_ref[slot, :, :, g * HDIM : (g + 1) * HDIM].reshape(BLK, HDIM)
            values = kv_ref[slot, :, :, KW + g * HDIM : KW + (g + 1) * HDIM].reshape(BLK, HDIM)
            passage = lax.dot_general(far, keys, over, preferred_element_type=jnp.float32)
            question = lax.dot_general(
                near,
                qkv_ref[:, g * HDIM : (g + 1) * HDIM],
                over,
                preferred_element_type=jnp.float32,
            )
            passage = jnp.where(live, passage * SCALE2, -1e30)
            question = jnp.where(own, question * SCALE2, -1e30)
            peak = jnp.maximum(
                jnp.max(passage, axis=-1, keepdims=True), jnp.max(question, axis=-1, keepdims=True)
            )
            passage = jnp.exp2(passage - peak)
            question = jnp.exp2(question - peak)
            total = jnp.sum(passage, axis=-1, keepdims=True) + jnp.sum(
                question, axis=-1, keepdims=True
            )
            mixed = jnp.dot(
                passage.astype(jnp.bfloat16), values, preferred_element_type=jnp.float32
            ) + jnp.dot(
                question.astype(jnp.bfloat16),
                qkv_ref[:, KW + g * HDIM : KW + (g + 1) * HDIM],
                preferred_element_type=jnp.float32,
            )
            context = (mixed / total).astype(jnp.bfloat16).astype(jnp.float32)
            total_score += jnp.sum(context * w_ref[g], axis=0, keepdims=True)
        result = jnp.sum(total_score, axis=-1, keepdims=True)
        out_ref[pl.ds(step, 1), :] = jnp.broadcast_to(result, (1, HDIM))
        return carry

    lax.fori_loop(0, count, body, 0)


def score(
    count, blocks, lengths, which, last, first, second, question_kv, kpos, cosine, sine, w
):
    slots = blocks.shape[0]
    anywhere = pl.BlockSpec(memory_space=pl.ANY)
    tokens = first[0].shape[2]

    def whole(array):
        return pl.BlockSpec(array.shape, lambda i, *_: (0,) * array.ndim)

    return pl.pallas_call(
        score_kernel,
        grid_spec=pltpu.PrefetchScalarGridSpec(
            num_scalar_prefetch=5,
            grid=(1,),
            in_specs=[
                whole(last),
                *[anywhere] * (2 * PARTS),
                whole(question_kv),
                whole(kpos),
                whole(cosine),
                whole(sine),
                whole(w),
            ],
            out_specs=pl.BlockSpec((slots, HDIM), lambda i, *_: (0, 0)),
            scratch_shapes=[
                pltpu.VMEM((2, SIDE * SIDE, tokens, 2 * KW), jnp.bfloat16),
                pltpu.SemaphoreType.DMA((2, PARTS)),
            ],
        ),
        out_shape=jax.ShapeDtypeStruct((slots, HDIM), jnp.float32),
        compiler_params=pltpu.CompilerParams(vmem_limit_bytes=VMEM),
        name="score",
    )(
        count,
        blocks,
        lengths,
        which,
        jnp.array([first[0].shape[1], QLEN], jnp.int32),
        last,
        *first,
        *second,
        question_kv,
        kpos,
        cosine,
        sine,
        w,
    )


def sorted_by(key):
    count = key.shape[0]
    place = jnp.arange(count, dtype=jnp.int32)
    ahead = (key[None, :] < key[:, None]) | (
        (key[None, :] == key[:, None]) & (place[None, :] < place[:, None])
    )
    rank = jnp.sum(ahead.astype(jnp.int32), axis=1)
    chosen = rank[None, :] == place[:, None]

    def arrange(values):
        return jnp.sum(jnp.where(chosen, values[None, :], 0), axis=1).astype(jnp.int32)

    return arrange


def on_device(
    store_rows,
    block_lengths,
    queries,
    cand_owner,
    cand_block,
    cand_query,
    norm_gain,
    w_query,
    w_key,
    w_value,
    w_score,
):
    n_corpus = lax.axis_size("corpus")
    n_rerank = lax.axis_size("rerank")
    corpus_index = lax.axis_index("corpus")
    member = lax.axis_index("rerank")
    pair_total = cand_block.shape[0]
    pair_group = pair_total // n_corpus
    own_blocks, tokens, width = store_rows.shape
    n_query, q_tokens, _ = queries.shape
    q_dev = n_query // n_rerank
    half_blocks = own_blocks // 2

    owners = cand_owner[:, 0]
    pair_order = jnp.arange(pair_total, dtype=jnp.int32)
    group_of = pair_order // pair_group
    earlier = (
        (owners[:, None] == owners[None, :])
        & (group_of[:, None] == group_of[None, :])
        & (pair_order[None, :] < pair_order[:, None])
    )
    owner_rank = jnp.sum(earlier.astype(jnp.int32), axis=1)
    slot_ids = jnp.arange(n_corpus * CAP, dtype=jnp.int32)
    wanted = (
        (group_of[None, :] == (slot_ids // CAP)[:, None])
        & (owners[None, :] == corpus_index)
        & (owner_rank[None, :] == (slot_ids % CAP)[:, None])
    )
    present = jnp.any(wanted, axis=1)

    def of_slot(values):
        return jnp.sum(jnp.where(wanted, values[None, :], 0), axis=1)

    slot_block, slot_query, slot_pair = of_slot(cand_block), of_slot(cand_query), of_slot(pair_order)
    own_lengths = lax.dynamic_slice_in_dim(block_lengths, corpus_index * own_blocks, own_blocks, 0)
    block_ids = jnp.arange(own_blocks, dtype=jnp.int32)
    slot_length = jnp.sum(
        jnp.where(slot_block[:, None] == block_ids[None, :], own_lengths[None, :], 0), axis=1
    )
    want = jnp.any(
        present[:, None] & (slot_block[:, None] == block_ids[None, :]), axis=0
    ).astype(jnp.int32)
    slot_or_none = jnp.where(present, slot_block, -1)
    mine = present & (slot_query // q_dev == member)
    by_mine = sorted_by(jnp.where(mine, slot_block, own_blocks))
    mine_count = jnp.sum(mine.astype(jnp.int32)).reshape(1)
    mine_block, mine_length = by_mine(slot_block), by_mine(slot_length)
    mine_which, mine_pair = by_mine(slot_query % q_dev), by_mine(slot_pair)

    all_cos, all_sin = rope_tables(jnp.arange(BLK + QLEN, dtype=jnp.int32))
    base = member * tokens
    own_cos, own_sin = rope_tables(base + jnp.arange(tokens, dtype=jnp.int32))
    x, y = member // SIDE, member % SIDE
    hops = jnp.array(HOPS, jnp.int32)
    xs, ys = (x + hops) % SIDE, (y + hops) % SIDE

    core, z = corpus_index % 2, corpus_index // 2
    strip = QW // (n_corpus - 1)
    mine_first = jnp.minimum(corpus_index, n_corpus - 2) * strip
    my_strip = lax.dynamic_slice_in_dim(w_query, mine_first, strip, 1)
    along_y = [my_strip] + [shift(my_strip, "y", -hop) for hop in HOPS[1:]]
    bundle = jnp.stack(along_y)
    spread = jnp.stack([bundle] + [shift(bundle, "x", -hop) for hop in HOPS[1:]])
    at = jnp.arange(SIDE, dtype=jnp.int32)
    to_hop = jnp.array([0, 2, 3, 1], jnp.int32)
    x_at, y_at = jnp.take(to_hop, (at - x) % SIDE), jnp.take(to_hop, (at - y) % SIDE)
    from_place = (x_at[:, None] * SIDE + y_at[None, :]).reshape(SIDE * SIDE)
    my_strip = jnp.take(
        spread.reshape(SIDE * SIDE, *w_query.shape[:1], strip), from_place, axis=0
    ).reshape(width, strip)

    def along_z(value, step):
        perm = [(i, ((i // 2 + step) % SIDE) * 2 + i % 2) for i in range(n_corpus)]
        return lax.ppermute(value, "corpus", perm)

    def other_core(value):
        return lax.ppermute(value, "corpus", [(i, i + 1 - 2 * (i % 2)) for i in range(n_corpus)])

    z_low, z_high = along_z(my_strip, 1), along_z(my_strip, -1)

    w_kv = lax.all_gather(
        jnp.concatenate([w_key, w_value], axis=1), "rerank", axis=0, tiled=True
    )
    gain = norm_gain.astype(jnp.float32).reshape(1, width)
    row_count = own_blocks * tokens
    normed = norm(store_rows.reshape(row_count, width), gain)
    kv = key_value(normed, w_kv, own_cos, own_sin)
    passage_kv = kv.reshape(own_blocks, tokens, 2 * KW)
    first, second = plane_gather(passage_kv[:half_blocks], passage_kv[half_blocks:])

    z_low, z_high, _ = tie(z_low, z_high, first[1])
    half_width = width // 2
    z_far = jnp.concatenate(
        [along_z(z_low[:half_width], 1), along_z(z_high[half_width:], -1)], axis=0
    )
    near_strips = (my_strip, z_low, z_high, z_far)
    strips = near_strips + tuple(other_core(value) for value in near_strips)
    z_of = (z + hops) % SIDE
    column = jnp.concatenate([2 * z_of + core, 2 * z_of + 1 - core]).astype(jnp.int32)

    sent, _ = tie(queries, first[1])
    asked = lax.all_to_all(sent, "rerank", 0, 1, tiled=True).reshape(q_dev * QLEN, width)
    asked_token = jnp.arange(asked.shape[0], dtype=jnp.int32) % QLEN
    asked_cos, asked_sin = rope_tables(asked_token)
    asked_normed, question_kv = asked_key_value(asked, gain, w_kv, asked_cos, asked_sin)
    asked_last = jnp.pad(asked_normed[QLEN - 1 :: QLEN], ((0, 16 - q_dev), (0, 0)))
    query_rot, query_last = project_query(column, strips, normed, asked_last, own_cos, own_sin)

    inside = jnp.arange(tokens, dtype=jnp.int32)

    def positions_of(ranks):
        return (ranks[..., None] * tokens + inside).reshape(1, BLK)

    xb = (x - jnp.arange(SIDE, dtype=jnp.int32)) % SIDE
    kpos = positions_of(xb[:, None] * SIDE + ys[None, :])
    part_pos = jnp.concatenate(
        [
            positions_of(xs[:, None] * SIDE + ys[None, :]),
            positions_of(xs[None, :] * SIDE + ys[:, None]),
        ]
    )

    last = query_last[:q_dev, :QW].reshape(q_dev, KVHEADS, PER, HDIM)
    last = jnp.pad(last, ((0, 0), (0, 0), (0, 8 - PER), (0, 0)))
    head_w = jnp.pad(
        w_score.astype(jnp.float32).reshape(KVHEADS, PER, HDIM), ((0, 0), (0, 8 - PER), (0, 0))
    )
    scored = score(
        mine_count,
        mine_block,
        mine_length,
        mine_which,
        last,
        first,
        second,
        question_kv,
        part_pos,
        all_cos,
        all_sin,
        head_w,
    )[: n_corpus * CAP, 0]
    valid = slot_ids < mine_count[0]
    placed = jnp.sum(
        jnp.where(
            valid[:, None] & (mine_pair[:, None] == pair_order[None, :]), scored[:, None], 0.0
        ),
        axis=0,
    )
    where = jnp.stack([base, x]).astype(jnp.int32)
    query_rot = query_rot.reshape(own_blocks, tokens, query_rot.shape[1])
    gathered = lax.all_to_all(placed.reshape(n_corpus, pair_group), "corpus", 0, 0, tiled=True)
    begun = attend(
        want, slot_or_none, own_lengths, where, query_rot, first, kpos, False, 0, None
    )
    gathered, begun = tie(gathered, begun)
    shared = jnp.sum(gathered, axis=0).reshape(n_rerank, pair_group // n_rerank)
    pair_scores = jnp.sum(lax.all_to_all(shared, "rerank", 0, 0, tiled=True), axis=0)
    passage_context = attend(
        want, slot_or_none, own_lengths, where, query_rot, second, kpos, True, half_blocks, begun
    )
    return (passage_context, pair_scores)


def solution(mesh):
    placed = (
        P("corpus", "rerank", None),
        P(),
        P(None, "rerank", None),
        P(),
        P(),
        P(),
        P(),
        P("rerank", None),
        P("rerank", None),
        P("rerank", None),
        P(),
    )
    return jax.shard_map(
        on_device,
        mesh=mesh,
        in_specs=placed,
        out_specs=(P("corpus", "rerank", None), P(("corpus", "rerank"))),
        check_vma=False,
    )
```

```python
import jax
import jax.numpy as jnp
from jax import lax
from jax.experimental import pallas as pl
from jax.experimental.pallas import tpu as pltpu
from jax.sharding import PartitionSpec as P

HDIM = 128
QHEADS = 14
KVHEADS = 2
PER = QHEADS // KVHEADS
QW = QHEADS * HDIM
KW = KVHEADS * HDIM
BLK = 512
QLEN = 64
CAP = 5
SIDE = 4
SIZES = (24, 28)
ROPE_BASE = 1000000.0
EPSILON = 1e-06
SCALE2 = HDIM ** (-0.5) * 1.4426950408889634
VMEM = 56 * 1024 * 1024


def rope_tables(positions):
    half = HDIM // 2
    inverse = jnp.power(ROPE_BASE, -2.0 * jnp.arange(half, dtype=jnp.float32) / HDIM)
    angles = positions.astype(jnp.float32)[:, None] * inverse
    cosine, sine = jnp.cos(angles), jnp.sin(angles)
    return (
        jnp.concatenate([cosine, cosine], axis=1),
        jnp.concatenate([-sine, sine], axis=1),
    )


def spin(part, cosine, sine):
    return part * cosine + pltpu.roll(part, HDIM // 2, part.ndim - 1) * sine


def shift(value, dim, step):
    def moved(index):
        x, y = index // SIDE, index % SIDE
        if dim == "x":
            x = (x + step) % SIDE
        else:
            y = (y + step) % SIDE
        return x * SIDE + y

    return lax.ppermute(value, "rerank", [(i, moved(i)) for i in range(SIDE * SIDE)])


def tie(*values):
    return lax.optimization_barrier(values)


def plane_gather(value_a, value_b):
    a_low, a_high, a_far = (shift(value_a, "y", step) for step in (1, -1, 2))
    b_low, b_high, b_far = (shift(value_b, "x", step) for step in (1, -1, 2))
    a_low, a_high, a_far, b_low, b_high, b_far = tie(a_low, a_high, a_far, b_low, b_high, b_far)
    a0, a1 = jnp.stack([value_a, a_low]), jnp.stack([a_high, a_far])
    b0, b1 = jnp.stack([value_b, b_low]), jnp.stack([b_high, b_far])
    a0_low, b0_low = shift(a0, "x", 1), shift(b0, "y", 1)
    a1_high, b1_high = shift(a1, "x", -1), shift(b1, "y", -1)
    a1_low, b1_low = shift(a1, "x", 1), shift(b1, "y", 1)
    a0_high, b0_high = shift(a0, "x", -1), shift(b0, "y", -1)
    a0_low, b0_low, a1_high, b1_high = tie(a0_low, b0_low, a1_high, b1_high)
    a0_far, b0_far = shift(a0_low, "x", 1), shift(b0_low, "y", 1)
    a1_far, b1_far = shift(a1_high, "x", -1), shift(b1_high, "y", -1)
    return (
        (a0, a1, a0_low, a1_low, a0_high, a1_high, a0_far, a1_far),
        (b0, b1, b0_low, b1_low, b0_high, b1_high, b0_far, b1_far),
    )


PARTS = 8
HOPS = (0, -1, 1, 2)
BACK = (0, 1, 3, 2)


def part_of(parts, swapped, dx, dy):
    outer, inner = (dy, dx) if swapped else (dx, dy)
    return parts[2 * outer + inner // 2], inner % 2


def normed_of(rows, gain):
    wide = rows.astype(jnp.float32)
    inverse = lax.rsqrt(jnp.mean(wide * wide, axis=-1, keepdims=True) + EPSILON)
    return (wide * inverse * gain).astype(jnp.bfloat16)


def norm_kernel(order_ref, x_ref, gain_ref, out_ref):
    out_ref[...] = normed_of(x_ref[0], gain_ref[...])


def norm(order, store, gain):
    blocks, tokens, width = store.shape
    return pl.pallas_call(
        norm_kernel,
        grid_spec=pltpu.PrefetchScalarGridSpec(
            num_scalar_prefetch=1,
            grid=(blocks,),
            in_specs=[
                pl.BlockSpec((1, tokens, width), lambda i, order: (order[i], 0, 0)),
                pl.BlockSpec((1, width), lambda i, order: (0, 0)),
            ],
            out_specs=pl.BlockSpec((tokens, width), lambda i, order: (i, 0)),
        ),
        out_shape=jax.ShapeDtypeStruct((blocks * tokens, width), jnp.bfloat16),
        compiler_params=pltpu.CompilerParams(vmem_limit_bytes=VMEM),
        name="norm",
    )(order, store, gain)


def key_value_kernel(normed_ref, w_ref, cos_ref, sin_ref, kv_ref):
    rows = normed_ref.shape[0]
    tokens = cos_ref.shape[0]
    raw = jnp.dot(normed_ref[...], w_ref[...], preferred_element_type=jnp.float32)
    for head in range(KVHEADS):
        cols = slice(head * HDIM, (head + 1) * HDIM)
        part = raw[:, cols].reshape(rows // tokens, tokens, HDIM)
        turned = spin(part, cos_ref[...][None], sin_ref[...][None])
        kv_ref[:, cols] = turned.reshape(rows, HDIM).astype(jnp.bfloat16)
    kv_ref[:, KW:] = raw[:, KW:].astype(jnp.bfloat16)


def key_value(normed, w_kv, cosine, sine, rows):
    tile = 128
    width = normed.shape[1]
    table = pl.BlockSpec(cosine.shape, lambda i: (0, 0))
    return pl.pallas_call(
        key_value_kernel,
        grid=(rows // tile,),
        in_specs=[
            pl.BlockSpec((tile, width), lambda i: (i, 0)),
            pl.BlockSpec((width, 2 * KW), lambda i: (0, 0)),
            table,
            table,
        ],
        out_specs=pl.BlockSpec((tile, 2 * KW), lambda i: (i, 0)),
        out_shape=jax.ShapeDtypeStruct((rows, 2 * KW), jnp.bfloat16),
        compiler_params=pltpu.CompilerParams(vmem_limit_bytes=VMEM),
        name="key_value",
    )(normed, w_kv, cosine, sine)


def asked_kernel(x_ref, gain_ref, w_ref, cos_ref, sin_ref, normed_ref, kv_ref):
    normed_ref[...] = normed_of(x_ref[...], gain_ref[...])
    raw = jnp.dot(normed_ref[...], w_ref[...], preferred_element_type=jnp.float32)
    for head in range(KVHEADS):
        cols = slice(head * HDIM, (head + 1) * HDIM)
        kv_ref[:, cols] = spin(raw[:, cols], cos_ref[...], sin_ref[...]).astype(jnp.bfloat16)
    kv_ref[:, KW:] = raw[:, KW:].astype(jnp.bfloat16)


def asked_key_value(rows, gain, w_kv, cosine, sine):
    return pl.pallas_call(
        asked_kernel,
        out_shape=[
            jax.ShapeDtypeStruct(rows.shape, jnp.bfloat16),
            jax.ShapeDtypeStruct((rows.shape[0], 2 * KW), jnp.bfloat16),
        ],
        compiler_params=pltpu.CompilerParams(vmem_limit_bytes=VMEM),
        name="asked_key_value",
    )(rows, gain, w_kv, cosine, sine)


def query_kernel(normed_ref, asked_ref, w_ref, cos_ref, sin_ref, out_ref, last_ref, x_ref, sems):
    rows, chunk = out_ref.shape
    tokens = cos_ref.shape[0]
    extra = asked_ref.shape[0]

    @pl.when(pl.program_id(0) == 0)
    def _():
        copies = (
            pltpu.make_async_copy(
                normed_ref.at[pl.ds(0, rows)], x_ref.at[pl.ds(0, rows)], sems.at[0]
            ),
            pltpu.make_async_copy(asked_ref, x_ref.at[pl.ds(rows, extra)], sems.at[1]),
        )
        for copy in copies:
            copy.start()
        for copy in copies:
            copy.wait()

    raw = jnp.dot(x_ref[...], w_ref[0], preferred_element_type=jnp.float32)
    for head in range(chunk // HDIM):
        cols = slice(head * HDIM, (head + 1) * HDIM)
        part = raw[:rows, cols].reshape(rows // tokens, tokens, HDIM)
        turned = spin(part, cos_ref[...][None], sin_ref[...][None])
        out_ref[:, cols] = turned.reshape(rows, HDIM).astype(jnp.bfloat16)
    last_ref[...] = raw[rows:]


def project_query(strips, normed, asked, cosine, sine, rows):
    width = normed.shape[1]
    chunk = strips.shape[2]
    extra = asked.shape[0]
    table = pl.BlockSpec(cosine.shape, lambda i: (0, 0))
    anywhere = pl.BlockSpec(memory_space=pl.ANY)
    return pl.pallas_call(
        query_kernel,
        grid=(QW // chunk,),
        in_specs=[
            anywhere,
            anywhere,
            pl.BlockSpec((1, width, chunk), lambda i: (i, 0, 0)),
            table,
            table,
        ],
        out_specs=[
            pl.BlockSpec((rows, chunk), lambda i: (0, i)),
            pl.BlockSpec((extra, chunk), lambda i: (0, i)),
        ],
        out_shape=[
            jax.ShapeDtypeStruct((rows, QW), jnp.bfloat16),
            jax.ShapeDtypeStruct((extra, QW), jnp.float32),
        ],
        scratch_shapes=[
            pltpu.VMEM((rows + extra, width), jnp.bfloat16),
            pltpu.SemaphoreType.DMA((2,)),
        ],
        compiler_params=pltpu.CompilerParams(vmem_limit_bytes=VMEM),
        name="project_query",
    )(normed, asked, strips, cosine, sine)


def attend_kernel(
    slot_ref, length_ref, where_ref, q_ref, *rest, swapped, start, absent
):
    parts, kpos_ref = rest[:PARTS], rest[PARTS]
    out_ref, held, zeros, listed, sems = rest[-5:]
    blocks, tokens, _ = q_ref.shape
    slots = slot_ref.shape[0]
    base = where_ref[0]
    row, wanted = where_ref[1], where_ref[2]
    rows = PER * tokens
    zeros[...] = jnp.zeros_like(zeros)

    def attend_block(block, groups):
        length = length_ref[start + block]
        kpos = kpos_ref[0:1, : groups * SIDE * tokens]
        qpos = base + lax.rem(lax.broadcasted_iota(jnp.int32, (rows, 1), 0), tokens)
        allowed = (kpos <= qpos) & (kpos < length)
        kept = (base + lax.broadcasted_iota(jnp.int32, (tokens, 1), 0)) < length

        def side_by_side(first):
            picked = []
            for dx in BACK[:groups]:
                for dy in range(SIDE):
                    ref, index = part_of(parts, swapped, dx, dy)
                    picked.append(ref[index, block, :, first : first + HDIM])
            return jnp.concatenate(picked, axis=0)

        for g in range(KVHEADS):
            heads = range(g * PER, (g + 1) * PER)
            queries = jnp.concatenate(
                [q_ref[block, :, h * HDIM : (h + 1) * HDIM] for h in heads], axis=0
            )
            logits = lax.dot_general(
                queries,
                side_by_side(g * HDIM),
                (((1,), (1,)), ((), ())),
                preferred_element_type=jnp.float32,
            )
            logits = jnp.where(allowed, logits * SCALE2, -1e30)
            weights = jnp.exp2(logits - jnp.max(logits, axis=-1, keepdims=True))
            total = jnp.sum(weights, axis=-1, keepdims=True)
            mixed = jnp.dot(
                weights.astype(jnp.bfloat16),
                side_by_side(KW + g * HDIM),
                preferred_element_type=jnp.float32,
            ) / total
            for h in heads:
                at = (h - g * PER) * tokens
                held[block, :, h * HDIM : (h + 1) * HDIM] = jnp.where(
                    kept, mixed[at : at + tokens], 0.0
                ).astype(jnp.bfloat16)

    def enlist(block, count):
        listed[count] = block
        alive = (start + block < wanted) & (base < length_ref[start + block])
        return count + alive.astype(jnp.int32)

    count = lax.fori_loop(0, blocks, enlist, jnp.int32(0))

    def each_block(groups):
        def body(pair, carry):
            attend_block(listed[2 * pair], groups)
            attend_block(listed[jnp.minimum(2 * pair + 1, count - 1)], groups)
            return carry

        lax.fori_loop(0, lax.div(count + 1, 2), body, 0)

    for x in range(SIDE):

        @pl.when(row == x)
        def _(x=x):
            each_block(x + 1)

    def copies(slot, act):
        block = slot_ref[slot]
        here = (block >= start) & (block < start + blocks)
        local = jnp.clip(block - start, 0, blocks - 1)
        filled = here & (base < length_ref[start + local])
        empty = here & jnp.logical_not(base < length_ref[start + local])
        if absent:
            empty = empty | (block < 0)

        @pl.when(filled)
        def _():
            act(pltpu.make_async_copy(held.at[local], out_ref.at[slot], sems.at[slot]))

        @pl.when(empty)
        def _():
            act(pltpu.make_async_copy(zeros, out_ref.at[slot], sems.at[slot]))

    def send(slot, carry):
        copies(slot, lambda copy: copy.start())
        return carry

    def finish(slot, carry):
        copies(slot, lambda copy: copy.wait())
        return carry

    lax.fori_loop(0, slots, send, 0)
    lax.fori_loop(0, slots, finish, 0)


def attend(slot_block, lengths, where, queries, parts, kpos, swapped, start, earlier):
    blocks, tokens = parts[0].shape[1:3]
    width = QW
    slots = slot_block.shape[0]
    anywhere = pl.BlockSpec(memory_space=pl.ANY)

    def whole(array):
        return pl.BlockSpec(array.shape, lambda i, *_: (0,) * array.ndim)

    given = () if earlier is None else (earlier,)
    return pl.pallas_call(
        lambda *refs: attend_kernel(
            *refs, swapped=swapped, start=start, absent=earlier is None
        ),
        grid_spec=pltpu.PrefetchScalarGridSpec(
            num_scalar_prefetch=3,
            grid=(1,),
            in_specs=[
                pl.BlockSpec((blocks, tokens, width), lambda i, *_: (start // blocks, 0, 0)),
                *[whole(part) for part in parts],
                whole(kpos),
                *[anywhere for _ in given],
            ],
            out_specs=anywhere,
            scratch_shapes=[
                pltpu.VMEM((blocks, tokens, width), jnp.bfloat16),
                pltpu.VMEM((tokens, width), jnp.bfloat16),
                pltpu.SMEM((blocks + 1,), jnp.int32),
                pltpu.SemaphoreType.DMA((slots,)),
            ],
        ),
        out_shape=jax.ShapeDtypeStruct((slots, tokens, width), jnp.bfloat16),
        input_output_aliases={5 + PARTS: 0} if given else {},
        compiler_params=pltpu.CompilerParams(vmem_limit_bytes=VMEM),
        name="attend_second" if given else "attend_first",
    )(slot_block, lengths, where, queries, *parts, kpos, *given)


def score_kernel(count_ref, block_ref, length_ref, which_ref, size_ref, last_ref, *rest):
    parts_a, parts_b, rest = rest[:PARTS], rest[PARTS : 2 * PARTS], rest[2 * PARTS :]
    qkv_ref, kpos_ref, cos_ref, sin_ref, w_ref, out_ref, kv_ref, sems = rest
    half, q_span = size_ref[0], size_ref[1]
    count = count_ref[0]

    def fetch(step, act):
        slot = lax.rem(step, 2)
        block = block_ref[step]
        for which, parts in enumerate((parts_a, parts_b)):

            @pl.when((block >= half) if which else (block < half))
            def _(which=which, parts=parts):
                local = jnp.clip(block - which * half, 0, parts[0].shape[1] - 1)
                for number, part in enumerate(parts):
                    held = kv_ref.at[slot, pl.ds(2 * number, 2)]
                    act(pltpu.make_async_copy(part.at[:, local], held, sems.at[slot, number]))

    @pl.when(count > 0)
    def _():
        fetch(0, lambda copy: copy.start())

    def body(step, carry):
        @pl.when(step + 1 < count)
        def _():
            fetch(step + 1, lambda copy: copy.start())

        fetch(step, lambda copy: copy.wait())
        slot = lax.rem(step, 2)
        length = length_ref[step]
        which = which_ref[step]
        second = (block_ref[step] >= half).astype(jnp.int32)
        kpos = kpos_ref[pl.ds(second, 1), :]
        live = kpos < length
        span = qkv_ref.shape[0]
        lane = lax.broadcasted_iota(jnp.int32, (1, span), 1)
        own = lax.div(lane, q_span) == which
        at_far = pl.ds(length + QLEN - 1, 1)
        far_cos, far_sin = cos_ref[at_far, :], sin_ref[at_far, :]
        near_cos, near_sin = cos_ref[QLEN - 1 : QLEN, :], sin_ref[QLEN - 1 : QLEN, :]
        total_score = jnp.zeros((1, HDIM), jnp.float32)
        over = (((1,), (1,)), ((), ()))
        for g in range(KVHEADS):
            raw = last_ref[which, g]
            far = spin(raw, far_cos, far_sin).astype(jnp.bfloat16)
            near = spin(raw, near_cos, near_sin).astype(jnp.bfloat16)
            keys = kv_ref[slot, :, :, g * HDIM : (g + 1) * HDIM].reshape(BLK, HDIM)
            values = kv_ref[slot, :, :, KW + g * HDIM : KW + (g + 1) * HDIM].reshape(BLK, HDIM)
            passage = lax.dot_general(far, keys, over, preferred_element_type=jnp.float32)
            question = lax.dot_general(
                near,
                qkv_ref[:, g * HDIM : (g + 1) * HDIM],
                over,
                preferred_element_type=jnp.float32,
            )
            passage = jnp.where(live, passage * SCALE2, -1e30)
            question = jnp.where(own, question * SCALE2, -1e30)
            peak = jnp.maximum(
                jnp.max(passage, axis=-1, keepdims=True), jnp.max(question, axis=-1, keepdims=True)
            )
            passage = jnp.exp2(passage - peak)
            question = jnp.exp2(question - peak)
            total = jnp.sum(passage, axis=-1, keepdims=True) + jnp.sum(
                question, axis=-1, keepdims=True
            )
            mixed = jnp.dot(
                passage.astype(jnp.bfloat16), values, preferred_element_type=jnp.float32
            ) + jnp.dot(
                question.astype(jnp.bfloat16),
                qkv_ref[:, KW + g * HDIM : KW + (g + 1) * HDIM],
                preferred_element_type=jnp.float32,
            )
            context = (mixed / total).astype(jnp.bfloat16).astype(jnp.float32)
            total_score += jnp.sum(context * w_ref[g], axis=0, keepdims=True)
        result = jnp.sum(total_score, axis=-1, keepdims=True)
        out_ref[pl.ds(step, 1), :] = jnp.broadcast_to(result, (1, HDIM))
        return carry

    lax.fori_loop(0, count, body, 0)


def score(
    count, blocks, lengths, which, last, first, second, question_kv, kpos, cosine, sine, w
):
    slots = blocks.shape[0]
    anywhere = pl.BlockSpec(memory_space=pl.ANY)
    tokens = first[0].shape[2]

    def whole(array):
        return pl.BlockSpec(array.shape, lambda i, *_: (0,) * array.ndim)

    return pl.pallas_call(
        score_kernel,
        grid_spec=pltpu.PrefetchScalarGridSpec(
            num_scalar_prefetch=5,
            grid=(1,),
            in_specs=[
                whole(last),
                *[anywhere] * (2 * PARTS),
                whole(question_kv),
                whole(kpos),
                whole(cosine),
                whole(sine),
                whole(w),
            ],
            out_specs=pl.BlockSpec((slots, HDIM), lambda i, *_: (0, 0)),
            scratch_shapes=[
                pltpu.VMEM((2, SIDE * SIDE, tokens, 2 * KW), jnp.bfloat16),
                pltpu.SemaphoreType.DMA((2, PARTS)),
            ],
        ),
        out_shape=jax.ShapeDtypeStruct((slots, HDIM), jnp.float32),
        compiler_params=pltpu.CompilerParams(vmem_limit_bytes=VMEM),
        name="score",
    )(
        count,
        blocks,
        lengths,
        which,
        jnp.array([first[0].shape[1], QLEN], jnp.int32),
        last,
        *first,
        *second,
        question_kv,
        kpos,
        cosine,
        sine,
        w,
    )


def sorted_by(key):
    count = key.shape[0]
    place = jnp.arange(count, dtype=jnp.int32)
    ahead = (key[None, :] < key[:, None]) | (
        (key[None, :] == key[:, None]) & (place[None, :] < place[:, None])
    )
    rank = jnp.sum(ahead.astype(jnp.int32), axis=1)
    chosen = rank[None, :] == place[:, None]

    def arrange(values):
        return jnp.sum(jnp.where(chosen, values[None, :], 0), axis=1).astype(jnp.int32)

    return arrange, rank


def on_device(
    store_rows,
    block_lengths,
    queries,
    cand_owner,
    cand_block,
    cand_query,
    norm_gain,
    w_query,
    w_key,
    w_value,
    w_score,
):
    n_corpus = lax.axis_size("corpus")
    n_rerank = lax.axis_size("rerank")
    corpus_index = lax.axis_index("corpus")
    member = lax.axis_index("rerank")
    pair_total = cand_block.shape[0]
    pair_group = pair_total // n_corpus
    own_blocks, tokens, width = store_rows.shape
    n_query, q_tokens, _ = queries.shape
    q_dev = n_query // n_rerank

    owners = cand_owner[:, 0]
    pair_order = jnp.arange(pair_total, dtype=jnp.int32)
    group_of = pair_order // pair_group
    earlier = (
        (owners[:, None] == owners[None, :])
        & (group_of[:, None] == group_of[None, :])
        & (pair_order[None, :] < pair_order[:, None])
    )
    owner_rank = jnp.sum(earlier.astype(jnp.int32), axis=1)
    slot_ids = jnp.arange(n_corpus * CAP, dtype=jnp.int32)
    wanted = (
        (group_of[None, :] == (slot_ids // CAP)[:, None])
        & (owners[None, :] == corpus_index)
        & (owner_rank[None, :] == (slot_ids % CAP)[:, None])
    )
    present = jnp.any(wanted, axis=1)

    def of_slot(values):
        return jnp.sum(jnp.where(wanted, values[None, :], 0), axis=1)

    slot_query, slot_pair, stored_block = of_slot(cand_query), of_slot(pair_order), of_slot(cand_block)
    block_ids = jnp.arange(own_blocks, dtype=jnp.int32)
    owner_ids = jnp.arange(n_corpus, dtype=jnp.int32)
    named = jnp.any(
        (owners[None, None, :] == owner_ids[:, None, None])
        & (cand_block[None, None, :] == block_ids[None, :, None]),
        axis=2,
    )
    most = jnp.max(jnp.sum(named.astype(jnp.int32), axis=1))
    want = jnp.any(named & (owner_ids[:, None] == corpus_index), axis=0)
    want_count = jnp.sum(want.astype(jnp.int32))
    by_want, want_rank = sorted_by(jnp.where(want, 0, 1))
    block_order = by_want(block_ids)
    own_lengths = by_want(
        lax.dynamic_slice_in_dim(block_lengths, corpus_index * own_blocks, own_blocks, 0)
    )
    is_block = stored_block[:, None] == block_ids[None, :]
    slot_block = jnp.sum(jnp.where(is_block, want_rank[None, :], 0), axis=1)
    slot_length = jnp.sum(
        jnp.where(slot_block[:, None] == block_ids[None, :], own_lengths[None, :], 0), axis=1
    )
    slot_or_none = jnp.where(present, slot_block, -1)
    mine = present & (slot_query // q_dev == member)
    by_mine, _ = sorted_by(jnp.where(mine, slot_block, own_blocks))
    mine_count = jnp.sum(mine.astype(jnp.int32)).reshape(1)
    mine_block, mine_length = by_mine(slot_block), by_mine(slot_length)
    mine_which, mine_pair = by_mine(slot_query % q_dev), by_mine(slot_pair)

    all_cos, all_sin = rope_tables(jnp.arange(BLK + QLEN, dtype=jnp.int32))
    base = member * tokens
    own_cos, own_sin = rope_tables(base + jnp.arange(tokens, dtype=jnp.int32))
    x, y = member // SIDE, member % SIDE
    hops = jnp.array(HOPS, jnp.int32)
    xs, ys = (x + hops) % SIDE, (y + hops) % SIDE

    w_kv = lax.all_gather(
        jnp.concatenate([w_key, w_value], axis=1), "rerank", axis=0, tiled=True
    )
    gain = norm_gain.astype(jnp.float32).reshape(1, width)
    normed = norm(block_order, store_rows, gain)

    asked = lax.all_to_all(queries, "rerank", 0, 1, tiled=True).reshape(q_dev * QLEN, width)
    asked_token = jnp.arange(asked.shape[0], dtype=jnp.int32) % QLEN
    asked_cos, asked_sin = rope_tables(asked_token)

    strip = QW // (n_corpus - 1)
    my_strip = lax.dynamic_slice_in_dim(
        w_query, jnp.minimum(corpus_index, n_corpus - 2) * strip, strip, 1
    )

    inside = jnp.arange(tokens, dtype=jnp.int32)

    def positions_of(ranks):
        return (ranks[..., None] * tokens + inside).reshape(1, BLK)

    xb = (x - jnp.arange(SIDE, dtype=jnp.int32)) % SIDE
    kpos = positions_of(xb[:, None] * SIDE + ys[None, :])
    part_pos = jnp.concatenate(
        [
            positions_of(xs[:, None] * SIDE + ys[None, :]),
            positions_of(xs[None, :] * SIDE + ys[:, None]),
        ]
    )

    head_w = jnp.pad(
        w_score.astype(jnp.float32).reshape(KVHEADS, PER, HDIM), ((0, 0), (0, 8 - PER), (0, 0))
    )
    where = jnp.stack([base, x, want_count]).astype(jnp.int32)
    def attended(blocks):
        half = blocks // 2
        strip_in, w_kv_in = tie(my_strip, w_kv)
        strips = lax.all_gather(strip_in, ("corpus", "rerank"), axis=0, tiled=False)
        strips = strips.reshape(n_corpus, width, strip)
        kv = key_value(normed, w_kv_in, own_cos, own_sin, blocks * tokens)
        passage_kv = kv.reshape(blocks, tokens, 2 * KW)
        first, second = plane_gather(passage_kv[:half], passage_kv[half:])
        asked_normed, question_kv = asked_key_value(asked, gain, w_kv_in, asked_cos, asked_sin)
        asked_last = jnp.pad(asked_normed[QLEN - 1 :: QLEN], ((0, 16 - q_dev), (0, 0)))
        query_rot, query_last = project_query(
            strips, normed, asked_last, own_cos, own_sin, blocks * tokens
        )
        last = query_last[:q_dev].reshape(q_dev, KVHEADS, PER, HDIM)
        last = jnp.pad(last, ((0, 0), (0, 0), (0, 8 - PER), (0, 0)))
        scored = score(
            mine_count,
            mine_block,
            mine_length,
            mine_which,
            last,
            first,
            second,
            question_kv,
            part_pos,
            all_cos,
            all_sin,
            head_w,
        )[: n_corpus * CAP, 0]
        valid = slot_ids < mine_count[0]
        placed = jnp.sum(
            jnp.where(
                valid[:, None] & (mine_pair[:, None] == pair_order[None, :]), scored[:, None], 0.0
            ),
            axis=0,
        )
        query_rot = query_rot.reshape(blocks, tokens, QW)
        gathered = lax.all_to_all(placed.reshape(n_corpus, pair_group), "corpus", 0, 0, tiled=True)
        begun = attend(
            slot_or_none, own_lengths, where, query_rot, first, kpos, False, 0, None
        )
        gathered, begun = tie(gathered, begun)
        shared = jnp.sum(gathered, axis=0).reshape(n_rerank, pair_group // n_rerank)
        pair_scores = jnp.sum(lax.all_to_all(shared, "rerank", 0, 0, tiled=True), axis=0)
        passage_context = attend(
            slot_or_none, own_lengths, where, query_rot, second, kpos, True, half, begun
        )
        return passage_context, pair_scores

    choice = sum((most > size).astype(jnp.int32) for size in SIZES)
    return lax.switch(choice, [lambda size=size: attended(size) for size in (*SIZES, own_blocks)])


def solution(mesh):
    placed = (
        P("corpus", "rerank", None),
        P(),
        P(None, "rerank", None),
        P(),
        P(),
        P(),
        P(),
        P("rerank", None),
        P("rerank", None),
        P("rerank", None),
        P(),
    )
    return jax.shard_map(
        on_device,
        mesh=mesh,
        in_specs=placed,
        out_specs=(P("corpus", "rerank", None), P(("corpus", "rerank"))),
        check_vma=False,
    )
```

```python
import jax
import jax.numpy as jnp
from jax import lax
from jax.experimental import pallas as pl
from jax.experimental.pallas import tpu as pltpu
from jax.sharding import PartitionSpec as P

HDIM = 128
QHEADS = 14
KVHEADS = 2
PER = QHEADS // KVHEADS
QW = QHEADS * HDIM
KW = KVHEADS * HDIM
BLK = 512
QLEN = 64
CAP = 5
SIDE = 4
SIZES = (24, 28)
ROPE_BASE = 1000000.0
EPSILON = 1e-06
SCALE2 = HDIM ** (-0.5) * 1.4426950408889634
VMEM = 56 * 1024 * 1024


def rope_tables(positions):
    half = HDIM // 2
    inverse = jnp.power(ROPE_BASE, -2.0 * jnp.arange(half, dtype=jnp.float32) / HDIM)
    angles = positions.astype(jnp.float32)[:, None] * inverse
    cosine, sine = jnp.cos(angles), jnp.sin(angles)
    return (
        jnp.concatenate([cosine, cosine], axis=1),
        jnp.concatenate([-sine, sine], axis=1),
    )


def spin(part, cosine, sine):
    return part * cosine + pltpu.roll(part, HDIM // 2, part.ndim - 1) * sine


def shift(value, dim, step):
    def moved(index):
        x, y = index // SIDE, index % SIDE
        if dim == "x":
            x = (x + step) % SIDE
        else:
            y = (y + step) % SIDE
        return x * SIDE + y

    return lax.ppermute(value, "rerank", [(i, moved(i)) for i in range(SIDE * SIDE)])


def tie(*values):
    return lax.optimization_barrier(values)


def plane_gather(value_a, value_b):
    a_low, a_high, a_far = (shift(value_a, "y", step) for step in (1, -1, 2))
    b_low, b_high, b_far = (shift(value_b, "x", step) for step in (1, -1, 2))
    a_low, a_high, a_far, b_low, b_high, b_far = tie(a_low, a_high, a_far, b_low, b_high, b_far)
    a0, a1 = jnp.stack([value_a, a_low]), jnp.stack([a_high, a_far])
    b0, b1 = jnp.stack([value_b, b_low]), jnp.stack([b_high, b_far])
    a0_low, b0_low = shift(a0, "x", 1), shift(b0, "y", 1)
    a1_high, b1_high = shift(a1, "x", -1), shift(b1, "y", -1)
    a1_low, b1_low = shift(a1, "x", 1), shift(b1, "y", 1)
    a0_high, b0_high = shift(a0, "x", -1), shift(b0, "y", -1)
    a0_low, b0_low, a1_high, b1_high = tie(a0_low, b0_low, a1_high, b1_high)
    a0_far, b0_far = shift(a0_low, "x", 1), shift(b0_low, "y", 1)
    a1_far, b1_far = shift(a1_high, "x", -1), shift(b1_high, "y", -1)
    return (
        (a0, a1, a0_low, a1_low, a0_high, a1_high, a0_far, a1_far),
        (b0, b1, b0_low, b1_low, b0_high, b1_high, b0_far, b1_far),
    )


PARTS = 8
HOPS = (0, -1, 1, 2)
BACK = (0, 1, 3, 2)


def part_of(parts, swapped, dx, dy):
    outer, inner = (dy, dx) if swapped else (dx, dy)
    return parts[2 * outer + inner // 2], inner % 2


def normed_of(rows, gain):
    wide = rows.astype(jnp.float32)
    inverse = lax.rsqrt(jnp.mean(wide * wide, axis=-1, keepdims=True) + EPSILON)
    return (wide * inverse * gain).astype(jnp.bfloat16)


GROUP = 4


def norm_kernel(order_ref, *refs):
    blocks, (gain_ref, out_ref) = refs[:GROUP], refs[GROUP:]
    tokens = blocks[0].shape[1]
    for number, block in enumerate(blocks):
        out_ref[number * tokens : (number + 1) * tokens] = normed_of(block[0], gain_ref[...])


def norm(order, store, gain):
    blocks, tokens, width = store.shape
    return pl.pallas_call(
        norm_kernel,
        grid_spec=pltpu.PrefetchScalarGridSpec(
            num_scalar_prefetch=1,
            grid=(blocks // GROUP,),
            in_specs=[
                *[
                    pl.BlockSpec(
                        (1, tokens, width), lambda i, order, n=n: (order[GROUP * i + n], 0, 0)
                    )
                    for n in range(GROUP)
                ],
                pl.BlockSpec((1, width), lambda i, order: (0, 0)),
            ],
            out_specs=pl.BlockSpec((GROUP * tokens, width), lambda i, order: (i, 0)),
        ),
        out_shape=jax.ShapeDtypeStruct((blocks * tokens, width), jnp.bfloat16),
        compiler_params=pltpu.CompilerParams(vmem_limit_bytes=VMEM),
        name="norm",
    )(order, *[store] * GROUP, gain)


def key_value_kernel(normed_ref, w_ref, cos_ref, sin_ref, kv_ref):
    rows = normed_ref.shape[0]
    tokens = cos_ref.shape[0]
    raw = jnp.dot(normed_ref[...], w_ref[...], preferred_element_type=jnp.float32)
    for head in range(KVHEADS):
        cols = slice(head * HDIM, (head + 1) * HDIM)
        part = raw[:, cols].reshape(rows // tokens, tokens, HDIM)
        turned = spin(part, cos_ref[...][None], sin_ref[...][None])
        kv_ref[:, cols] = turned.reshape(rows, HDIM).astype(jnp.bfloat16)
    kv_ref[:, KW:] = raw[:, KW:].astype(jnp.bfloat16)


def key_value(normed, w_kv, cosine, sine, rows):
    tile = 128
    width = normed.shape[1]
    table = pl.BlockSpec(cosine.shape, lambda i: (0, 0))
    return pl.pallas_call(
        key_value_kernel,
        grid=(rows // tile,),
        in_specs=[
            pl.BlockSpec((tile, width), lambda i: (i, 0)),
            pl.BlockSpec((width, 2 * KW), lambda i: (0, 0)),
            table,
            table,
        ],
        out_specs=pl.BlockSpec((tile, 2 * KW), lambda i: (i, 0)),
        out_shape=jax.ShapeDtypeStruct((rows, 2 * KW), jnp.bfloat16),
        compiler_params=pltpu.CompilerParams(vmem_limit_bytes=VMEM),
        name="key_value",
    )(normed, w_kv, cosine, sine)


def asked_kernel(x_ref, gain_ref, w_ref, cos_ref, sin_ref, normed_ref, kv_ref):
    normed_ref[...] = normed_of(x_ref[...], gain_ref[...])
    raw = jnp.dot(normed_ref[...], w_ref[...], preferred_element_type=jnp.float32)
    for head in range(KVHEADS):
        cols = slice(head * HDIM, (head + 1) * HDIM)
        kv_ref[:, cols] = spin(raw[:, cols], cos_ref[...], sin_ref[...]).astype(jnp.bfloat16)
    kv_ref[:, KW:] = raw[:, KW:].astype(jnp.bfloat16)


def asked_key_value(rows, gain, w_kv, cosine, sine):
    def whole(shape):
        return pl.BlockSpec(shape, lambda i: (0, 0))

    width = rows.shape[1]
    return pl.pallas_call(
        asked_kernel,
        grid=(1,),
        in_specs=[
            whole(rows.shape),
            whole(gain.shape),
            whole((width, 2 * KW)),
            whole(cosine.shape),
            whole(sine.shape),
        ],
        out_specs=[whole(rows.shape), whole((rows.shape[0], 2 * KW))],
        out_shape=[
            jax.ShapeDtypeStruct(rows.shape, jnp.bfloat16),
            jax.ShapeDtypeStruct((rows.shape[0], 2 * KW), jnp.bfloat16),
        ],
        compiler_params=pltpu.CompilerParams(vmem_limit_bytes=VMEM),
        name="asked_key_value",
    )(rows, gain, w_kv, cosine, sine)


def query_kernel(normed_ref, asked_ref, w_ref, cos_ref, sin_ref, out_ref, last_ref, x_ref, sems):
    rows, chunk = out_ref.shape
    tokens = cos_ref.shape[0]
    extra = asked_ref.shape[0]

    @pl.when(pl.program_id(0) == 0)
    def _():
        copies = (
            pltpu.make_async_copy(
                normed_ref.at[pl.ds(0, rows)], x_ref.at[pl.ds(0, rows)], sems.at[0]
            ),
            pltpu.make_async_copy(asked_ref, x_ref.at[pl.ds(rows, extra)], sems.at[1]),
        )
        for copy in copies:
            copy.start()
        for copy in copies:
            copy.wait()

    raw = jnp.dot(x_ref[...], w_ref[0], preferred_element_type=jnp.float32)
    for head in range(chunk // HDIM):
        cols = slice(head * HDIM, (head + 1) * HDIM)
        part = raw[:rows, cols].reshape(rows // tokens, tokens, HDIM)
        turned = spin(part, cos_ref[...][None], sin_ref[...][None])
        out_ref[:, cols] = turned.reshape(rows, HDIM).astype(jnp.bfloat16)
    last_ref[...] = raw[rows:]


def project_query(strips, normed, asked, cosine, sine, rows):
    width = normed.shape[1]
    chunk = strips.shape[2]
    extra = asked.shape[0]
    table = pl.BlockSpec(cosine.shape, lambda i: (0, 0))
    anywhere = pl.BlockSpec(memory_space=pl.ANY)
    return pl.pallas_call(
        query_kernel,
        grid=(QW // chunk,),
        in_specs=[
            anywhere,
            anywhere,
            pl.BlockSpec((1, width, chunk), lambda i: (i, 0, 0)),
            table,
            table,
        ],
        out_specs=[
            pl.BlockSpec((rows, chunk), lambda i: (0, i)),
            pl.BlockSpec((extra, chunk), lambda i: (0, i)),
        ],
        out_shape=[
            jax.ShapeDtypeStruct((rows, QW), jnp.bfloat16),
            jax.ShapeDtypeStruct((extra, QW), jnp.float32),
        ],
        scratch_shapes=[
            pltpu.VMEM((rows + extra, width), jnp.bfloat16),
            pltpu.SemaphoreType.DMA((2,)),
        ],
        compiler_params=pltpu.CompilerParams(vmem_limit_bytes=VMEM),
        name="project_query",
    )(normed, asked, strips, cosine, sine)


def attend_kernel(
    slot_ref, length_ref, where_ref, q_ref, *rest, swapped, start, absent
):
    parts, kpos_ref = rest[:PARTS], rest[PARTS]
    out_ref, held, zeros, listed, sems = rest[-5:]
    blocks, tokens, _ = q_ref.shape
    slots = slot_ref.shape[0]
    base = where_ref[0]
    row, wanted = where_ref[1], where_ref[2]
    rows = PER * tokens
    zeros[...] = jnp.zeros_like(zeros)

    def attend_block(block, groups):
        length = length_ref[start + block]
        kpos = kpos_ref[0:1, : groups * SIDE * tokens]
        qpos = base + lax.rem(lax.broadcasted_iota(jnp.int32, (rows, 1), 0), tokens)
        allowed = (kpos <= qpos) & (kpos < length)
        kept = (base + lax.broadcasted_iota(jnp.int32, (tokens, 1), 0)) < length

        def side_by_side(first):
            picked = []
            for dx in BACK[:groups]:
                for dy in range(SIDE):
                    ref, index = part_of(parts, swapped, dx, dy)
                    picked.append(ref[index, block, :, first : first + HDIM])
            return jnp.concatenate(picked, axis=0)

        for g in range(KVHEADS):
            heads = range(g * PER, (g + 1) * PER)
            queries = jnp.concatenate(
                [q_ref[block, :, h * HDIM : (h + 1) * HDIM] for h in heads], axis=0
            )
            logits = lax.dot_general(
                queries,
                side_by_side(g * HDIM),
                (((1,), (1,)), ((), ())),
                preferred_element_type=jnp.float32,
            )
            logits = jnp.where(allowed, logits * SCALE2, -1e30)
            weights = jnp.exp2(logits - jnp.max(logits, axis=-1, keepdims=True))
            total = jnp.sum(weights, axis=-1, keepdims=True)
            mixed = jnp.dot(
                weights.astype(jnp.bfloat16),
                side_by_side(KW + g * HDIM),
                preferred_element_type=jnp.float32,
            ) / total
            for h in heads:
                at = (h - g * PER) * tokens
                held[block, :, h * HDIM : (h + 1) * HDIM] = jnp.where(
                    kept, mixed[at : at + tokens], 0.0
                ).astype(jnp.bfloat16)

    def enlist(block, count):
        listed[count] = block
        alive = (start + block < wanted) & (base < length_ref[start + block])
        return count + alive.astype(jnp.int32)

    count = lax.fori_loop(0, blocks, enlist, jnp.int32(0))

    def each_block(groups):
        def body(pair, carry):
            attend_block(listed[2 * pair], groups)
            attend_block(listed[jnp.minimum(2 * pair + 1, count - 1)], groups)
            return carry

        lax.fori_loop(0, lax.div(count + 1, 2), body, 0)

    for x in range(SIDE):

        @pl.when(row == x)
        def _(x=x):
            each_block(x + 1)

    def copies(slot, act):
        block = slot_ref[slot]
        here = (block >= start) & (block < start + blocks)
        local = jnp.clip(block - start, 0, blocks - 1)
        filled = here & (base < length_ref[start + local])
        empty = here & jnp.logical_not(base < length_ref[start + local])
        if absent:
            empty = empty | (block < 0)

        @pl.when(filled)
        def _():
            act(pltpu.make_async_copy(held.at[local], out_ref.at[slot], sems.at[slot]))

        @pl.when(empty)
        def _():
            act(pltpu.make_async_copy(zeros, out_ref.at[slot], sems.at[slot]))

    def send(slot, carry):
        copies(slot, lambda copy: copy.start())
        return carry

    def finish(slot, carry):
        copies(slot, lambda copy: copy.wait())
        return carry

    lax.fori_loop(0, slots, send, 0)
    lax.fori_loop(0, slots, finish, 0)


def attend(slot_block, lengths, where, queries, parts, kpos, swapped, start, earlier):
    blocks, tokens = parts[0].shape[1:3]
    width = QW
    slots = slot_block.shape[0]
    anywhere = pl.BlockSpec(memory_space=pl.ANY)

    def whole(array):
        return pl.BlockSpec(array.shape, lambda i, *_: (0,) * array.ndim)

    given = () if earlier is None else (earlier,)
    return pl.pallas_call(
        lambda *refs: attend_kernel(
            *refs, swapped=swapped, start=start, absent=earlier is None
        ),
        grid_spec=pltpu.PrefetchScalarGridSpec(
            num_scalar_prefetch=3,
            grid=(1,),
            in_specs=[
                pl.BlockSpec((blocks, tokens, width), lambda i, *_: (start // blocks, 0, 0)),
                *[whole(part) for part in parts],
                whole(kpos),
                *[anywhere for _ in given],
            ],
            out_specs=anywhere,
            scratch_shapes=[
                pltpu.VMEM((blocks, tokens, width), jnp.bfloat16),
                pltpu.VMEM((tokens, width), jnp.bfloat16),
                pltpu.SMEM((blocks + 1,), jnp.int32),
                pltpu.SemaphoreType.DMA((slots,)),
            ],
        ),
        out_shape=jax.ShapeDtypeStruct((slots, tokens, width), jnp.bfloat16),
        input_output_aliases={5 + PARTS: 0} if given else {},
        compiler_params=pltpu.CompilerParams(vmem_limit_bytes=VMEM),
        name="attend_second" if given else "attend_first",
    )(slot_block, lengths, where, queries, *parts, kpos, *given)


def score_kernel(count_ref, block_ref, length_ref, which_ref, size_ref, last_ref, *rest):
    parts_a, parts_b, rest = rest[:PARTS], rest[PARTS : 2 * PARTS], rest[2 * PARTS :]
    qkv_ref, kpos_ref, cos_ref, sin_ref, w_ref, out_ref, kv_ref, sems = rest
    half, q_span = size_ref[0], size_ref[1]
    count = count_ref[0]

    def fetch(step, act):
        slot = lax.rem(step, 2)
        block = block_ref[step]
        for which, parts in enumerate((parts_a, parts_b)):

            @pl.when((block >= half) if which else (block < half))
            def _(which=which, parts=parts):
                local = jnp.clip(block - which * half, 0, parts[0].shape[1] - 1)
                for number, part in enumerate(parts):
                    held = kv_ref.at[slot, pl.ds(2 * number, 2)]
                    act(pltpu.make_async_copy(part.at[:, local], held, sems.at[slot, number]))

    @pl.when(count > 0)
    def _():
        fetch(0, lambda copy: copy.start())

    def body(step, carry):
        @pl.when(step + 1 < count)
        def _():
            fetch(step + 1, lambda copy: copy.start())

        fetch(step, lambda copy: copy.wait())
        slot = lax.rem(step, 2)
        length = length_ref[step]
        which = which_ref[step]
        second = (block_ref[step] >= half).astype(jnp.int32)
        kpos = kpos_ref[pl.ds(second, 1), :]
        live = kpos < length
        span = qkv_ref.shape[0]
        lane = lax.broadcasted_iota(jnp.int32, (1, span), 1)
        own = lax.div(lane, q_span) == which
        at_far = pl.ds(length + QLEN - 1, 1)
        far_cos, far_sin = cos_ref[at_far, :], sin_ref[at_far, :]
        near_cos, near_sin = cos_ref[QLEN - 1 : QLEN, :], sin_ref[QLEN - 1 : QLEN, :]
        total_score = jnp.zeros((1, HDIM), jnp.float32)
        over = (((1,), (1,)), ((), ()))
        for g in range(KVHEADS):
            raw = last_ref[which, g]
            far = spin(raw, far_cos, far_sin).astype(jnp.bfloat16)
            near = spin(raw, near_cos, near_sin).astype(jnp.bfloat16)
            keys = kv_ref[slot, :, :, g * HDIM : (g + 1) * HDIM].reshape(BLK, HDIM)
            values = kv_ref[slot, :, :, KW + g * HDIM : KW + (g + 1) * HDIM].reshape(BLK, HDIM)
            passage = lax.dot_general(far, keys, over, preferred_element_type=jnp.float32)
            question = lax.dot_general(
                near,
                qkv_ref[:, g * HDIM : (g + 1) * HDIM],
                over,
                preferred_element_type=jnp.float32,
            )
            passage = jnp.where(live, passage * SCALE2, -1e30)
            question = jnp.where(own, question * SCALE2, -1e30)
            peak = jnp.maximum(
                jnp.max(passage, axis=-1, keepdims=True), jnp.max(question, axis=-1, keepdims=True)
            )
            passage = jnp.exp2(passage - peak)
            question = jnp.exp2(question - peak)
            total = jnp.sum(passage, axis=-1, keepdims=True) + jnp.sum(
                question, axis=-1, keepdims=True
            )
            mixed = jnp.dot(
                passage.astype(jnp.bfloat16), values, preferred_element_type=jnp.float32
            ) + jnp.dot(
                question.astype(jnp.bfloat16),
                qkv_ref[:, KW + g * HDIM : KW + (g + 1) * HDIM],
                preferred_element_type=jnp.float32,
            )
            context = (mixed / total).astype(jnp.bfloat16).astype(jnp.float32)
            total_score += jnp.sum(context * w_ref[g], axis=0, keepdims=True)
        result = jnp.sum(total_score, axis=-1, keepdims=True)
        out_ref[pl.ds(step, 1), :] = jnp.broadcast_to(result, (1, HDIM))
        return carry

    lax.fori_loop(0, count, body, 0)


def score(
    count, blocks, lengths, which, last, first, second, question_kv, kpos, cosine, sine, w
):
    slots = blocks.shape[0]
    anywhere = pl.BlockSpec(memory_space=pl.ANY)
    tokens = first[0].shape[2]

    def whole(array):
        return pl.BlockSpec(array.shape, lambda i, *_: (0,) * array.ndim)

    return pl.pallas_call(
        score_kernel,
        grid_spec=pltpu.PrefetchScalarGridSpec(
            num_scalar_prefetch=5,
            grid=(1,),
            in_specs=[
                whole(last),
                *[anywhere] * (2 * PARTS),
                whole(question_kv),
                whole(kpos),
                whole(cosine),
                whole(sine),
                whole(w),
            ],
            out_specs=pl.BlockSpec((slots, HDIM), lambda i, *_: (0, 0)),
            scratch_shapes=[
                pltpu.VMEM((2, SIDE * SIDE, tokens, 2 * KW), jnp.bfloat16),
                pltpu.SemaphoreType.DMA((2, PARTS)),
            ],
        ),
        out_shape=jax.ShapeDtypeStruct((slots, HDIM), jnp.float32),
        compiler_params=pltpu.CompilerParams(vmem_limit_bytes=VMEM),
        name="score",
    )(
        count,
        blocks,
        lengths,
        which,
        jnp.array([first[0].shape[1], QLEN], jnp.int32),
        last,
        *first,
        *second,
        question_kv,
        kpos,
        cosine,
        sine,
        w,
    )


def sorted_by(key):
    count = key.shape[0]
    place = jnp.arange(count, dtype=jnp.int32)
    ahead = (key[None, :] < key[:, None]) | (
        (key[None, :] == key[:, None]) & (place[None, :] < place[:, None])
    )
    rank = jnp.sum(ahead.astype(jnp.int32), axis=1)
    chosen = rank[None, :] == place[:, None]

    def arrange(values):
        return jnp.sum(jnp.where(chosen, values[None, :], 0), axis=1).astype(jnp.int32)

    return arrange, rank


def on_device(
    store_rows,
    block_lengths,
    queries,
    cand_owner,
    cand_block,
    cand_query,
    norm_gain,
    w_query,
    w_key,
    w_value,
    w_score,
):
    n_corpus = lax.axis_size("corpus")
    n_rerank = lax.axis_size("rerank")
    corpus_index = lax.axis_index("corpus")
    member = lax.axis_index("rerank")
    pair_total = cand_block.shape[0]
    pair_group = pair_total // n_corpus
    own_blocks, tokens, width = store_rows.shape
    n_query, q_tokens, _ = queries.shape
    q_dev = n_query // n_rerank

    owners = cand_owner[:, 0]
    pair_order = jnp.arange(pair_total, dtype=jnp.int32)
    group_of = pair_order // pair_group
    earlier = (
        (owners[:, None] == owners[None, :])
        & (group_of[:, None] == group_of[None, :])
        & (pair_order[None, :] < pair_order[:, None])
    )
    owner_rank = jnp.sum(earlier.astype(jnp.int32), axis=1)
    slot_ids = jnp.arange(n_corpus * CAP, dtype=jnp.int32)
    wanted = (
        (group_of[None, :] == (slot_ids // CAP)[:, None])
        & (owners[None, :] == corpus_index)
        & (owner_rank[None, :] == (slot_ids % CAP)[:, None])
    )
    present = jnp.any(wanted, axis=1)

    def of_slot(values):
        return jnp.sum(jnp.where(wanted, values[None, :], 0), axis=1)

    slot_query, slot_pair, stored_block = of_slot(cand_query), of_slot(pair_order), of_slot(cand_block)
    block_ids = jnp.arange(own_blocks, dtype=jnp.int32)
    owner_ids = jnp.arange(n_corpus, dtype=jnp.int32)
    named = jnp.any(
        (owners[None, None, :] == owner_ids[:, None, None])
        & (cand_block[None, None, :] == block_ids[None, :, None]),
        axis=2,
    )
    most = jnp.max(jnp.sum(named.astype(jnp.int32), axis=1))
    want = jnp.any(named & (owner_ids[:, None] == corpus_index), axis=0)
    want_count = jnp.sum(want.astype(jnp.int32))
    by_want, want_rank = sorted_by(jnp.where(want, 0, 1))
    block_order = by_want(block_ids)
    own_lengths = by_want(
        lax.dynamic_slice_in_dim(block_lengths, corpus_index * own_blocks, own_blocks, 0)
    )
    is_block = stored_block[:, None] == block_ids[None, :]
    slot_block = jnp.sum(jnp.where(is_block, want_rank[None, :], 0), axis=1)
    slot_length = jnp.sum(
        jnp.where(slot_block[:, None] == block_ids[None, :], own_lengths[None, :], 0), axis=1
    )
    slot_or_none = jnp.where(present, slot_block, -1)
    mine = present & (slot_query // q_dev == member)
    by_mine, _ = sorted_by(jnp.where(mine, slot_block, own_blocks))
    mine_count = jnp.sum(mine.astype(jnp.int32)).reshape(1)
    mine_block, mine_length = by_mine(slot_block), by_mine(slot_length)
    mine_which, mine_pair = by_mine(slot_query % q_dev), by_mine(slot_pair)

    all_cos, all_sin = rope_tables(jnp.arange(BLK + QLEN, dtype=jnp.int32))
    base = member * tokens
    own_cos, own_sin = rope_tables(base + jnp.arange(tokens, dtype=jnp.int32))
    x, y = member // SIDE, member % SIDE
    hops = jnp.array(HOPS, jnp.int32)
    xs, ys = (x + hops) % SIDE, (y + hops) % SIDE

    strip = QW // (n_corpus - 1)
    my_columns = lax.dynamic_slice_in_dim(
        w_query, jnp.minimum(corpus_index, n_corpus - 2) * strip, strip, 1
    )
    w_first = lax.all_gather(
        jnp.concatenate([w_key, w_value, my_columns], axis=1), "rerank", axis=0, tiled=True
    )
    my_strip = w_first[:, 2 * KW :]
    gain = norm_gain.astype(jnp.float32).reshape(1, width)
    normed = norm(block_order, store_rows, gain)

    asked = lax.all_to_all(queries, "rerank", 0, 1, tiled=True).reshape(q_dev * QLEN, width)
    asked_token = jnp.arange(asked.shape[0], dtype=jnp.int32) % QLEN
    asked_cos, asked_sin = rope_tables(asked_token)


    inside = jnp.arange(tokens, dtype=jnp.int32)

    def positions_of(ranks):
        return (ranks[..., None] * tokens + inside).reshape(1, BLK)

    xb = (x - jnp.arange(SIDE, dtype=jnp.int32)) % SIDE
    kpos = positions_of(xb[:, None] * SIDE + ys[None, :])
    part_pos = jnp.concatenate(
        [
            positions_of(xs[:, None] * SIDE + ys[None, :]),
            positions_of(xs[None, :] * SIDE + ys[:, None]),
        ]
    )

    head_w = jnp.pad(
        w_score.astype(jnp.float32).reshape(KVHEADS, PER, HDIM), ((0, 0), (0, 8 - PER), (0, 0))
    )
    where = jnp.stack([base, x, want_count]).astype(jnp.int32)
    def attended(blocks):
        half = blocks // 2
        strips = lax.all_gather(my_strip, "corpus", axis=0, tiled=False)
        kv = key_value(normed, w_first, own_cos, own_sin, blocks * tokens)
        passage_kv = kv.reshape(blocks, tokens, 2 * KW)
        first, second = plane_gather(passage_kv[:half], passage_kv[half:])
        asked_normed, question_kv = asked_key_value(asked, gain, w_first, asked_cos, asked_sin)
        asked_last = jnp.pad(asked_normed[QLEN - 1 :: QLEN], ((0, 16 - q_dev), (0, 0)))
        query_rot, query_last = project_query(
            strips, normed, asked_last, own_cos, own_sin, blocks * tokens
        )
        last = query_last[:q_dev].reshape(q_dev, KVHEADS, PER, HDIM)
        last = jnp.pad(last, ((0, 0), (0, 0), (0, 8 - PER), (0, 0)))
        scored = score(
            mine_count,
            mine_block,
            mine_length,
            mine_which,
            last,
            first,
            second,
            question_kv,
            part_pos,
            all_cos,
            all_sin,
            head_w,
        )[: n_corpus * CAP, 0]
        valid = slot_ids < mine_count[0]
        placed = jnp.sum(
            jnp.where(
                valid[:, None] & (mine_pair[:, None] == pair_order[None, :]), scored[:, None], 0.0
            ),
            axis=0,
        )
        query_rot = query_rot.reshape(blocks, tokens, QW)
        gathered = lax.all_to_all(placed.reshape(n_corpus, pair_group), "corpus", 0, 0, tiled=True)
        begun = attend(
            slot_or_none, own_lengths, where, query_rot, first, kpos, False, 0, None
        )
        gathered, begun = tie(gathered, begun)
        shared = jnp.sum(gathered, axis=0).reshape(n_rerank, pair_group // n_rerank)
        pair_scores = jnp.sum(lax.all_to_all(shared, "rerank", 0, 0, tiled=True), axis=0)
        passage_context = attend(
            slot_or_none, own_lengths, where, query_rot, second, kpos, True, half, begun
        )
        return passage_context, pair_scores

    choice = sum((most > size).astype(jnp.int32) for size in SIZES)
    return lax.switch(choice, [lambda size=size: attended(size) for size in (*SIZES, own_blocks)])


def solution(mesh):
    placed = (
        P("corpus", "rerank", None),
        P(),
        P(None, "rerank", None),
        P(),
        P(),
        P(),
        P(),
        P("rerank", None),
        P("rerank", None),
        P("rerank", None),
        P(),
    )
    return jax.shard_map(
        on_device,
        mesh=mesh,
        in_specs=placed,
        out_specs=(P("corpus", "rerank", None), P(("corpus", "rerank"))),
        check_vma=False,
    )
```

```python
import jax
import jax.numpy as jnp
from jax import lax
from jax.experimental import pallas as pl
from jax.experimental.pallas import tpu as pltpu
from jax.sharding import PartitionSpec as P

HDIM = 128
QHEADS = 14
KVHEADS = 2
PER = QHEADS // KVHEADS
QW = QHEADS * HDIM
KW = KVHEADS * HDIM
BLK = 512
QLEN = 64
CAP = 5
SIDE = 4
SIZES = (24, 26, 28)
ROPE_BASE = 1000000.0
EPSILON = 1e-06
SCALE2 = HDIM ** (-0.5) * 1.4426950408889634
VMEM = 56 * 1024 * 1024


def rope_tables(positions):
    half = HDIM // 2
    inverse = jnp.power(ROPE_BASE, -2.0 * jnp.arange(half, dtype=jnp.float32) / HDIM)
    angles = positions.astype(jnp.float32)[:, None] * inverse
    cosine, sine = jnp.cos(angles), jnp.sin(angles)
    return (
        jnp.concatenate([cosine, cosine], axis=1),
        jnp.concatenate([-sine, sine], axis=1),
    )


def spin(part, cosine, sine):
    return part * cosine + pltpu.roll(part, HDIM // 2, part.ndim - 1) * sine


def shift(value, dim, step):
    def moved(index):
        x, y = index // SIDE, index % SIDE
        if dim == "x":
            x = (x + step) % SIDE
        else:
            y = (y + step) % SIDE
        return x * SIDE + y

    return lax.ppermute(value, "rerank", [(i, moved(i)) for i in range(SIDE * SIDE)])


def tie(*values):
    return lax.optimization_barrier(values)


def plane_gather(value_a, value_b):
    a_low, a_high, a_far = (shift(value_a, "y", step) for step in (1, -1, 2))
    b_low, b_high, b_far = (shift(value_b, "x", step) for step in (1, -1, 2))
    a_low, a_high, a_far, b_low, b_high, b_far = tie(a_low, a_high, a_far, b_low, b_high, b_far)
    a0, a1 = jnp.stack([value_a, a_low]), jnp.stack([a_high, a_far])
    b0, b1 = jnp.stack([value_b, b_low]), jnp.stack([b_high, b_far])
    a0_low, b0_low = shift(a0, "x", 1), shift(b0, "y", 1)
    a1_high, b1_high = shift(a1, "x", -1), shift(b1, "y", -1)
    a1_low, b1_low = shift(a1, "x", 1), shift(b1, "y", 1)
    a0_high, b0_high = shift(a0, "x", -1), shift(b0, "y", -1)
    a0_low, b0_low, a1_high, b1_high = tie(a0_low, b0_low, a1_high, b1_high)
    a0_far, b0_far = shift(a0_low, "x", 1), shift(b0_low, "y", 1)
    a1_far, b1_far = shift(a1_high, "x", -1), shift(b1_high, "y", -1)
    return (
        (a0, a1, a0_low, a1_low, a0_high, a1_high, a0_far, a1_far),
        (b0, b1, b0_low, b1_low, b0_high, b1_high, b0_far, b1_far),
    )


PARTS = 8
HOPS = (0, -1, 1, 2)
BACK = (0, 1, 3, 2)


def part_of(parts, swapped, dx, dy):
    outer, inner = (dy, dx) if swapped else (dx, dy)
    return parts[2 * outer + inner // 2], inner % 2


def normed_of(rows, gain):
    wide = rows.astype(jnp.float32)
    inverse = lax.rsqrt(jnp.mean(wide * wide, axis=-1, keepdims=True) + EPSILON)
    return (wide * inverse * gain).astype(jnp.bfloat16)


GROUP = 4


def norm_kernel(order_ref, *refs):
    blocks, (gain_ref, out_ref) = refs[:GROUP], refs[GROUP:]
    tokens = blocks[0].shape[1]
    for number, block in enumerate(blocks):
        out_ref[number * tokens : (number + 1) * tokens] = normed_of(block[0], gain_ref[...])


def norm(order, store, gain):
    blocks, tokens, width = store.shape
    return pl.pallas_call(
        norm_kernel,
        grid_spec=pltpu.PrefetchScalarGridSpec(
            num_scalar_prefetch=1,
            grid=(blocks // GROUP,),
            in_specs=[
                *[
                    pl.BlockSpec(
                        (1, tokens, width), lambda i, order, n=n: (order[GROUP * i + n], 0, 0)
                    )
                    for n in range(GROUP)
                ],
                pl.BlockSpec((1, width), lambda i, order: (0, 0)),
            ],
            out_specs=pl.BlockSpec((GROUP * tokens, width), lambda i, order: (i, 0)),
        ),
        out_shape=jax.ShapeDtypeStruct((blocks * tokens, width), jnp.bfloat16),
        compiler_params=pltpu.CompilerParams(vmem_limit_bytes=VMEM),
        name="norm",
    )(order, *[store] * GROUP, gain)


def key_value_kernel(normed_ref, w_ref, cos_ref, sin_ref, kv_ref):
    rows = normed_ref.shape[0]
    tokens = cos_ref.shape[0]
    raw = jnp.dot(normed_ref[...], w_ref[...], preferred_element_type=jnp.float32)
    for head in range(KVHEADS):
        cols = slice(head * HDIM, (head + 1) * HDIM)
        part = raw[:, cols].reshape(rows // tokens, tokens, HDIM)
        turned = spin(part, cos_ref[...][None], sin_ref[...][None])
        kv_ref[:, cols] = turned.reshape(rows, HDIM).astype(jnp.bfloat16)
    kv_ref[:, KW:] = raw[:, KW:].astype(jnp.bfloat16)


def key_value(normed, w_kv, cosine, sine, rows):
    tile = 128 if rows % 128 == 0 else rows // 2
    width = normed.shape[1]
    table = pl.BlockSpec(cosine.shape, lambda i: (0, 0))
    return pl.pallas_call(
        key_value_kernel,
        grid=(rows // tile,),
        in_specs=[
            pl.BlockSpec((tile, width), lambda i: (i, 0)),
            pl.BlockSpec((width, 2 * KW), lambda i: (0, 0)),
            table,
            table,
        ],
        out_specs=pl.BlockSpec((tile, 2 * KW), lambda i: (i, 0)),
        out_shape=jax.ShapeDtypeStruct((rows, 2 * KW), jnp.bfloat16),
        compiler_params=pltpu.CompilerParams(vmem_limit_bytes=VMEM),
        name="key_value",
    )(normed, w_kv, cosine, sine)


def asked_kernel(x_ref, gain_ref, w_ref, cos_ref, sin_ref, normed_ref, kv_ref):
    normed_ref[...] = normed_of(x_ref[...], gain_ref[...])
    raw = jnp.dot(normed_ref[...], w_ref[...], preferred_element_type=jnp.float32)
    for head in range(KVHEADS):
        cols = slice(head * HDIM, (head + 1) * HDIM)
        kv_ref[:, cols] = spin(raw[:, cols], cos_ref[...], sin_ref[...]).astype(jnp.bfloat16)
    kv_ref[:, KW:] = raw[:, KW:].astype(jnp.bfloat16)


def asked_key_value(rows, gain, w_kv, cosine, sine):
    def whole(shape):
        return pl.BlockSpec(shape, lambda i: (0, 0))

    width = rows.shape[1]
    return pl.pallas_call(
        asked_kernel,
        grid=(1,),
        in_specs=[
            whole(rows.shape),
            whole(gain.shape),
            whole((width, 2 * KW)),
            whole(cosine.shape),
            whole(sine.shape),
        ],
        out_specs=[whole(rows.shape), whole((rows.shape[0], 2 * KW))],
        out_shape=[
            jax.ShapeDtypeStruct(rows.shape, jnp.bfloat16),
            jax.ShapeDtypeStruct((rows.shape[0], 2 * KW), jnp.bfloat16),
        ],
        compiler_params=pltpu.CompilerParams(vmem_limit_bytes=VMEM),
        name="asked_key_value",
    )(rows, gain, w_kv, cosine, sine)


def query_kernel(normed_ref, asked_ref, w_ref, cos_ref, sin_ref, out_ref, last_ref, x_ref, sems):
    rows, chunk = out_ref.shape
    tokens = cos_ref.shape[0]
    extra = asked_ref.shape[0]

    @pl.when(pl.program_id(0) == 0)
    def _():
        copies = (
            pltpu.make_async_copy(
                normed_ref.at[pl.ds(0, rows)], x_ref.at[pl.ds(0, rows)], sems.at[0]
            ),
            pltpu.make_async_copy(asked_ref, x_ref.at[pl.ds(rows, extra)], sems.at[1]),
        )
        for copy in copies:
            copy.start()
        for copy in copies:
            copy.wait()

    raw = jnp.dot(x_ref[...], w_ref[0], preferred_element_type=jnp.float32)
    for head in range(chunk // HDIM):
        cols = slice(head * HDIM, (head + 1) * HDIM)
        part = raw[:rows, cols].reshape(rows // tokens, tokens, HDIM)
        turned = spin(part, cos_ref[...][None], sin_ref[...][None])
        out_ref[:, cols] = turned.reshape(rows, HDIM).astype(jnp.bfloat16)
    last_ref[...] = raw[rows:]


def project_query(strips, normed, asked, cosine, sine, rows):
    width = normed.shape[1]
    chunk = strips.shape[2]
    extra = asked.shape[0]
    table = pl.BlockSpec(cosine.shape, lambda i: (0, 0))
    anywhere = pl.BlockSpec(memory_space=pl.ANY)
    return pl.pallas_call(
        query_kernel,
        grid=(QW // chunk,),
        in_specs=[
            anywhere,
            anywhere,
            pl.BlockSpec((1, width, chunk), lambda i: (i, 0, 0)),
            table,
            table,
        ],
        out_specs=[
            pl.BlockSpec((rows, chunk), lambda i: (0, i)),
            pl.BlockSpec((extra, chunk), lambda i: (0, i)),
        ],
        out_shape=[
            jax.ShapeDtypeStruct((rows, QW), jnp.bfloat16),
            jax.ShapeDtypeStruct((extra, QW), jnp.float32),
        ],
        scratch_shapes=[
            pltpu.VMEM((rows + extra, width), jnp.bfloat16),
            pltpu.SemaphoreType.DMA((2,)),
        ],
        compiler_params=pltpu.CompilerParams(vmem_limit_bytes=VMEM),
        name="project_query",
    )(normed, asked, strips, cosine, sine)


def attend_kernel(
    slot_ref, length_ref, where_ref, q_ref, *rest, swapped, start, absent
):
    parts, kpos_ref = rest[:PARTS], rest[PARTS]
    out_ref, held, zeros, listed, sems = rest[-5:]
    blocks, tokens, _ = q_ref.shape
    slots = slot_ref.shape[0]
    base = where_ref[0]
    row, wanted = where_ref[1], where_ref[2]
    rows = PER * tokens
    zeros[...] = jnp.zeros_like(zeros)

    def attend_block(block, groups):
        length = length_ref[start + block]
        kpos = kpos_ref[0:1, : groups * SIDE * tokens]
        qpos = base + lax.rem(lax.broadcasted_iota(jnp.int32, (rows, 1), 0), tokens)
        allowed = (kpos <= qpos) & (kpos < length)
        kept = (base + lax.broadcasted_iota(jnp.int32, (tokens, 1), 0)) < length

        def side_by_side(first):
            picked = []
            for dx in BACK[:groups]:
                for dy in range(SIDE):
                    ref, index = part_of(parts, swapped, dx, dy)
                    picked.append(ref[index, block, :, first : first + HDIM])
            return jnp.concatenate(picked, axis=0)

        for g in range(KVHEADS):
            heads = range(g * PER, (g + 1) * PER)
            queries = jnp.concatenate(
                [q_ref[block, :, h * HDIM : (h + 1) * HDIM] for h in heads], axis=0
            )
            logits = lax.dot_general(
                queries,
                side_by_side(g * HDIM),
                (((1,), (1,)), ((), ())),
                preferred_element_type=jnp.float32,
            )
            logits = jnp.where(allowed, logits * SCALE2, -1e30)
            weights = jnp.exp2(logits - jnp.max(logits, axis=-1, keepdims=True))
            total = jnp.sum(weights, axis=-1, keepdims=True)
            mixed = jnp.dot(
                weights.astype(jnp.bfloat16),
                side_by_side(KW + g * HDIM),
                preferred_element_type=jnp.float32,
            ) / total
            for h in heads:
                at = (h - g * PER) * tokens
                held[block, :, h * HDIM : (h + 1) * HDIM] = jnp.where(
                    kept, mixed[at : at + tokens], 0.0
                ).astype(jnp.bfloat16)

    def enlist(block, count):
        listed[count] = block
        alive = (start + block < wanted) & (base < length_ref[start + block])
        return count + alive.astype(jnp.int32)

    count = lax.fori_loop(0, blocks, enlist, jnp.int32(0))

    def each_block(groups):
        def body(pair, carry):
            attend_block(listed[2 * pair], groups)
            attend_block(listed[jnp.minimum(2 * pair + 1, count - 1)], groups)
            return carry

        lax.fori_loop(0, lax.div(count + 1, 2), body, 0)

    for x in range(SIDE):

        @pl.when(row == x)
        def _(x=x):
            each_block(x + 1)

    def copies(slot, act):
        block = slot_ref[slot]
        here = (block >= start) & (block < start + blocks)
        local = jnp.clip(block - start, 0, blocks - 1)
        filled = here & (base < length_ref[start + local])
        empty = here & jnp.logical_not(base < length_ref[start + local])
        if absent:
            empty = empty | (block < 0)

        @pl.when(filled)
        def _():
            act(pltpu.make_async_copy(held.at[local], out_ref.at[slot], sems.at[slot]))

        @pl.when(empty)
        def _():
            act(pltpu.make_async_copy(zeros, out_ref.at[slot], sems.at[slot]))

    def send(slot, carry):
        copies(slot, lambda copy: copy.start())
        return carry

    def finish(slot, carry):
        copies(slot, lambda copy: copy.wait())
        return carry

    lax.fori_loop(0, slots, send, 0)
    lax.fori_loop(0, slots, finish, 0)


def attend(slot_block, lengths, where, queries, parts, kpos, swapped, start, earlier):
    blocks, tokens = parts[0].shape[1:3]
    width = QW
    slots = slot_block.shape[0]
    anywhere = pl.BlockSpec(memory_space=pl.ANY)

    def whole(array):
        return pl.BlockSpec(array.shape, lambda i, *_: (0,) * array.ndim)

    given = () if earlier is None else (earlier,)
    return pl.pallas_call(
        lambda *refs: attend_kernel(
            *refs, swapped=swapped, start=start, absent=earlier is None
        ),
        grid_spec=pltpu.PrefetchScalarGridSpec(
            num_scalar_prefetch=3,
            grid=(1,),
            in_specs=[
                pl.BlockSpec((blocks, tokens, width), lambda i, *_: (start // blocks, 0, 0)),
                *[whole(part) for part in parts],
                whole(kpos),
                *[anywhere for _ in given],
            ],
            out_specs=anywhere,
            scratch_shapes=[
                pltpu.VMEM((blocks, tokens, width), jnp.bfloat16),
                pltpu.VMEM((tokens, width), jnp.bfloat16),
                pltpu.SMEM((blocks + 1,), jnp.int32),
                pltpu.SemaphoreType.DMA((slots,)),
            ],
        ),
        out_shape=jax.ShapeDtypeStruct((slots, tokens, width), jnp.bfloat16),
        input_output_aliases={5 + PARTS: 0} if given else {},
        compiler_params=pltpu.CompilerParams(vmem_limit_bytes=VMEM),
        name="attend_second" if given else "attend_first",
    )(slot_block, lengths, where, queries, *parts, kpos, *given)


def score_kernel(count_ref, block_ref, length_ref, which_ref, size_ref, last_ref, *rest):
    parts_a, parts_b, rest = rest[:PARTS], rest[PARTS : 2 * PARTS], rest[2 * PARTS :]
    qkv_ref, kpos_ref, cos_ref, sin_ref, w_ref, out_ref, kv_ref, sems = rest
    half, q_span = size_ref[0], size_ref[1]
    count = count_ref[0]

    def fetch(step, act):
        slot = lax.rem(step, 2)
        block = block_ref[step]
        for which, parts in enumerate((parts_a, parts_b)):

            @pl.when((block >= half) if which else (block < half))
            def _(which=which, parts=parts):
                local = jnp.clip(block - which * half, 0, parts[0].shape[1] - 1)
                for number, part in enumerate(parts):
                    held = kv_ref.at[slot, pl.ds(2 * number, 2)]
                    act(pltpu.make_async_copy(part.at[:, local], held, sems.at[slot, number]))

    @pl.when(count > 0)
    def _():
        fetch(0, lambda copy: copy.start())

    def body(step, carry):
        @pl.when(step + 1 < count)
        def _():
            fetch(step + 1, lambda copy: copy.start())

        fetch(step, lambda copy: copy.wait())
        slot = lax.rem(step, 2)
        length = length_ref[step]
        which = which_ref[step]
        second = (block_ref[step] >= half).astype(jnp.int32)
        kpos = kpos_ref[pl.ds(second, 1), :]
        live = kpos < length
        span = qkv_ref.shape[0]
        lane = lax.broadcasted_iota(jnp.int32, (1, span), 1)
        own = lax.div(lane, q_span) == which
        at_far = pl.ds(length + QLEN - 1, 1)
        far_cos, far_sin = cos_ref[at_far, :], sin_ref[at_far, :]
        near_cos, near_sin = cos_ref[QLEN - 1 : QLEN, :], sin_ref[QLEN - 1 : QLEN, :]
        total_score = jnp.zeros((1, HDIM), jnp.float32)
        over = (((1,), (1,)), ((), ()))
        for g in range(KVHEADS):
            raw = last_ref[which, g]
            far = spin(raw, far_cos, far_sin).astype(jnp.bfloat16)
            near = spin(raw, near_cos, near_sin).astype(jnp.bfloat16)
            keys = kv_ref[slot, :, :, g * HDIM : (g + 1) * HDIM].reshape(BLK, HDIM)
            values = kv_ref[slot, :, :, KW + g * HDIM : KW + (g + 1) * HDIM].reshape(BLK, HDIM)
            passage = lax.dot_general(far, keys, over, preferred_element_type=jnp.float32)
            question = lax.dot_general(
                near,
                qkv_ref[:, g * HDIM : (g + 1) * HDIM],
                over,
                preferred_element_type=jnp.float32,
            )
            passage = jnp.where(live, passage * SCALE2, -1e30)
            question = jnp.where(own, question * SCALE2, -1e30)
            peak = jnp.maximum(
                jnp.max(passage, axis=-1, keepdims=True), jnp.max(question, axis=-1, keepdims=True)
            )
            passage = jnp.exp2(passage - peak)
            question = jnp.exp2(question - peak)
            total = jnp.sum(passage, axis=-1, keepdims=True) + jnp.sum(
                question, axis=-1, keepdims=True
            )
            mixed = jnp.dot(
                passage.astype(jnp.bfloat16), values, preferred_element_type=jnp.float32
            ) + jnp.dot(
                question.astype(jnp.bfloat16),
                qkv_ref[:, KW + g * HDIM : KW + (g + 1) * HDIM],
                preferred_element_type=jnp.float32,
            )
            context = (mixed / total).astype(jnp.bfloat16).astype(jnp.float32)
            total_score += jnp.sum(context * w_ref[g], axis=0, keepdims=True)
        result = jnp.sum(total_score, axis=-1, keepdims=True)
        out_ref[pl.ds(step, 1), :] = jnp.broadcast_to(result, (1, HDIM))
        return carry

    lax.fori_loop(0, count, body, 0)


def score(
    count, blocks, lengths, which, last, first, second, question_kv, kpos, cosine, sine, w
):
    slots = blocks.shape[0]
    anywhere = pl.BlockSpec(memory_space=pl.ANY)
    tokens = first[0].shape[2]

    def whole(array):
        return pl.BlockSpec(array.shape, lambda i, *_: (0,) * array.ndim)

    return pl.pallas_call(
        score_kernel,
        grid_spec=pltpu.PrefetchScalarGridSpec(
            num_scalar_prefetch=5,
            grid=(1,),
            in_specs=[
                whole(last),
                *[anywhere] * (2 * PARTS),
                whole(question_kv),
                whole(kpos),
                whole(cosine),
                whole(sine),
                whole(w),
            ],
            out_specs=pl.BlockSpec((slots, HDIM), lambda i, *_: (0, 0)),
            scratch_shapes=[
                pltpu.VMEM((2, SIDE * SIDE, tokens, 2 * KW), jnp.bfloat16),
                pltpu.SemaphoreType.DMA((2, PARTS)),
            ],
        ),
        out_shape=jax.ShapeDtypeStruct((slots, HDIM), jnp.float32),
        compiler_params=pltpu.CompilerParams(vmem_limit_bytes=VMEM),
        name="score",
    )(
        count,
        blocks,
        lengths,
        which,
        jnp.array([first[0].shape[1], QLEN], jnp.int32),
        last,
        *first,
        *second,
        question_kv,
        kpos,
        cosine,
        sine,
        w,
    )


def sorted_by(key):
    count = key.shape[0]
    place = jnp.arange(count, dtype=jnp.int32)
    ahead = (key[None, :] < key[:, None]) | (
        (key[None, :] == key[:, None]) & (place[None, :] < place[:, None])
    )
    rank = jnp.sum(ahead.astype(jnp.int32), axis=1)
    chosen = rank[None, :] == place[:, None]

    def arrange(values):
        return jnp.sum(jnp.where(chosen, values[None, :], 0), axis=1).astype(jnp.int32)

    return arrange, rank


def on_device(
    store_rows,
    block_lengths,
    queries,
    cand_owner,
    cand_block,
    cand_query,
    norm_gain,
    w_query,
    w_key,
    w_value,
    w_score,
):
    n_corpus = lax.axis_size("corpus")
    n_rerank = lax.axis_size("rerank")
    corpus_index = lax.axis_index("corpus")
    member = lax.axis_index("rerank")
    pair_total = cand_block.shape[0]
    pair_group = pair_total // n_corpus
    own_blocks, tokens, width = store_rows.shape
    n_query, q_tokens, _ = queries.shape
    q_dev = n_query // n_rerank

    owners = cand_owner[:, 0]
    pair_order = jnp.arange(pair_total, dtype=jnp.int32)
    group_of = pair_order // pair_group
    earlier = (
        (owners[:, None] == owners[None, :])
        & (group_of[:, None] == group_of[None, :])
        & (pair_order[None, :] < pair_order[:, None])
    )
    owner_rank = jnp.sum(earlier.astype(jnp.int32), axis=1)
    slot_ids = jnp.arange(n_corpus * CAP, dtype=jnp.int32)
    wanted = (
        (group_of[None, :] == (slot_ids // CAP)[:, None])
        & (owners[None, :] == corpus_index)
        & (owner_rank[None, :] == (slot_ids % CAP)[:, None])
    )
    present = jnp.any(wanted, axis=1)

    def of_slot(values):
        return jnp.sum(jnp.where(wanted, values[None, :], 0), axis=1)

    slot_query, slot_pair, stored_block = of_slot(cand_query), of_slot(pair_order), of_slot(cand_block)
    block_ids = jnp.arange(own_blocks, dtype=jnp.int32)
    owner_ids = jnp.arange(n_corpus, dtype=jnp.int32)
    named = jnp.any(
        (owners[None, None, :] == owner_ids[:, None, None])
        & (cand_block[None, None, :] == block_ids[None, :, None]),
        axis=2,
    )
    most = jnp.max(jnp.sum(named.astype(jnp.int32), axis=1))
    want = jnp.any(named & (owner_ids[:, None] == corpus_index), axis=0)
    want_count = jnp.sum(want.astype(jnp.int32))
    by_want, want_rank = sorted_by(jnp.where(want, 0, 1))
    block_order = by_want(block_ids)
    own_lengths = by_want(
        lax.dynamic_slice_in_dim(block_lengths, corpus_index * own_blocks, own_blocks, 0)
    )
    is_block = stored_block[:, None] == block_ids[None, :]
    slot_block = jnp.sum(jnp.where(is_block, want_rank[None, :], 0), axis=1)
    slot_length = jnp.sum(
        jnp.where(slot_block[:, None] == block_ids[None, :], own_lengths[None, :], 0), axis=1
    )
    slot_or_none = jnp.where(present, slot_block, -1)
    mine = present & (slot_query // q_dev == member)
    by_mine, _ = sorted_by(jnp.where(mine, slot_block, own_blocks))
    mine_count = jnp.sum(mine.astype(jnp.int32)).reshape(1)
    mine_block, mine_length = by_mine(slot_block), by_mine(slot_length)
    mine_which, mine_pair = by_mine(slot_query % q_dev), by_mine(slot_pair)

    all_cos, all_sin = rope_tables(jnp.arange(BLK + QLEN, dtype=jnp.int32))
    base = member * tokens
    own_cos, own_sin = rope_tables(base + jnp.arange(tokens, dtype=jnp.int32))
    x, y = member // SIDE, member % SIDE
    hops = jnp.array(HOPS, jnp.int32)
    xs, ys = (x + hops) % SIDE, (y + hops) % SIDE

    strip = QW // (n_corpus - 1)
    my_columns = lax.dynamic_slice_in_dim(
        w_query, jnp.minimum(corpus_index, n_corpus - 2) * strip, strip, 1
    )
    w_first = lax.all_gather(
        jnp.concatenate([w_key, w_value, my_columns], axis=1), "rerank", axis=0, tiled=True
    )
    gain = norm_gain.astype(jnp.float32).reshape(1, width)
    normed = norm(block_order, store_rows, gain)

    asked = lax.all_to_all(queries, "rerank", 0, 1, tiled=True).reshape(q_dev * QLEN, width)
    asked_token = jnp.arange(asked.shape[0], dtype=jnp.int32) % QLEN
    asked_cos, asked_sin = rope_tables(asked_token)


    inside = jnp.arange(tokens, dtype=jnp.int32)

    def positions_of(ranks):
        return (ranks[..., None] * tokens + inside).reshape(1, BLK)

    xb = (x - jnp.arange(SIDE, dtype=jnp.int32)) % SIDE
    kpos = positions_of(xb[:, None] * SIDE + ys[None, :])
    part_pos = jnp.concatenate(
        [
            positions_of(xs[:, None] * SIDE + ys[None, :]),
            positions_of(xs[None, :] * SIDE + ys[:, None]),
        ]
    )

    head_w = jnp.pad(
        w_score.astype(jnp.float32).reshape(KVHEADS, PER, HDIM), ((0, 0), (0, 8 - PER), (0, 0))
    )
    where = jnp.stack([base, x, want_count]).astype(jnp.int32)
    belongs = (slot_ids < mine_count[0])[:, None] & (mine_pair[:, None] == pair_order[None, :])
    pair_dev = pair_group // n_rerank

    def attended(blocks):
        half = blocks // 2
        strips = lax.all_gather(w_first[:, 2 * KW :], "corpus", axis=0, tiled=False)
        kv = key_value(normed, w_first, own_cos, own_sin, blocks * tokens)
        passage_kv = kv.reshape(blocks, tokens, 2 * KW)
        first, second = plane_gather(passage_kv[:half], passage_kv[half:])
        asked_normed, question_kv = asked_key_value(asked, gain, w_first, asked_cos, asked_sin)
        asked_last = jnp.pad(asked_normed[QLEN - 1 :: QLEN], ((0, 16 - q_dev), (0, 0)))
        query_rot, query_last = project_query(
            strips, normed, asked_last, own_cos, own_sin, blocks * tokens
        )
        last = query_last[:q_dev].reshape(q_dev, KVHEADS, PER, HDIM)
        last = jnp.pad(last, ((0, 0), (0, 0), (0, 8 - PER), (0, 0)))
        scored = score(
            mine_count,
            mine_block,
            mine_length,
            mine_which,
            last,
            first,
            second,
            question_kv,
            part_pos,
            all_cos,
            all_sin,
            head_w,
        )[: n_corpus * CAP, 0]
        placed = jnp.sum(jnp.where(belongs, scored[:, None], 0.0), axis=0)
        query_rot = query_rot.reshape(blocks, tokens, QW)
        gathered = lax.all_to_all(
            placed.reshape(n_corpus * n_rerank, pair_dev), ("corpus", "rerank"), 0, 0, tiled=True
        )
        pair_scores = jnp.sum(gathered, axis=0)
        begun = attend(
            slot_or_none, own_lengths, where, query_rot, first, kpos, False, 0, None
        )
        passage_context = attend(
            slot_or_none, own_lengths, where, query_rot, second, kpos, True, half, begun
        )
        return passage_context, pair_scores

    choice = sum((most > size).astype(jnp.int32) for size in SIZES)
    return lax.switch(choice, [lambda size=size: attended(size) for size in (*SIZES, own_blocks)])


def solution(mesh):
    placed = (
        P("corpus", "rerank", None),
        P(),
        P(None, "rerank", None),
        P(),
        P(),
        P(),
        P(),
        P("rerank", None),
        P("rerank", None),
        P("rerank", None),
        P(),
    )
    return jax.shard_map(
        on_device,
        mesh=mesh,
        in_specs=placed,
        out_specs=(P("corpus", "rerank", None), P(("corpus", "rerank"))),
        check_vma=False,
    )
```

```python
import jax
import jax.numpy as jnp
from jax import lax
from jax.experimental import pallas as pl
from jax.experimental.pallas import tpu as pltpu
from jax.sharding import PartitionSpec as P

HDIM = 128
QHEADS = 14
KVHEADS = 2
PER = QHEADS // KVHEADS
QW = QHEADS * HDIM
KW = KVHEADS * HDIM
BLK = 512
QLEN = 64
CAP = 5
SIDE = 4
SIZES = (24, 26)
ROPE_BASE = 1000000.0
EPSILON = 1e-06
SCALE2 = HDIM ** (-0.5) * 1.4426950408889634
VMEM = 56 * 1024 * 1024


def rope_tables(positions):
    half = HDIM // 2
    inverse = jnp.power(ROPE_BASE, -2.0 * jnp.arange(half, dtype=jnp.float32) / HDIM)
    angles = positions.astype(jnp.float32)[:, None] * inverse
    cosine, sine = jnp.cos(angles), jnp.sin(angles)
    return (
        jnp.concatenate([cosine, cosine], axis=1),
        jnp.concatenate([-sine, sine], axis=1),
    )


def spin(part, cosine, sine):
    return part * cosine + pltpu.roll(part, HDIM // 2, part.ndim - 1) * sine


def shift(value, dim, step):
    def moved(index):
        x, y = index // SIDE, index % SIDE
        if dim == "x":
            x = (x + step) % SIDE
        else:
            y = (y + step) % SIDE
        return x * SIDE + y

    return lax.ppermute(value, "rerank", [(i, moved(i)) for i in range(SIDE * SIDE)])


def tie(*values):
    return lax.optimization_barrier(values)


def plane_gather(value_a, value_b, beside):
    a_low, a_high, a_far = (shift(value_a, "y", step) for step in (1, -1, 2))
    b_low, b_high, b_far = (shift(value_b, "x", step) for step in (1, -1, 2))
    a_low, a_high, a_far, b_low, b_high, b_far, beside = tie(
        a_low, a_high, a_far, b_low, b_high, b_far, beside
    )
    a0, a1 = jnp.stack([value_a, a_low]), jnp.stack([a_high, a_far])
    b0, b1 = jnp.stack([value_b, b_low]), jnp.stack([b_high, b_far])
    a0_low, b0_low = shift(a0, "x", 1), shift(b0, "y", 1)
    a1_high, b1_high = shift(a1, "x", -1), shift(b1, "y", -1)
    a1_low, b1_low = shift(a1, "x", 1), shift(b1, "y", 1)
    a0_high, b0_high = shift(a0, "x", -1), shift(b0, "y", -1)
    a0_low, b0_low, a1_high, b1_high = tie(a0_low, b0_low, a1_high, b1_high)
    a0_far, b0_far = shift(a0_low, "x", 1), shift(b0_low, "y", 1)
    a1_far, b1_far = shift(a1_high, "x", -1), shift(b1_high, "y", -1)
    return (
        (a0, a1, a0_low, a1_low, a0_high, a1_high, a0_far, a1_far),
        (b0, b1, b0_low, b1_low, b0_high, b1_high, b0_far, b1_far),
        beside,
    )


PARTS = 8
HOPS = (0, -1, 1, 2)
BACK = (0, 1, 3, 2)


def part_of(parts, swapped, dx, dy):
    outer, inner = (dy, dx) if swapped else (dx, dy)
    return parts[2 * outer + inner // 2], inner % 2


def normed_of(rows, gain):
    wide = rows.astype(jnp.float32)
    inverse = lax.rsqrt(jnp.mean(wide * wide, axis=-1, keepdims=True) + EPSILON)
    return (wide * inverse * gain).astype(jnp.bfloat16)


GROUP = 4


def norm_kernel(order_ref, *refs):
    blocks, (gain_ref, out_ref) = refs[:GROUP], refs[GROUP:]
    tokens = blocks[0].shape[1]
    for number, block in enumerate(blocks):
        out_ref[number * tokens : (number + 1) * tokens] = normed_of(block[0], gain_ref[...])


def norm(order, store, gain):
    blocks, tokens, width = store.shape
    return pl.pallas_call(
        norm_kernel,
        grid_spec=pltpu.PrefetchScalarGridSpec(
            num_scalar_prefetch=1,
            grid=(blocks // GROUP,),
            in_specs=[
                *[
                    pl.BlockSpec(
                        (1, tokens, width), lambda i, order, n=n: (order[GROUP * i + n], 0, 0)
                    )
                    for n in range(GROUP)
                ],
                pl.BlockSpec((1, width), lambda i, order: (0, 0)),
            ],
            out_specs=pl.BlockSpec((GROUP * tokens, width), lambda i, order: (i, 0)),
        ),
        out_shape=jax.ShapeDtypeStruct((blocks * tokens, width), jnp.bfloat16),
        compiler_params=pltpu.CompilerParams(vmem_limit_bytes=VMEM),
        name="norm",
    )(order, *[store] * GROUP, gain)


def key_value_kernel(normed_ref, w_ref, cos_ref, sin_ref, kv_ref):
    rows = normed_ref.shape[0]
    tokens = cos_ref.shape[0]
    raw = jnp.dot(normed_ref[...], w_ref[...], preferred_element_type=jnp.float32)
    for head in range(KVHEADS):
        cols = slice(head * HDIM, (head + 1) * HDIM)
        part = raw[:, cols].reshape(rows // tokens, tokens, HDIM)
        turned = spin(part, cos_ref[...][None], sin_ref[...][None])
        kv_ref[:, cols] = turned.reshape(rows, HDIM).astype(jnp.bfloat16)
    kv_ref[:, KW:] = raw[:, KW:].astype(jnp.bfloat16)


def key_value(normed, w_kv, cosine, sine, rows):
    tile = 128 if rows % 128 == 0 else rows // 2
    width = normed.shape[1]
    table = pl.BlockSpec(cosine.shape, lambda i: (0, 0))
    return pl.pallas_call(
        key_value_kernel,
        grid=(rows // tile,),
        in_specs=[
            pl.BlockSpec((tile, width), lambda i: (i, 0)),
            pl.BlockSpec((width, 2 * KW), lambda i: (0, 0)),
            table,
            table,
        ],
        out_specs=pl.BlockSpec((tile, 2 * KW), lambda i: (i, 0)),
        out_shape=jax.ShapeDtypeStruct((rows, 2 * KW), jnp.bfloat16),
        compiler_params=pltpu.CompilerParams(vmem_limit_bytes=VMEM),
        name="key_value",
    )(normed, w_kv, cosine, sine)


def asked_kernel(x_ref, gain_ref, w_ref, cos_ref, sin_ref, normed_ref, kv_ref):
    normed_ref[...] = normed_of(x_ref[...], gain_ref[...])
    raw = jnp.dot(normed_ref[...], w_ref[...], preferred_element_type=jnp.float32)
    for head in range(KVHEADS):
        cols = slice(head * HDIM, (head + 1) * HDIM)
        kv_ref[:, cols] = spin(raw[:, cols], cos_ref[...], sin_ref[...]).astype(jnp.bfloat16)
    kv_ref[:, KW:] = raw[:, KW:].astype(jnp.bfloat16)


def asked_key_value(rows, gain, w_kv, cosine, sine):
    def whole(shape):
        return pl.BlockSpec(shape, lambda i: (0, 0))

    width = rows.shape[1]
    return pl.pallas_call(
        asked_kernel,
        grid=(1,),
        in_specs=[
            whole(rows.shape),
            whole(gain.shape),
            whole((width, 2 * KW)),
            whole(cosine.shape),
            whole(sine.shape),
        ],
        out_specs=[whole(rows.shape), whole((rows.shape[0], 2 * KW))],
        out_shape=[
            jax.ShapeDtypeStruct(rows.shape, jnp.bfloat16),
            jax.ShapeDtypeStruct((rows.shape[0], 2 * KW), jnp.bfloat16),
        ],
        compiler_params=pltpu.CompilerParams(vmem_limit_bytes=VMEM),
        name="asked_key_value",
    )(rows, gain, w_kv, cosine, sine)


def query_kernel(normed_ref, asked_ref, w_ref, cos_ref, sin_ref, out_ref, last_ref, x_ref, sems):
    rows, chunk = out_ref.shape
    tokens = cos_ref.shape[0]
    extra = asked_ref.shape[0]

    @pl.when(pl.program_id(0) == 0)
    def _():
        copies = (
            pltpu.make_async_copy(
                normed_ref.at[pl.ds(0, rows)], x_ref.at[pl.ds(0, rows)], sems.at[0]
            ),
            pltpu.make_async_copy(asked_ref, x_ref.at[pl.ds(rows, extra)], sems.at[1]),
        )
        for copy in copies:
            copy.start()
        for copy in copies:
            copy.wait()

    raw = jnp.dot(x_ref[...], w_ref[0], preferred_element_type=jnp.float32)
    for head in range(chunk // HDIM):
        cols = slice(head * HDIM, (head + 1) * HDIM)
        part = raw[:rows, cols].reshape(rows // tokens, tokens, HDIM)
        turned = spin(part, cos_ref[...][None], sin_ref[...][None])
        out_ref[:, cols] = turned.reshape(rows, HDIM).astype(jnp.bfloat16)
    last_ref[...] = raw[rows:]


def project_query(strips, normed, asked, cosine, sine, rows):
    width = normed.shape[1]
    chunk = strips.shape[2]
    extra = asked.shape[0]
    table = pl.BlockSpec(cosine.shape, lambda i: (0, 0))
    anywhere = pl.BlockSpec(memory_space=pl.ANY)
    return pl.pallas_call(
        query_kernel,
        grid=(QW // chunk,),
        in_specs=[
            anywhere,
            anywhere,
            pl.BlockSpec((1, width, chunk), lambda i: (i, 0, 0)),
            table,
            table,
        ],
        out_specs=[
            pl.BlockSpec((rows, chunk), lambda i: (0, i)),
            pl.BlockSpec((extra, chunk), lambda i: (0, i)),
        ],
        out_shape=[
            jax.ShapeDtypeStruct((rows, QW), jnp.bfloat16),
            jax.ShapeDtypeStruct((extra, QW), jnp.float32),
        ],
        scratch_shapes=[
            pltpu.VMEM((rows + extra, width), jnp.bfloat16),
            pltpu.SemaphoreType.DMA((2,)),
        ],
        compiler_params=pltpu.CompilerParams(vmem_limit_bytes=VMEM),
        name="project_query",
    )(normed, asked, strips, cosine, sine)


def attend_kernel(
    slot_ref, length_ref, where_ref, q_ref, *rest, swapped, start, absent
):
    parts, kpos_ref = rest[:PARTS], rest[PARTS]
    out_ref, held, zeros, listed, sems = rest[-5:]
    blocks, tokens, _ = q_ref.shape
    slots = slot_ref.shape[0]
    base = where_ref[0]
    row, wanted = where_ref[1], where_ref[2]
    rows = PER * tokens
    zeros[...] = jnp.zeros_like(zeros)

    def attend_block(block, groups):
        length = length_ref[start + block]
        kpos = kpos_ref[0:1, : groups * SIDE * tokens]
        qpos = base + lax.rem(lax.broadcasted_iota(jnp.int32, (rows, 1), 0), tokens)
        allowed = (kpos <= qpos) & (kpos < length)
        kept = (base + lax.broadcasted_iota(jnp.int32, (tokens, 1), 0)) < length

        def side_by_side(first):
            picked = []
            for dx in BACK[:groups]:
                for dy in range(SIDE):
                    ref, index = part_of(parts, swapped, dx, dy)
                    picked.append(ref[index, block, :, first : first + HDIM])
            return jnp.concatenate(picked, axis=0)

        for g in range(KVHEADS):
            heads = range(g * PER, (g + 1) * PER)
            queries = jnp.concatenate(
                [q_ref[block, :, h * HDIM : (h + 1) * HDIM] for h in heads], axis=0
            )
            logits = lax.dot_general(
                queries,
                side_by_side(g * HDIM),
                (((1,), (1,)), ((), ())),
                preferred_element_type=jnp.float32,
            )
            logits = jnp.where(allowed, logits * SCALE2, -1e30)
            weights = jnp.exp2(logits - jnp.max(logits, axis=-1, keepdims=True))
            total = jnp.sum(weights, axis=-1, keepdims=True)
            mixed = jnp.dot(
                weights.astype(jnp.bfloat16),
                side_by_side(KW + g * HDIM),
                preferred_element_type=jnp.float32,
            ) / total
            for h in heads:
                at = (h - g * PER) * tokens
                held[block, :, h * HDIM : (h + 1) * HDIM] = jnp.where(
                    kept, mixed[at : at + tokens], 0.0
                ).astype(jnp.bfloat16)

    def enlist(block, count):
        listed[count] = block
        alive = (start + block < wanted) & (base < length_ref[start + block])
        return count + alive.astype(jnp.int32)

    count = lax.fori_loop(0, blocks, enlist, jnp.int32(0))

    def each_block(groups):
        def body(pair, carry):
            attend_block(listed[2 * pair], groups)
            attend_block(listed[jnp.minimum(2 * pair + 1, count - 1)], groups)
            return carry

        lax.fori_loop(0, lax.div(count + 1, 2), body, 0)

    for x in range(SIDE):

        @pl.when(row == x)
        def _(x=x):
            each_block(x + 1)

    def copies(slot, act):
        block = slot_ref[slot]
        here = (block >= start) & (block < start + blocks)
        local = jnp.clip(block - start, 0, blocks - 1)
        filled = here & (base < length_ref[start + local])
        empty = here & jnp.logical_not(base < length_ref[start + local])
        if absent:
            empty = empty | (block < 0)

        @pl.when(filled)
        def _():
            act(pltpu.make_async_copy(held.at[local], out_ref.at[slot], sems.at[slot]))

        @pl.when(empty)
        def _():
            act(pltpu.make_async_copy(zeros, out_ref.at[slot], sems.at[slot]))

    def send(slot, carry):
        copies(slot, lambda copy: copy.start())
        return carry

    def finish(slot, carry):
        copies(slot, lambda copy: copy.wait())
        return carry

    lax.fori_loop(0, slots, send, 0)
    lax.fori_loop(0, slots, finish, 0)


def attend(slot_block, lengths, where, queries, parts, kpos, swapped, start, earlier):
    blocks, tokens = parts[0].shape[1:3]
    width = QW
    slots = slot_block.shape[0]
    anywhere = pl.BlockSpec(memory_space=pl.ANY)

    def whole(array):
        return pl.BlockSpec(array.shape, lambda i, *_: (0,) * array.ndim)

    given = () if earlier is None else (earlier,)
    return pl.pallas_call(
        lambda *refs: attend_kernel(
            *refs, swapped=swapped, start=start, absent=earlier is None
        ),
        grid_spec=pltpu.PrefetchScalarGridSpec(
            num_scalar_prefetch=3,
            grid=(1,),
            in_specs=[
                pl.BlockSpec((blocks, tokens, width), lambda i, *_: (start // blocks, 0, 0)),
                *[whole(part) for part in parts],
                whole(kpos),
                *[anywhere for _ in given],
            ],
            out_specs=anywhere,
            scratch_shapes=[
                pltpu.VMEM((blocks, tokens, width), jnp.bfloat16),
                pltpu.VMEM((tokens, width), jnp.bfloat16),
                pltpu.SMEM((blocks + 1,), jnp.int32),
                pltpu.SemaphoreType.DMA((slots,)),
            ],
        ),
        out_shape=jax.ShapeDtypeStruct((slots, tokens, width), jnp.bfloat16),
        input_output_aliases={5 + PARTS: 0} if given else {},
        compiler_params=pltpu.CompilerParams(vmem_limit_bytes=VMEM),
        name="attend_second" if given else "attend_first",
    )(slot_block, lengths, where, queries, *parts, kpos, *given)


def score_kernel(count_ref, block_ref, length_ref, which_ref, size_ref, last_ref, *rest):
    parts_a, parts_b, rest = rest[:PARTS], rest[PARTS : 2 * PARTS], rest[2 * PARTS :]
    qkv_ref, kpos_ref, cos_ref, sin_ref, w_ref, out_ref, kv_ref, sems = rest
    half, q_span = size_ref[0], size_ref[1]
    count = count_ref[0]

    def fetch(step, act):
        slot = lax.rem(step, 2)
        block = block_ref[step]
        for which, parts in enumerate((parts_a, parts_b)):

            @pl.when((block >= half) if which else (block < half))
            def _(which=which, parts=parts):
                local = jnp.clip(block - which * half, 0, parts[0].shape[1] - 1)
                for number, part in enumerate(parts):
                    held = kv_ref.at[slot, pl.ds(2 * number, 2)]
                    act(pltpu.make_async_copy(part.at[:, local], held, sems.at[slot, number]))

    @pl.when(count > 0)
    def _():
        fetch(0, lambda copy: copy.start())

    def body(step, carry):
        @pl.when(step + 1 < count)
        def _():
            fetch(step + 1, lambda copy: copy.start())

        fetch(step, lambda copy: copy.wait())
        slot = lax.rem(step, 2)
        length = length_ref[step]
        which = which_ref[step]
        second = (block_ref[step] >= half).astype(jnp.int32)
        kpos = kpos_ref[pl.ds(second, 1), :]
        live = kpos < length
        span = qkv_ref.shape[0]
        lane = lax.broadcasted_iota(jnp.int32, (1, span), 1)
        own = lax.div(lane, q_span) == which
        at_far = pl.ds(length + QLEN - 1, 1)
        far_cos, far_sin = cos_ref[at_far, :], sin_ref[at_far, :]
        near_cos, near_sin = cos_ref[QLEN - 1 : QLEN, :], sin_ref[QLEN - 1 : QLEN, :]
        total_score = jnp.zeros((1, HDIM), jnp.float32)
        over = (((1,), (1,)), ((), ()))
        for g in range(KVHEADS):
            raw = last_ref[which, g]
            far = spin(raw, far_cos, far_sin).astype(jnp.bfloat16)
            near = spin(raw, near_cos, near_sin).astype(jnp.bfloat16)
            keys = kv_ref[slot, :, :, g * HDIM : (g + 1) * HDIM].reshape(BLK, HDIM)
            values = kv_ref[slot, :, :, KW + g * HDIM : KW + (g + 1) * HDIM].reshape(BLK, HDIM)
            passage = lax.dot_general(far, keys, over, preferred_element_type=jnp.float32)
            question = lax.dot_general(
                near,
                qkv_ref[:, g * HDIM : (g + 1) * HDIM],
                over,
                preferred_element_type=jnp.float32,
            )
            passage = jnp.where(live, passage * SCALE2, -1e30)
            question = jnp.where(own, question * SCALE2, -1e30)
            peak = jnp.maximum(
                jnp.max(passage, axis=-1, keepdims=True), jnp.max(question, axis=-1, keepdims=True)
            )
            passage = jnp.exp2(passage - peak)
            question = jnp.exp2(question - peak)
            total = jnp.sum(passage, axis=-1, keepdims=True) + jnp.sum(
                question, axis=-1, keepdims=True
            )
            mixed = jnp.dot(
                passage.astype(jnp.bfloat16), values, preferred_element_type=jnp.float32
            ) + jnp.dot(
                question.astype(jnp.bfloat16),
                qkv_ref[:, KW + g * HDIM : KW + (g + 1) * HDIM],
                preferred_element_type=jnp.float32,
            )
            context = (mixed / total).astype(jnp.bfloat16).astype(jnp.float32)
            total_score += jnp.sum(context * w_ref[g], axis=0, keepdims=True)
        result = jnp.sum(total_score, axis=-1, keepdims=True)
        out_ref[pl.ds(step, 1), :] = jnp.broadcast_to(result, (1, HDIM))
        return carry

    lax.fori_loop(0, count, body, 0)


def score(
    count, blocks, lengths, which, last, first, second, question_kv, kpos, cosine, sine, w
):
    slots = blocks.shape[0]
    anywhere = pl.BlockSpec(memory_space=pl.ANY)
    tokens = first[0].shape[2]

    def whole(array):
        return pl.BlockSpec(array.shape, lambda i, *_: (0,) * array.ndim)

    return pl.pallas_call(
        score_kernel,
        grid_spec=pltpu.PrefetchScalarGridSpec(
            num_scalar_prefetch=5,
            grid=(1,),
            in_specs=[
                whole(last),
                *[anywhere] * (2 * PARTS),
                whole(question_kv),
                whole(kpos),
                whole(cosine),
                whole(sine),
                whole(w),
            ],
            out_specs=pl.BlockSpec((slots, HDIM), lambda i, *_: (0, 0)),
            scratch_shapes=[
                pltpu.VMEM((2, SIDE * SIDE, tokens, 2 * KW), jnp.bfloat16),
                pltpu.SemaphoreType.DMA((2, PARTS)),
            ],
        ),
        out_shape=jax.ShapeDtypeStruct((slots, HDIM), jnp.float32),
        compiler_params=pltpu.CompilerParams(vmem_limit_bytes=VMEM),
        name="score",
    )(
        count,
        blocks,
        lengths,
        which,
        jnp.array([first[0].shape[1], QLEN], jnp.int32),
        last,
        *first,
        *second,
        question_kv,
        kpos,
        cosine,
        sine,
        w,
    )


def sorted_by(key):
    count = key.shape[0]
    place = jnp.arange(count, dtype=jnp.int32)
    ahead = (key[None, :] < key[:, None]) | (
        (key[None, :] == key[:, None]) & (place[None, :] < place[:, None])
    )
    rank = jnp.sum(ahead.astype(jnp.int32), axis=1)
    chosen = rank[None, :] == place[:, None]

    def arrange(values):
        return jnp.sum(jnp.where(chosen, values[None, :], 0), axis=1).astype(jnp.int32)

    return arrange, rank


def on_device(
    store_rows,
    block_lengths,
    queries,
    cand_owner,
    cand_block,
    cand_query,
    norm_gain,
    w_query,
    w_key,
    w_value,
    w_score,
):
    n_corpus = lax.axis_size("corpus")
    n_rerank = lax.axis_size("rerank")
    corpus_index = lax.axis_index("corpus")
    member = lax.axis_index("rerank")
    pair_total = cand_block.shape[0]
    pair_group = pair_total // n_corpus
    own_blocks, tokens, width = store_rows.shape
    n_query, q_tokens, _ = queries.shape
    q_dev = n_query // n_rerank

    owners = cand_owner[:, 0]
    pair_order = jnp.arange(pair_total, dtype=jnp.int32)
    group_of = pair_order // pair_group
    earlier = (
        (owners[:, None] == owners[None, :])
        & (group_of[:, None] == group_of[None, :])
        & (pair_order[None, :] < pair_order[:, None])
    )
    owner_rank = jnp.sum(earlier.astype(jnp.int32), axis=1)
    slot_ids = jnp.arange(n_corpus * CAP, dtype=jnp.int32)
    wanted = (
        (group_of[None, :] == (slot_ids // CAP)[:, None])
        & (owners[None, :] == corpus_index)
        & (owner_rank[None, :] == (slot_ids % CAP)[:, None])
    )
    present = jnp.any(wanted, axis=1)

    def of_slot(values):
        return jnp.sum(jnp.where(wanted, values[None, :], 0), axis=1)

    slot_query, slot_pair, stored_block = of_slot(cand_query), of_slot(pair_order), of_slot(cand_block)
    block_ids = jnp.arange(own_blocks, dtype=jnp.int32)
    owner_ids = jnp.arange(n_corpus, dtype=jnp.int32)
    named = jnp.any(
        (owners[None, None, :] == owner_ids[:, None, None])
        & (cand_block[None, None, :] == block_ids[None, :, None]),
        axis=2,
    )
    most = jnp.max(jnp.sum(named.astype(jnp.int32), axis=1))
    want = jnp.any(named & (owner_ids[:, None] == corpus_index), axis=0)
    want_count = jnp.sum(want.astype(jnp.int32))
    by_want, want_rank = sorted_by(jnp.where(want, 0, 1))
    block_order = by_want(block_ids)
    own_lengths = by_want(
        lax.dynamic_slice_in_dim(block_lengths, corpus_index * own_blocks, own_blocks, 0)
    )
    is_block = stored_block[:, None] == block_ids[None, :]
    slot_block = jnp.sum(jnp.where(is_block, want_rank[None, :], 0), axis=1)
    slot_length = jnp.sum(
        jnp.where(slot_block[:, None] == block_ids[None, :], own_lengths[None, :], 0), axis=1
    )
    slot_or_none = jnp.where(present, slot_block, -1)
    mine = present & (slot_query // q_dev == member)
    by_mine, _ = sorted_by(jnp.where(mine, slot_block, own_blocks))
    mine_count = jnp.sum(mine.astype(jnp.int32)).reshape(1)
    mine_block, mine_length = by_mine(slot_block), by_mine(slot_length)
    mine_which, mine_pair = by_mine(slot_query % q_dev), by_mine(slot_pair)

    all_cos, all_sin = rope_tables(jnp.arange(BLK + QLEN, dtype=jnp.int32))
    base = member * tokens
    own_cos, own_sin = rope_tables(base + jnp.arange(tokens, dtype=jnp.int32))
    x, y = member // SIDE, member % SIDE
    hops = jnp.array(HOPS, jnp.int32)
    xs, ys = (x + hops) % SIDE, (y + hops) % SIDE

    strip = QW // (n_corpus - 1)
    my_columns = lax.dynamic_slice_in_dim(
        w_query, jnp.minimum(corpus_index, n_corpus - 2) * strip, strip, 1
    )
    w_first = lax.all_gather(
        jnp.concatenate([w_key, w_value, my_columns], axis=1), "rerank", axis=0, tiled=True
    )
    gain = norm_gain.astype(jnp.float32).reshape(1, width)
    normed = norm(block_order, store_rows, gain)

    asked = lax.all_to_all(queries, "rerank", 0, 1, tiled=True).reshape(q_dev * QLEN, width)
    asked_token = jnp.arange(asked.shape[0], dtype=jnp.int32) % QLEN
    asked_cos, asked_sin = rope_tables(asked_token)


    inside = jnp.arange(tokens, dtype=jnp.int32)

    def positions_of(ranks):
        return (ranks[..., None] * tokens + inside).reshape(1, BLK)

    xb = (x - jnp.arange(SIDE, dtype=jnp.int32)) % SIDE
    kpos = positions_of(xb[:, None] * SIDE + ys[None, :])
    part_pos = jnp.concatenate(
        [
            positions_of(xs[:, None] * SIDE + ys[None, :]),
            positions_of(xs[None, :] * SIDE + ys[:, None]),
        ]
    )

    head_w = jnp.pad(
        w_score.astype(jnp.float32).reshape(KVHEADS, PER, HDIM), ((0, 0), (0, 8 - PER), (0, 0))
    )
    where = jnp.stack([base, x, want_count]).astype(jnp.int32)
    belongs = (slot_ids < mine_count[0])[:, None] & (mine_pair[:, None] == pair_order[None, :])
    pair_dev = pair_group // n_rerank

    def attended(blocks):
        half = blocks // 2
        strips = lax.all_gather(w_first[:, 2 * KW :], "corpus", axis=0, tiled=False)
        kv = key_value(normed, w_first, own_cos, own_sin, blocks * tokens)
        passage_kv = kv.reshape(blocks, tokens, 2 * KW)
        asked_normed, question_kv = asked_key_value(asked, gain, w_first, asked_cos, asked_sin)
        asked_last = jnp.pad(asked_normed[QLEN - 1 :: QLEN], ((0, 16 - q_dev), (0, 0)))
        first, second, (asked_last, question_kv) = plane_gather(
            passage_kv[:half], passage_kv[half:], (asked_last, question_kv)
        )
        query_rot, query_last = project_query(
            strips, normed, asked_last, own_cos, own_sin, blocks * tokens
        )
        last = query_last[:q_dev].reshape(q_dev, KVHEADS, PER, HDIM)
        last = jnp.pad(last, ((0, 0), (0, 0), (0, 8 - PER), (0, 0)))
        scored = score(
            mine_count,
            mine_block,
            mine_length,
            mine_which,
            last,
            first,
            second,
            question_kv,
            part_pos,
            all_cos,
            all_sin,
            head_w,
        )[: n_corpus * CAP, 0]
        placed = jnp.sum(jnp.where(belongs, scored[:, None], 0.0), axis=0)
        query_rot = query_rot.reshape(blocks, tokens, QW)
        gathered = lax.all_to_all(
            placed.reshape(n_corpus * n_rerank, pair_dev), ("corpus", "rerank"), 0, 0, tiled=True
        )
        pair_scores = jnp.sum(gathered, axis=0)
        begun = attend(
            slot_or_none, own_lengths, where, query_rot, first, kpos, False, 0, None
        )
        passage_context = attend(
            slot_or_none, own_lengths, where, query_rot, second, kpos, True, half, begun
        )
        return passage_context, pair_scores

    choice = sum((most > size).astype(jnp.int32) for size in SIZES)
    return lax.switch(choice, [lambda size=size: attended(size) for size in (*SIZES, own_blocks)])


def solution(mesh):
    placed = (
        P("corpus", "rerank", None),
        P(),
        P(None, "rerank", None),
        P(),
        P(),
        P(),
        P(),
        P("rerank", None),
        P("rerank", None),
        P("rerank", None),
        P(),
    )
    return jax.shard_map(
        on_device,
        mesh=mesh,
        in_specs=placed,
        out_specs=(P("corpus", "rerank", None), P(("corpus", "rerank"))),
        check_vma=False,
    )
```

```python
import jax
import jax.numpy as jnp
from jax import lax
from jax.experimental import pallas as pl
from jax.experimental.pallas import tpu as pltpu
from jax.sharding import PartitionSpec as P

HDIM = 128
QHEADS = 14
KVHEADS = 2
PER = QHEADS // KVHEADS
QW = QHEADS * HDIM
KW = KVHEADS * HDIM
BLK = 512
QLEN = 64
CAP = 5
SIDE = 4
SIZES = (24, 28)
ROPE_BASE = 1000000.0
EPSILON = 1e-06
SCALE2 = HDIM ** (-0.5) * 1.4426950408889634
VMEM = 56 * 1024 * 1024


def rope_tables(positions):
    half = HDIM // 2
    inverse = jnp.power(ROPE_BASE, -2.0 * jnp.arange(half, dtype=jnp.float32) / HDIM)
    angles = positions.astype(jnp.float32)[:, None] * inverse
    cosine, sine = jnp.cos(angles), jnp.sin(angles)
    return (
        jnp.concatenate([cosine, cosine], axis=1),
        jnp.concatenate([-sine, sine], axis=1),
    )


def spin(part, cosine, sine):
    return part * cosine + pltpu.roll(part, HDIM // 2, part.ndim - 1) * sine


def shift(value, dim, step):
    def moved(index):
        x, y = index // SIDE, index % SIDE
        if dim == "x":
            x = (x + step) % SIDE
        else:
            y = (y + step) % SIDE
        return x * SIDE + y

    return lax.ppermute(value, "rerank", [(i, moved(i)) for i in range(SIDE * SIDE)])


def tie(*values):
    return lax.optimization_barrier(values)


def plane_gather(value_a, value_b, beside):
    a_low, a_high, a_far = (shift(value_a, "y", step) for step in (1, -1, 2))
    b_low, b_high, b_far = (shift(value_b, "x", step) for step in (1, -1, 2))
    a_low, a_high, a_far, b_low, b_high, b_far, beside = tie(
        a_low, a_high, a_far, b_low, b_high, b_far, beside
    )
    a0, a1 = jnp.stack([value_a, a_low]), jnp.stack([a_high, a_far])
    b0, b1 = jnp.stack([value_b, b_low]), jnp.stack([b_high, b_far])
    a0_low, b0_low = shift(a0, "x", 1), shift(b0, "y", 1)
    a1_high, b1_high = shift(a1, "x", -1), shift(b1, "y", -1)
    a1_low, b1_low = shift(a1, "x", 1), shift(b1, "y", 1)
    a0_high, b0_high = shift(a0, "x", -1), shift(b0, "y", -1)
    a0_low, b0_low, a1_high, b1_high = tie(a0_low, b0_low, a1_high, b1_high)
    a0_far, b0_far = shift(a0_low, "x", 1), shift(b0_low, "y", 1)
    a1_far, b1_far = shift(a1_high, "x", -1), shift(b1_high, "y", -1)
    return (
        (a0, a1, a0_low, a1_low, a0_high, a1_high, a0_far, a1_far),
        (b0, b1, b0_low, b1_low, b0_high, b1_high, b0_far, b1_far),
        beside,
    )


PARTS = 8
HOPS = (0, -1, 1, 2)
BACK = (0, 1, 3, 2)


def part_of(parts, swapped, dx, dy):
    outer, inner = (dy, dx) if swapped else (dx, dy)
    return parts[2 * outer + inner // 2], inner % 2


def normed_of(rows, gain):
    wide = rows.astype(jnp.float32)
    inverse = lax.rsqrt(jnp.mean(wide * wide, axis=-1, keepdims=True) + EPSILON)
    return (wide * inverse * gain).astype(jnp.bfloat16)


GROUP = 4


def norm_kernel(order_ref, *refs):
    blocks, (gain_ref, out_ref) = refs[:GROUP], refs[GROUP:]
    tokens = blocks[0].shape[1]
    for number, block in enumerate(blocks):
        out_ref[number * tokens : (number + 1) * tokens] = normed_of(block[0], gain_ref[...])


def norm(order, store, gain):
    blocks, tokens, width = store.shape
    return pl.pallas_call(
        norm_kernel,
        grid_spec=pltpu.PrefetchScalarGridSpec(
            num_scalar_prefetch=1,
            grid=(blocks // GROUP,),
            in_specs=[
                *[
                    pl.BlockSpec(
                        (1, tokens, width), lambda i, order, n=n: (order[GROUP * i + n], 0, 0)
                    )
                    for n in range(GROUP)
                ],
                pl.BlockSpec((1, width), lambda i, order: (0, 0)),
            ],
            out_specs=pl.BlockSpec((GROUP * tokens, width), lambda i, order: (i, 0)),
        ),
        out_shape=jax.ShapeDtypeStruct((blocks * tokens, width), jnp.bfloat16),
        compiler_params=pltpu.CompilerParams(vmem_limit_bytes=VMEM),
        name="norm",
    )(order, *[store] * GROUP, gain)


def key_value_kernel(normed_ref, w_ref, cos_ref, sin_ref, kv_ref):
    rows = normed_ref.shape[0]
    tokens = cos_ref.shape[0]
    raw = jnp.dot(normed_ref[...], w_ref[...], preferred_element_type=jnp.float32)
    for head in range(KVHEADS):
        cols = slice(head * HDIM, (head + 1) * HDIM)
        part = raw[:, cols].reshape(rows // tokens, tokens, HDIM)
        turned = spin(part, cos_ref[...][None], sin_ref[...][None])
        kv_ref[:, cols] = turned.reshape(rows, HDIM).astype(jnp.bfloat16)
    kv_ref[:, KW:] = raw[:, KW:].astype(jnp.bfloat16)


def key_value(normed, w_kv, cosine, sine, rows):
    tile = 128 if rows % 128 == 0 else rows // 2
    width = normed.shape[1]
    table = pl.BlockSpec(cosine.shape, lambda i: (0, 0))
    return pl.pallas_call(
        key_value_kernel,
        grid=(rows // tile,),
        in_specs=[
            pl.BlockSpec((tile, width), lambda i: (i, 0)),
            pl.BlockSpec((width, 2 * KW), lambda i: (0, 0)),
            table,
            table,
        ],
        out_specs=pl.BlockSpec((tile, 2 * KW), lambda i: (i, 0)),
        out_shape=jax.ShapeDtypeStruct((rows, 2 * KW), jnp.bfloat16),
        compiler_params=pltpu.CompilerParams(vmem_limit_bytes=VMEM),
        name="key_value",
    )(normed, w_kv, cosine, sine)


def asked_kernel(x_ref, gain_ref, w_ref, cos_ref, sin_ref, normed_ref, kv_ref):
    normed_ref[...] = normed_of(x_ref[...], gain_ref[...])
    raw = jnp.dot(normed_ref[...], w_ref[...], preferred_element_type=jnp.float32)
    for head in range(KVHEADS):
        cols = slice(head * HDIM, (head + 1) * HDIM)
        kv_ref[:, cols] = spin(raw[:, cols], cos_ref[...], sin_ref[...]).astype(jnp.bfloat16)
    kv_ref[:, KW:] = raw[:, KW:].astype(jnp.bfloat16)


def asked_key_value(rows, gain, w_kv, cosine, sine):
    def whole(shape):
        return pl.BlockSpec(shape, lambda i: (0, 0))

    width = rows.shape[1]
    return pl.pallas_call(
        asked_kernel,
        grid=(1,),
        in_specs=[
            whole(rows.shape),
            whole(gain.shape),
            whole((width, 2 * KW)),
            whole(cosine.shape),
            whole(sine.shape),
        ],
        out_specs=[whole(rows.shape), whole((rows.shape[0], 2 * KW))],
        out_shape=[
            jax.ShapeDtypeStruct(rows.shape, jnp.bfloat16),
            jax.ShapeDtypeStruct((rows.shape[0], 2 * KW), jnp.bfloat16),
        ],
        compiler_params=pltpu.CompilerParams(vmem_limit_bytes=VMEM),
        name="asked_key_value",
    )(rows, gain, w_kv, cosine, sine)


def query_kernel(normed_ref, asked_ref, w_ref, cos_ref, sin_ref, out_ref, last_ref, x_ref, sems):
    rows, chunk = out_ref.shape
    tokens = cos_ref.shape[0]
    extra = asked_ref.shape[0]

    @pl.when(pl.program_id(0) == 0)
    def _():
        copies = (
            pltpu.make_async_copy(
                normed_ref.at[pl.ds(0, rows)], x_ref.at[pl.ds(0, rows)], sems.at[0]
            ),
            pltpu.make_async_copy(asked_ref, x_ref.at[pl.ds(rows, extra)], sems.at[1]),
        )
        for copy in copies:
            copy.start()
        for copy in copies:
            copy.wait()

    raw = jnp.dot(x_ref[...], w_ref[0], preferred_element_type=jnp.float32)
    for head in range(chunk // HDIM):
        cols = slice(head * HDIM, (head + 1) * HDIM)
        part = raw[:rows, cols].reshape(rows // tokens, tokens, HDIM)
        turned = spin(part, cos_ref[...][None], sin_ref[...][None])
        out_ref[:, cols] = turned.reshape(rows, HDIM).astype(jnp.bfloat16)
    last_ref[...] = raw[rows:]


def project_query(strips, normed, asked, cosine, sine, rows):
    width = normed.shape[1]
    chunk = strips.shape[2]
    extra = asked.shape[0]
    table = pl.BlockSpec(cosine.shape, lambda i: (0, 0))
    anywhere = pl.BlockSpec(memory_space=pl.ANY)
    return pl.pallas_call(
        query_kernel,
        grid=(QW // chunk,),
        in_specs=[
            anywhere,
            anywhere,
            pl.BlockSpec((1, width, chunk), lambda i: (i, 0, 0)),
            table,
            table,
        ],
        out_specs=[
            pl.BlockSpec((rows, chunk), lambda i: (0, i)),
            pl.BlockSpec((extra, chunk), lambda i: (0, i)),
        ],
        out_shape=[
            jax.ShapeDtypeStruct((rows, QW), jnp.bfloat16),
            jax.ShapeDtypeStruct((extra, QW), jnp.float32),
        ],
        scratch_shapes=[
            pltpu.VMEM((rows + extra, width), jnp.bfloat16),
            pltpu.SemaphoreType.DMA((2,)),
        ],
        compiler_params=pltpu.CompilerParams(vmem_limit_bytes=VMEM),
        name="project_query",
    )(normed, asked, strips, cosine, sine)


def attend_kernel(
    slot_ref, length_ref, where_ref, q_ref, *rest, swapped, start, absent
):
    parts, kpos_ref = rest[:PARTS], rest[PARTS]
    out_ref, held, zeros, listed, sems = rest[-5:]
    blocks, tokens, _ = q_ref.shape
    slots = slot_ref.shape[0]
    base = where_ref[0]
    row, wanted = where_ref[1], where_ref[2]
    rows = PER * tokens
    zeros[...] = jnp.zeros_like(zeros)

    def attend_block(block, groups):
        length = length_ref[start + block]
        kpos = kpos_ref[0:1, : groups * SIDE * tokens]
        qpos = base + lax.rem(lax.broadcasted_iota(jnp.int32, (rows, 1), 0), tokens)
        allowed = (kpos <= qpos) & (kpos < length)
        kept = (base + lax.broadcasted_iota(jnp.int32, (tokens, 1), 0)) < length

        def side_by_side(first):
            picked = []
            for dx in BACK[:groups]:
                for dy in range(SIDE):
                    ref, index = part_of(parts, swapped, dx, dy)
                    picked.append(ref[index, block, :, first : first + HDIM])
            return jnp.concatenate(picked, axis=0)

        for g in range(KVHEADS):
            heads = range(g * PER, (g + 1) * PER)
            queries = jnp.concatenate(
                [q_ref[block, :, h * HDIM : (h + 1) * HDIM] for h in heads], axis=0
            )
            logits = lax.dot_general(
                queries,
                side_by_side(g * HDIM),
                (((1,), (1,)), ((), ())),
                preferred_element_type=jnp.float32,
            )
            logits = jnp.where(allowed, logits * SCALE2, -1e30)
            weights = jnp.exp2(logits - jnp.max(logits, axis=-1, keepdims=True))
            total = jnp.sum(weights, axis=-1, keepdims=True)
            mixed = jnp.dot(
                weights.astype(jnp.bfloat16),
                side_by_side(KW + g * HDIM),
                preferred_element_type=jnp.float32,
            ) / total
            for h in heads:
                at = (h - g * PER) * tokens
                held[block, :, h * HDIM : (h + 1) * HDIM] = jnp.where(
                    kept, mixed[at : at + tokens], 0.0
                ).astype(jnp.bfloat16)

    def enlist(block, count):
        listed[count] = block
        alive = (start + block < wanted) & (base < length_ref[start + block])
        return count + alive.astype(jnp.int32)

    count = lax.fori_loop(0, blocks, enlist, jnp.int32(0))

    def each_block(groups):
        def body(pair, carry):
            attend_block(listed[2 * pair], groups)
            attend_block(listed[jnp.minimum(2 * pair + 1, count - 1)], groups)
            return carry

        lax.fori_loop(0, lax.div(count + 1, 2), body, 0)

    for x in range(SIDE):

        @pl.when(row == x)
        def _(x=x):
            each_block(x + 1)

    def copies(slot, act):
        block = slot_ref[slot]
        here = (block >= start) & (block < start + blocks)
        local = jnp.clip(block - start, 0, blocks - 1)
        filled = here & (base < length_ref[start + local])
        empty = here & jnp.logical_not(base < length_ref[start + local])
        if absent:
            empty = empty | (block < 0)

        @pl.when(filled)
        def _():
            act(pltpu.make_async_copy(held.at[local], out_ref.at[slot], sems.at[slot]))

        @pl.when(empty)
        def _():
            act(pltpu.make_async_copy(zeros, out_ref.at[slot], sems.at[slot]))

    def send(slot, carry):
        copies(slot, lambda copy: copy.start())
        return carry

    def finish(slot, carry):
        copies(slot, lambda copy: copy.wait())
        return carry

    lax.fori_loop(0, slots, send, 0)
    lax.fori_loop(0, slots, finish, 0)


def attend(slot_block, lengths, where, queries, parts, kpos, swapped, start, earlier):
    blocks, tokens = parts[0].shape[1:3]
    width = QW
    slots = slot_block.shape[0]
    anywhere = pl.BlockSpec(memory_space=pl.ANY)

    def whole(array):
        return pl.BlockSpec(array.shape, lambda i, *_: (0,) * array.ndim)

    given = () if earlier is None else (earlier,)
    return pl.pallas_call(
        lambda *refs: attend_kernel(
            *refs, swapped=swapped, start=start, absent=earlier is None
        ),
        grid_spec=pltpu.PrefetchScalarGridSpec(
            num_scalar_prefetch=3,
            grid=(1,),
            in_specs=[
                pl.BlockSpec((blocks, tokens, width), lambda i, *_: (start // blocks, 0, 0)),
                *[whole(part) for part in parts],
                whole(kpos),
                *[anywhere for _ in given],
            ],
            out_specs=anywhere,
            scratch_shapes=[
                pltpu.VMEM((blocks, tokens, width), jnp.bfloat16),
                pltpu.VMEM((tokens, width), jnp.bfloat16),
                pltpu.SMEM((blocks + 1,), jnp.int32),
                pltpu.SemaphoreType.DMA((slots,)),
            ],
        ),
        out_shape=jax.ShapeDtypeStruct((slots, tokens, width), jnp.bfloat16),
        input_output_aliases={5 + PARTS: 0} if given else {},
        compiler_params=pltpu.CompilerParams(vmem_limit_bytes=VMEM),
        name="attend_second" if given else "attend_first",
    )(slot_block, lengths, where, queries, *parts, kpos, *given)


def score_kernel(count_ref, block_ref, length_ref, which_ref, size_ref, last_ref, *rest):
    parts_a, parts_b, rest = rest[:PARTS], rest[PARTS : 2 * PARTS], rest[2 * PARTS :]
    qkv_ref, kpos_ref, cos_ref, sin_ref, w_ref, out_ref, kv_ref, sems = rest
    half, q_span = size_ref[0], size_ref[1]
    count = count_ref[0]

    def fetch(step, act):
        slot = lax.rem(step, 2)
        block = block_ref[step]
        for which, parts in enumerate((parts_a, parts_b)):

            @pl.when((block >= half) if which else (block < half))
            def _(which=which, parts=parts):
                local = jnp.clip(block - which * half, 0, parts[0].shape[1] - 1)
                for number, part in enumerate(parts):
                    held = kv_ref.at[slot, pl.ds(2 * number, 2)]
                    act(pltpu.make_async_copy(part.at[:, local], held, sems.at[slot, number]))

    @pl.when(count > 0)
    def _():
        fetch(0, lambda copy: copy.start())

    def body(step, carry):
        @pl.when(step + 1 < count)
        def _():
            fetch(step + 1, lambda copy: copy.start())

        fetch(step, lambda copy: copy.wait())
        slot = lax.rem(step, 2)
        length = length_ref[step]
        which = which_ref[step]
        second = (block_ref[step] >= half).astype(jnp.int32)
        kpos = kpos_ref[pl.ds(second, 1), :]
        live = kpos < length
        span = qkv_ref.shape[0]
        lane = lax.broadcasted_iota(jnp.int32, (1, span), 1)
        own = lax.div(lane, q_span) == which
        at_far = pl.ds(length + QLEN - 1, 1)
        far_cos, far_sin = cos_ref[at_far, :], sin_ref[at_far, :]
        near_cos, near_sin = cos_ref[QLEN - 1 : QLEN, :], sin_ref[QLEN - 1 : QLEN, :]
        total_score = jnp.zeros((1, HDIM), jnp.float32)
        over = (((1,), (1,)), ((), ()))
        for g in range(KVHEADS):
            raw = last_ref[which, g]
            far = spin(raw, far_cos, far_sin).astype(jnp.bfloat16)
            near = spin(raw, near_cos, near_sin).astype(jnp.bfloat16)
            keys = kv_ref[slot, :, :, g * HDIM : (g + 1) * HDIM].reshape(BLK, HDIM)
            values = kv_ref[slot, :, :, KW + g * HDIM : KW + (g + 1) * HDIM].reshape(BLK, HDIM)
            passage = lax.dot_general(far, keys, over, preferred_element_type=jnp.float32)
            question = lax.dot_general(
                near,
                qkv_ref[:, g * HDIM : (g + 1) * HDIM],
                over,
                preferred_element_type=jnp.float32,
            )
            passage = jnp.where(live, passage * SCALE2, -1e30)
            question = jnp.where(own, question * SCALE2, -1e30)
            peak = jnp.maximum(
                jnp.max(passage, axis=-1, keepdims=True), jnp.max(question, axis=-1, keepdims=True)
            )
            passage = jnp.exp2(passage - peak)
            question = jnp.exp2(question - peak)
            total = jnp.sum(passage, axis=-1, keepdims=True) + jnp.sum(
                question, axis=-1, keepdims=True
            )
            mixed = jnp.dot(
                passage.astype(jnp.bfloat16), values, preferred_element_type=jnp.float32
            ) + jnp.dot(
                question.astype(jnp.bfloat16),
                qkv_ref[:, KW + g * HDIM : KW + (g + 1) * HDIM],
                preferred_element_type=jnp.float32,
            )
            context = (mixed / total).astype(jnp.bfloat16).astype(jnp.float32)
            total_score += jnp.sum(context * w_ref[g], axis=0, keepdims=True)
        result = jnp.sum(total_score, axis=-1, keepdims=True)
        out_ref[pl.ds(step, 1), :] = jnp.broadcast_to(result, (1, HDIM))
        return carry

    lax.fori_loop(0, count, body, 0)


def score(
    count, blocks, lengths, which, last, first, second, question_kv, kpos, cosine, sine, w
):
    slots = blocks.shape[0]
    anywhere = pl.BlockSpec(memory_space=pl.ANY)
    tokens = first[0].shape[2]

    def whole(array):
        return pl.BlockSpec(array.shape, lambda i, *_: (0,) * array.ndim)

    return pl.pallas_call(
        score_kernel,
        grid_spec=pltpu.PrefetchScalarGridSpec(
            num_scalar_prefetch=5,
            grid=(1,),
            in_specs=[
                whole(last),
                *[anywhere] * (2 * PARTS),
                whole(question_kv),
                whole(kpos),
                whole(cosine),
                whole(sine),
                whole(w),
            ],
            out_specs=pl.BlockSpec((slots, HDIM), lambda i, *_: (0, 0)),
            scratch_shapes=[
                pltpu.VMEM((2, SIDE * SIDE, tokens, 2 * KW), jnp.bfloat16),
                pltpu.SemaphoreType.DMA((2, PARTS)),
            ],
        ),
        out_shape=jax.ShapeDtypeStruct((slots, HDIM), jnp.float32),
        compiler_params=pltpu.CompilerParams(vmem_limit_bytes=VMEM),
        name="score",
    )(
        count,
        blocks,
        lengths,
        which,
        jnp.array([first[0].shape[1], QLEN], jnp.int32),
        last,
        *first,
        *second,
        question_kv,
        kpos,
        cosine,
        sine,
        w,
    )


def sorted_by(key):
    count = key.shape[0]
    place = jnp.arange(count, dtype=jnp.int32)
    ahead = (key[None, :] < key[:, None]) | (
        (key[None, :] == key[:, None]) & (place[None, :] < place[:, None])
    )
    rank = jnp.sum(ahead.astype(jnp.int32), axis=1)
    chosen = rank[None, :] == place[:, None]

    def arrange(values):
        return jnp.sum(jnp.where(chosen, values[None, :], 0), axis=1).astype(jnp.int32)

    return arrange, rank


def on_device(
    store_rows,
    block_lengths,
    queries,
    cand_owner,
    cand_block,
    cand_query,
    norm_gain,
    w_query,
    w_key,
    w_value,
    w_score,
):
    n_corpus = lax.axis_size("corpus")
    n_rerank = lax.axis_size("rerank")
    corpus_index = lax.axis_index("corpus")
    member = lax.axis_index("rerank")
    pair_total = cand_block.shape[0]
    pair_group = pair_total // n_corpus
    own_blocks, tokens, width = store_rows.shape
    n_query, q_tokens, _ = queries.shape
    q_dev = n_query // n_rerank

    owners = cand_owner[:, 0]
    pair_order = jnp.arange(pair_total, dtype=jnp.int32)
    group_of = pair_order // pair_group
    earlier = (
        (owners[:, None] == owners[None, :])
        & (group_of[:, None] == group_of[None, :])
        & (pair_order[None, :] < pair_order[:, None])
    )
    owner_rank = jnp.sum(earlier.astype(jnp.int32), axis=1)
    slot_ids = jnp.arange(n_corpus * CAP, dtype=jnp.int32)
    wanted = (
        (group_of[None, :] == (slot_ids // CAP)[:, None])
        & (owners[None, :] == corpus_index)
        & (owner_rank[None, :] == (slot_ids % CAP)[:, None])
    )
    present = jnp.any(wanted, axis=1)

    def of_slot(values):
        return jnp.sum(jnp.where(wanted, values[None, :], 0), axis=1)

    slot_query, slot_pair, stored_block = of_slot(cand_query), of_slot(pair_order), of_slot(cand_block)
    block_ids = jnp.arange(own_blocks, dtype=jnp.int32)
    owner_ids = jnp.arange(n_corpus, dtype=jnp.int32)
    named = jnp.any(
        (owners[None, None, :] == owner_ids[:, None, None])
        & (cand_block[None, None, :] == block_ids[None, :, None]),
        axis=2,
    )
    most = jnp.max(jnp.sum(named.astype(jnp.int32), axis=1))
    want = jnp.any(named & (owner_ids[:, None] == corpus_index), axis=0)
    want_count = jnp.sum(want.astype(jnp.int32))
    by_want, want_rank = sorted_by(jnp.where(want, 0, 1))
    block_order = by_want(block_ids)
    own_lengths = by_want(
        lax.dynamic_slice_in_dim(block_lengths, corpus_index * own_blocks, own_blocks, 0)
    )
    is_block = stored_block[:, None] == block_ids[None, :]
    slot_block = jnp.sum(jnp.where(is_block, want_rank[None, :], 0), axis=1)
    slot_length = jnp.sum(
        jnp.where(slot_block[:, None] == block_ids[None, :], own_lengths[None, :], 0), axis=1
    )
    slot_or_none = jnp.where(present, slot_block, -1)
    mine = present & (slot_query // q_dev == member)
    by_mine, _ = sorted_by(jnp.where(mine, slot_block, own_blocks))
    mine_count = jnp.sum(mine.astype(jnp.int32)).reshape(1)
    mine_block, mine_length = by_mine(slot_block), by_mine(slot_length)
    mine_which, mine_pair = by_mine(slot_query % q_dev), by_mine(slot_pair)

    all_cos, all_sin = rope_tables(jnp.arange(BLK + QLEN, dtype=jnp.int32))
    base = member * tokens
    own_cos, own_sin = rope_tables(base + jnp.arange(tokens, dtype=jnp.int32))
    x, y = member // SIDE, member % SIDE
    hops = jnp.array(HOPS, jnp.int32)
    xs, ys = (x + hops) % SIDE, (y + hops) % SIDE

    strip = QW // (n_corpus - 1)
    my_columns = lax.dynamic_slice_in_dim(
        w_query, jnp.minimum(corpus_index, n_corpus - 2) * strip, strip, 1
    )
    w_first = lax.all_gather(
        jnp.concatenate([w_key, w_value, my_columns], axis=1), "rerank", axis=0, tiled=True
    )
    gain = norm_gain.astype(jnp.float32).reshape(1, width)
    normed = norm(block_order, store_rows, gain)

    asked = lax.all_to_all(queries, "rerank", 0, 1, tiled=True).reshape(q_dev * QLEN, width)
    asked_token = jnp.arange(asked.shape[0], dtype=jnp.int32) % QLEN
    asked_cos, asked_sin = rope_tables(asked_token)


    inside = jnp.arange(tokens, dtype=jnp.int32)

    def positions_of(ranks):
        return (ranks[..., None] * tokens + inside).reshape(1, BLK)

    xb = (x - jnp.arange(SIDE, dtype=jnp.int32)) % SIDE
    kpos = positions_of(xb[:, None] * SIDE + ys[None, :])
    part_pos = jnp.concatenate(
        [
            positions_of(xs[:, None] * SIDE + ys[None, :]),
            positions_of(xs[None, :] * SIDE + ys[:, None]),
        ]
    )

    head_w = jnp.pad(
        w_score.astype(jnp.float32).reshape(KVHEADS, PER, HDIM), ((0, 0), (0, 8 - PER), (0, 0))
    )
    where = jnp.stack([base, x, want_count]).astype(jnp.int32)
    belongs = (slot_ids < mine_count[0])[:, None] & (mine_pair[:, None] == pair_order[None, :])
    pair_dev = pair_group // n_rerank

    def attended(blocks):
        half = blocks // 2
        strips = lax.all_gather(w_first[:, 2 * KW :], "corpus", axis=0, tiled=False)
        kv = key_value(normed, w_first, own_cos, own_sin, blocks * tokens)
        passage_kv = kv.reshape(blocks, tokens, 2 * KW)
        asked_normed, question_kv = asked_key_value(asked, gain, w_first, asked_cos, asked_sin)
        asked_last = jnp.pad(asked_normed[QLEN - 1 :: QLEN], ((0, 16 - q_dev), (0, 0)))
        first, second, (asked_last, question_kv) = plane_gather(
            passage_kv[:half], passage_kv[half:], (asked_last, question_kv)
        )
        query_rot, query_last = project_query(
            strips, normed, asked_last, own_cos, own_sin, blocks * tokens
        )
        last = query_last[:q_dev].reshape(q_dev, KVHEADS, PER, HDIM)
        last = jnp.pad(last, ((0, 0), (0, 0), (0, 8 - PER), (0, 0)))
        scored = score(
            mine_count,
            mine_block,
            mine_length,
            mine_which,
            last,
            first,
            second,
            question_kv,
            part_pos,
            all_cos,
            all_sin,
            head_w,
        )[: n_corpus * CAP, 0]
        placed = jnp.sum(jnp.where(belongs, scored[:, None], 0.0), axis=0)
        query_rot = query_rot.reshape(blocks, tokens, QW)
        gathered = lax.all_to_all(
            placed.reshape(n_corpus * n_rerank, pair_dev), ("corpus", "rerank"), 0, 0, tiled=True
        )
        pair_scores = jnp.sum(gathered, axis=0)
        begun = attend(
            slot_or_none, own_lengths, where, query_rot, first, kpos, False, 0, None
        )
        passage_context = attend(
            slot_or_none, own_lengths, where, query_rot, second, kpos, True, half, begun
        )
        return passage_context, pair_scores

    choice = sum((most > size).astype(jnp.int32) for size in SIZES)
    return lax.switch(choice, [lambda size=size: attended(size) for size in (*SIZES, own_blocks)])


def solution(mesh):
    placed = (
        P("corpus", "rerank", None),
        P(),
        P(None, "rerank", None),
        P(),
        P(),
        P(),
        P(),
        P("rerank", None),
        P("rerank", None),
        P("rerank", None),
        P(),
    )
    return jax.shard_map(
        on_device,
        mesh=mesh,
        in_specs=placed,
        out_specs=(P("corpus", "rerank", None), P(("corpus", "rerank"))),
        check_vma=False,
    )
```
